512 devices in a mesh: queue: 16 (over x, y), seq: 32 (over z, core).
Axes of the slice: x: 4, y: 4, z: 16, core: 2. Of those that a mesh axis runs over, the one named last changes fastest.
Arguments:
- t_qkv: bfloat16 [4, 16, 2304, 1728], P(None, 'queue', 'seq'), may hold values from -6 to 6
- hidden: bfloat16 [4, 16, 2304, 1152], P(None, 'queue', 'seq'), may hold values from -6 to 6
- latents: bfloat16 [4, 16, 2304, 16], P(None, 'queue', 'seq'), may hold values from -6 to 6
- fresh: bfloat16 [4, 2304, 16], P(None, 'seq'), may hold values from -6 to 6
- levels: int32 [16], replicated, may hold values from 1 to 64, as said below
- alpha_bar: float32 [65], replicated, may hold values from 0.05 to 0.95
- modulation: bfloat16 [65, 6, 1152], replicated, may hold values from -3 to 3
- w_tout: bfloat16 [576, 1152], P('queue'), may hold values from -0.25 to 0.25
- w_final: bfloat16 [1152, 16], replicated, may hold values from -0.1875 to 0.1875
- w_embed: bfloat16 [16, 1152], replicated, may hold values from -1.5 to 1.5
- w_sqkv: bfloat16 [1152, 1728], P('queue'), may hold values from -0.20623948 to 0.20623948
- w_sout: bfloat16 [576, 1152], P('queue'), may hold values from -0.25 to 0.25
Outputs:
- queued: bfloat16 [4, 16, 2304, 16], P(None, 'queue', 'seq')
- block_out: bfloat16 [4, 16, 2304, 1152], P(None, 'queue', 'seq')
The draws below stay inside these ranges and needn't reach their ends.
Inputs may be any that keep to these rules, and one draw needn't show every extreme that they name: levels rise strictly along the queue; the head frame is at level 1 and the tail frame at level 64.
All inputs are finite; a program needn't handle non-finite values.
Results may differ from the reference program's by a relative error of at most 0.011.
Values may be sent and summed in bfloat16 or wider, within the bound.
No kernel may reach another device: no remote copies, remote signals or barrier semaphores. Data moves between devices by JAX's collectives and lax.ppermute only.
A program may use at most 64 MiB of HBM per device.

```python
import math
import jax
import jax.numpy as jnp
from jax import lax

D = 1152
HEADS = 8
HDIM = 72
PATCH = 16
TOKENS = 2304
VIDEOS = 4
HD = 576
FRAMES = 16
LEVELS = 64


def draw_levels(key, part):
    key = jax.random.fold_in(key, 11)
    candidates = jax.random.permutation(key, LEVELS - 2) + 2
    middle = jnp.sort(candidates[:FRAMES - 2]).astype(jnp.int32)
    return jnp.concatenate([jnp.ones((1,), jnp.int32), middle, jnp.full((1,), LEVELS, jnp.int32)])


def draw_t_qkv(key, part):
    key = jax.random.fold_in(key, 21)
    sample_key = jax.random.fold_in(key, 0)
    sample = jax.random.normal(sample_key, (VIDEOS, FRAMES, TOKENS, HEADS, 3, HDIM), jnp.float32)
    sample = jnp.clip(sample, -6.0, 6.0)
    return sample.reshape(VIDEOS, FRAMES, TOKENS, 3 * HEADS * HDIM).astype(jnp.bfloat16)


def draw_modulation(key, part):
    key = jax.random.fold_in(key, 31)
    normal_key = jax.random.fold_in(key, 0)
    normals = jax.random.normal(normal_key, (LEVELS + 1, 6, D), jnp.float32)
    row_index = jnp.arange(6)[None, :, None]
    sample = jnp.where(row_index == 5, 1.5, 0.5) * normals
    return jnp.clip(sample, -3.0, 3.0).astype(jnp.bfloat16)


def draw_w_sqkv(key, part):
    key = jax.random.fold_in(key, 41)
    normal_key = jax.random.fold_in(key, 0)
    normals = jax.random.normal(normal_key, (D, HEADS, 3, HDIM), jnp.float32)
    sample = jnp.clip(normals, -6.0, 6.0) * float(D) ** (-0.5)
    return sample.reshape(D, 3 * HEADS * HDIM).astype(jnp.bfloat16)


def block_levels(own_key, extent, cuts, low, top_value):
    loudness, own = 1.0, jax.random.fold_in(own_key, 6)
    for axis_at, blocks in cuts:
        draws = jnp.exp(jax.random.uniform(jax.random.fold_in(own, axis_at), (blocks,), jnp.float32, low / len(cuts), top_value / len(cuts)))
        loudness = loudness * jnp.repeat(draws, extent[axis_at] // blocks).reshape([-1 if axis == axis_at else 1 for axis in range(len(extent))])
    return loudness


def scatter_about(stream_key, dims, width, reach, cuts=(), kind=jnp.bfloat16):
    entries = jax.random.normal(stream_key, dims, jnp.float32) * width
    if len(cuts) > 0:
        entries = block_levels(stream_key, dims, cuts, -0.22, 0.18) * entries
    return jnp.clip(entries, min=-reach, max=reach).astype(kind)


def setup_inputs(seed: int = 0) -> dict:
    key_list = jax.random.split(jax.random.key(seed), 13)
    t_qkv = draw_t_qkv(jax.random.fold_in(key_list[12], 71), 0)
    hidden = scatter_about(key_list[1], (VIDEOS, FRAMES, TOKENS, D), 1.0, 6.0, ((1, 16), (2, 32)))
    latents = scatter_about(key_list[2], (VIDEOS, FRAMES, TOKENS, PATCH), 1.0, 6.0, ((1, 16), (2, 32)))
    fresh = scatter_about(key_list[3], (VIDEOS, TOKENS, PATCH), 1.0, 6.0, ((1, 32),))
    levels = draw_levels(jax.random.fold_in(key_list[12], 71), 0)
    alpha_bar = jnp.clip(jax.random.uniform(key_list[5], (LEVELS + 1,), jnp.float32, 0.05, 0.95), 0.05, 0.95)
    modulation = draw_modulation(jax.random.fold_in(key_list[12], 71), 0)
    w_tout = scatter_about(key_list[7], (HD, D), HD ** -0.5, 0.25, ((0, 16),))
    w_final = scatter_about(key_list[8], (D, PATCH), D ** -0.5, 0.1875)
    w_embed = scatter_about(key_list[9], (PATCH, D), PATCH ** -0.5, 1.5)
    w_sqkv = draw_w_sqkv(jax.random.fold_in(key_list[12], 71), 0)
    w_sout = scatter_about(key_list[11], (HD, D), HD ** -0.5, 0.25, ((0, 16),))
    return {"t_qkv": t_qkv, "hidden": hidden, "latents": latents, "fresh": fresh, "levels": levels, "alpha_bar": alpha_bar, "modulation": modulation, "w_tout": w_tout, "w_final": w_final, "w_embed": w_embed, "w_sqkv": w_sqkv, "w_sout": w_sout}


def layer_norm(values):
    center = values - lax.optimization_barrier(jnp.mean(values, axis=-1, keepdims=True))
    spread = lax.optimization_barrier(jnp.mean(center * center, axis=-1, keepdims=True))
    return center * lax.rsqrt(spread + 1e-06)

def position_table(token_index, model_width):
    half_width = model_width // 2
    frequency = jnp.exp(jnp.arange(half_width, dtype=jnp.float32) * (-math.log(10000.0) / half_width))
    phase_angle = token_index[:, None] * frequency[None, :]
    return jnp.concatenate([jnp.sin(phase_angle), jnp.cos(phase_angle)], axis=-1)

def ddim_update(noisy_latent, predicted, alpha_now, alpha_next):
    clean_latent = (noisy_latent - jnp.sqrt(1.0 - alpha_now) * predicted) / jnp.sqrt(alpha_now)
    return jnp.sqrt(alpha_next) * clean_latent + jnp.sqrt(1.0 - alpha_next) * predicted

def rounded_copy(values):
    return lax.optimization_barrier(values.astype(jnp.bfloat16)).astype(jnp.float32)

def reference(t_qkv, hidden, latents, fresh, levels, alpha_bar, modulation, w_tout, w_final, w_embed, w_sqkv, w_sout):
    inverse_scale = 1.0 / math.sqrt(HDIM)
    level_mods = modulation[levels].astype(jnp.float32)
    new_levels = jnp.concatenate([levels[1:] - 1, jnp.full((1,), LEVELS, jnp.int32)]).astype(jnp.int32)
    new_mods = modulation[new_levels].astype(jnp.float32)
    divided = t_qkv.reshape(VIDEOS, FRAMES, TOKENS, HEADS, 3, HDIM)
    queries = divided[..., 0, :].astype(jnp.float32)
    key_part = divided[..., 1, :].astype(jnp.float32)
    values = divided[..., 2, :].astype(jnp.float32)
    scores = jnp.einsum('vfnhd,vgnhd->vnhfg', queries, key_part) * inverse_scale
    weights = rounded_copy(jax.nn.softmax(scores, axis=-1))
    blended = jnp.einsum('vnhfg,vgnhd->vfnhd', weights, values)
    temporal_out = blended.astype(jnp.bfloat16).reshape(VIDEOS * FRAMES * TOKENS, HD)
    temporal_proj = jnp.dot(temporal_out, w_tout, preferred_element_type=jnp.float32).reshape(VIDEOS, FRAMES, TOKENS, D)
    residual = hidden.astype(jnp.float32) + level_mods[:, 0][None, :, None, :] * temporal_proj
    final_in = (layer_norm(residual) * (1.0 + level_mods[:, 2][None, :, None, :]) + level_mods[:, 1][None, :, None, :]).astype(jnp.bfloat16)
    predicted = jnp.dot(final_in.reshape(-1, D), w_final, preferred_element_type=jnp.float32).reshape(VIDEOS, FRAMES, TOKENS, PATCH)
    alpha_now = alpha_bar[levels][None, :, None, None]
    alpha_next = alpha_bar[levels - 1][None, :, None, None]
    stepped = ddim_update(latents.astype(jnp.float32), predicted, alpha_now, alpha_next).astype(jnp.bfloat16)
    queued = jnp.concatenate([stepped[:, 1:], fresh[:, None]], axis=1)
    position = position_table(jnp.arange(TOKENS, dtype=jnp.float32), D)
    embedded = jnp.dot(queued.reshape(-1, PATCH), w_embed, preferred_element_type=jnp.float32).reshape(VIDEOS, FRAMES, TOKENS, D) + position[None, None]
    spatial_in = (layer_norm(embedded) * (1.0 + new_mods[:, 4][None, :, None, :]) + new_mods[:, 3][None, :, None, :]).astype(jnp.bfloat16)
    spatial_qkv = jnp.dot(spatial_in.reshape(-1, D), w_sqkv, preferred_element_type=jnp.float32).astype(jnp.bfloat16)
    spatial_qkv = spatial_qkv.reshape(VIDEOS * FRAMES, TOKENS, HEADS, 3, HDIM)

    def attend(head_item):
        entry_queries = head_item[:, :, 0].astype(jnp.float32)
        entry_keys = head_item[:, :, 1].astype(jnp.float32)
        entry_values = head_item[:, :, 2].astype(jnp.float32)
        entry_scores = jnp.einsum('wqr,vqr->qwv', entry_queries, entry_keys) * inverse_scale
        entry_weights = rounded_copy(jax.nn.softmax(entry_scores, axis=-1))
        return jnp.einsum('lfb,bla->fla', entry_weights, entry_values).astype(jnp.bfloat16)
    spatial_out = lax.map(attend, spatial_qkv).reshape(-1, HD)
    spatial_proj = jnp.dot(spatial_out, w_sout, preferred_element_type=jnp.float32).reshape(VIDEOS, FRAMES, TOKENS, D)
    block_out = (embedded + new_mods[:, 5][None, :, None, :] * spatial_proj).astype(jnp.bfloat16)
    return (queued, block_out)
```

```python
import math

import jax
import jax.numpy as jnp
import numpy as np
from jax import lax
from jax.experimental import pallas as pl
from jax.experimental.pallas import tpu as pltpu
from jax.sharding import PartitionSpec as P

HEADS = 8
HDIM = 72
HALF = HDIM // 2
SLOT = 40
HSLOT = 2 * SLOT
SCORE_SCALE = 1.0 / math.sqrt(HDIM)
LOG2E = math.log2(math.e)
F32 = jnp.float32
BF16 = jnp.bfloat16
VMEM_LIMIT = 56 * 1024 * 1024


def mm(a, b):
    return jnp.dot(a, b, preferred_element_type=F32)


def mm_nt(a, b):
    return lax.dot_general(a, b, (((1,), (1,)), ((), ())), preferred_element_type=F32)


def call(kernel, out_shape, args, scratch=(), smem=(), flops=0, grid=None, in_specs=None, out_specs=None):
    moved = sum(a.size * a.dtype.itemsize for a in args)
    if in_specs is None:
        in_specs = [
            pl.BlockSpec(memory_space=pltpu.SMEM if i in smem else pltpu.VMEM) for i in range(len(args))
        ]
        out_specs = pl.BlockSpec(memory_space=pltpu.VMEM)
    return pl.pallas_call(
        kernel,
        out_shape=out_shape,
        in_specs=in_specs,
        out_specs=out_specs,
        scratch_shapes=list(scratch),
        compiler_params=pltpu.CompilerParams(vmem_limit_bytes=VMEM_LIMIT),
        cost_estimate=pl.CostEstimate(flops=flops, bytes_accessed=moved, transcendentals=0),
        **({"grid": grid} if grid else {}),
    )(*args)


def layer_norm(values):
    center = values - jnp.mean(values, axis=-1, keepdims=True)
    spread = jnp.mean(center * center, axis=-1, keepdims=True)
    return center * lax.rsqrt(spread + 1e-06)


def pack_kernel(x_ref, o_ref):
    width = o_ref.shape[-1]
    for part in range(o_ref.shape[0]):
        o_ref[part] = x_ref[0, :, part * width : (part + 1) * width]


def temporal_columns():
    pick = np.zeros((6 * HDIM, 1024), np.float32)
    for head in range(2):
        base = 3 * HDIM * head
        for i in range(HDIM):
            pick[base + i, 256 * head + i] = 1.0
            pick[base + HDIM + i, 256 * head + 128 + i] = 1.0
            place = HSLOT * head + (i // HALF) * SLOT + i % HALF
            pick[base + 2 * HDIM + i, 512 + 256 * head + place] = 1.0
    return pick


def temporal_kernel(x_ref, pick_ref, o_ref, parts, total):
    frames, tokens, _ = x_ref.shape
    pick = pick_ref[...]
    for f in range(frames):
        parts[f] = mm(x_ref[f], pick)
    rows = frames * 8
    same = (
        lax.broadcasted_iota(jnp.int32, (rows, rows), 0) % 8
        == lax.broadcasted_iota(jnp.int32, (rows, rows), 1) % 8
    )
    for block in range(tokens // 8):
        piece = parts[:, 8 * block : 8 * block + 8, :].reshape(rows, 1024).astype(BF16)
        out = None
        for head in range(2):
            q = piece[:, 256 * head : 256 * head + 128]
            k = piece[:, 256 * head + 128 : 256 * head + 256]
            v = piece[:, 512 + 256 * head : 512 + 256 * head + 2 * HSLOT]
            scores = jnp.where(same, mm_nt(q, k) * SCORE_SCALE, -jnp.inf)
            top = jnp.max(scores, axis=-1, keepdims=True)
            raised = jnp.exp(scores - top)
            weights = (raised / jnp.sum(raised, axis=-1, keepdims=True)).astype(BF16)
            found = mm(weights, v)
            out = found if out is None else out + found
        total[:, 8 * block : 8 * block + 8, :] = out.reshape(frames, 8, 2 * HSLOT)
    o_ref[...] = total[...].astype(BF16)


def step_kernel(coef_ref, att_ref, hid_ref, lat_ref, w_ref, wf_ref, mod_ref, o_ref):
    videos, tokens, width = hid_ref.shape
    rows = videos * tokens
    pairs = att_ref.shape[0] // videos
    att = att_ref[...].astype(F32).reshape(videos, pairs, tokens, 2 * HSLOT)
    proj = None
    for p in range(pairs):
        part = att[:, p].reshape(rows, 2 * HSLOT).astype(BF16)
        term = mm(part, w_ref[2 * HSLOT * p : 2 * HSLOT * (p + 1), :])
        proj = term if proj is None else proj + term
    residual = hid_ref[...].astype(F32).reshape(rows, width) + mod_ref[0:1, :] * proj
    final_in = (layer_norm(residual) * (1.0 + mod_ref[2:3, :]) + mod_ref[1:2, :]).astype(BF16)
    predicted = mm_nt(wf_ref[...], final_in)
    for v in range(videos):
        pred = predicted[:, tokens * v : tokens * (v + 1)]
        clean = (lat_ref[v].astype(F32) - coef_ref[0] * pred) * coef_ref[1]
        o_ref[v] = (coef_ref[2] * clean + coef_ref[3] * pred).astype(BF16)


def spatial_kernel(
    group_ref, lat_ref, wemb_ref, ua_ref, va_ref, cb_ref, sb_ref, mod_ref, wq_ref, wkv_ref,
    o_ref, xs, keys, vals, qs, outs,
):
    chunks, _, tokens = lat_ref.shape
    members = o_ref.shape[0]
    total_rows = chunks * tokens
    own_rows = members * tokens
    wemb = wemb_ref[...]
    gain = 1.0 + mod_ref[4:5, :]
    shift = mod_ref[3:4, :]

    def build(pair, carry):
        made = []
        for i in range(2):
            c = 2 * pair + i
            latent = lat_ref[c].astype(F32).T.astype(BF16)
            place = ua_ref[c] * cb_ref[...] + va_ref[c] * sb_ref[...]
            embedded = mm(latent, wemb) + place
            made.append(layer_norm(embedded) * gain + shift)
        start = pl.multiple_of(pair * (2 * tokens), 2 * tokens)
        xs[pl.ds(start, 2 * tokens), :] = jnp.concatenate(made, axis=0).astype(BF16)
        return carry

    lax.fori_loop(0, chunks // 2, build, 0)

    lane = lax.broadcasted_iota(jnp.int32, (1, HSLOT), 1)
    ones = jnp.where(lane == HALF, 1.0, 0.0)
    block = 384

    def project(step, carry):
        start = pl.multiple_of(step * block, block)
        kv = mm(xs[pl.ds(start, block), :], wkv_ref[...])
        for h in range(HEADS):
            at = (HDIM + HSLOT) * h
            keys[h, pl.ds(start, block), :] = kv[:, at : at + HDIM].astype(BF16)
            vals[h, pl.ds(start, block), :] = (kv[:, at + HDIM : at + HDIM + HSLOT] + ones).astype(BF16)
        return carry

    lax.fori_loop(0, total_rows // block, project, 0)

    first = pl.multiple_of(group_ref[0] * own_rows, own_rows)
    q_all = mm(xs[pl.ds(first, own_rows), :], wq_ref[...])
    for h in range(HEADS):
        qs[h] = q_all[:, HDIM * h : HDIM * (h + 1)].astype(BF16)

    def attend(h, carry):
        scores = mm_nt(qs[h], keys[h])
        top = jnp.max(scores, axis=-1, keepdims=True)
        raised = jnp.exp2((scores - top) * (SCORE_SCALE * LOG2E)).astype(BF16)
        found = mm(raised, vals[h])
        outs[h] = found * (1.0 / found[:, HALF : HALF + 1])
        return carry

    lax.fori_loop(0, HEADS, attend, 0)
    merged = jnp.concatenate([outs[h] for h in range(HEADS)], axis=-1)
    o_ref[...] = merged.reshape(members, tokens, HEADS * HSLOT).astype(BF16)


def finish_kernel(seq_ref, att_ref, lat_ref, wemb_ref, ua_ref, va_ref, cb_ref, sb_ref, mod_ref, w_ref, o_ref):
    videos, tokens, width = o_ref.shape
    att = att_ref[...].astype(F32).reshape(videos * tokens, HEADS * HSLOT).astype(BF16)
    gated = mm(att, w_ref[...]) * mod_ref[5:6, :]
    s = seq_ref[0]
    place = ua_ref[s] * cb_ref[...] + va_ref[s] * sb_ref[...]
    for v in range(videos):
        latent = lat_ref[v].astype(F32).T.astype(BF16)
        embedded = mm(latent, wemb_ref[...]) + place
        o_ref[v] = (embedded + gated[tokens * v : tokens * (v + 1), :]).astype(BF16)


def position_factors(chunks, tokens, width):
    half = width // 2
    frequency = jnp.exp(jnp.arange(half, dtype=F32) * (-math.log(10000.0) / half))
    start = (jnp.arange(chunks, dtype=F32) * tokens)[:, None] * frequency[None, :]
    inner = jnp.arange(tokens, dtype=F32)[:, None] * frequency[None, :]
    sin_a, cos_a, sin_b, cos_b = jnp.sin(start), jnp.cos(start), jnp.sin(inner), jnp.cos(inner)
    ua = jnp.concatenate([sin_a, cos_a], axis=-1).reshape(chunks, 1, width)
    va = jnp.concatenate([cos_a, -sin_a], axis=-1).reshape(chunks, 1, width)
    cb = jnp.concatenate([cos_b, cos_b], axis=-1)
    sb = jnp.concatenate([sin_b, sin_b], axis=-1)
    return ua, va, cb, sb


def pad_rows(weight):
    return jnp.pad(weight, ((0, SLOT - HALF), (0, 0)))


def spread(value, axis):
    count = lax.axis_size(axis)
    copies = jnp.broadcast_to(value[None], (count,) + value.shape)
    return lax.all_to_all(copies, axis, split_axis=0, concat_axis=0, tiled=True)


def shards(
    t_qkv, hidden, latents, fresh, levels, alpha_bar, modulation, w_tout, w_final, w_embed, w_sqkv, w_sout,
):
    frames = lax.axis_size("queue")
    seqs = lax.axis_size("seq")
    queue_pos = lax.axis_index("queue")
    seq_pos = lax.axis_index("seq")
    videos, _, tokens, width = hidden.shape
    top_level = alpha_bar.shape[0] - 1
    pairs = frames // videos

    by_head = w_sqkv.reshape(-1, HEADS, 3, HDIM)
    q_cols = by_head[:, :, 0].reshape(-1, HEADS * HDIM)
    v_cols = jnp.pad(
        by_head[:, :, 2].reshape(-1, HEADS, 2, HALF), ((0, 0), (0, 0), (0, 0), (0, SLOT - HALF))
    ).reshape(-1, HEADS, HSLOT)
    kv_cols = jnp.concatenate([by_head[:, :, 1], v_cols], axis=-1).reshape(-1, HEADS * (HDIM + HSLOT))
    w_spatial = lax.all_gather(jnp.concatenate([q_cols, kv_cols], axis=-1), "queue", axis=0, tiled=True)

    width_part = t_qkv.shape[-1] // pairs
    packed = call(
        pack_kernel,
        jax.ShapeDtypeStruct((frames, tokens, width_part), BF16),
        (t_qkv.reshape(videos, tokens, -1),),
        grid=(videos,),
        in_specs=[pl.BlockSpec((1, tokens, t_qkv.shape[-1]), lambda v: (v, 0, 0))],
        out_specs=pl.BlockSpec((pairs, tokens, width_part), lambda v: (v, 0, 0)),
    )
    arrived = lax.all_to_all(packed, "queue", split_axis=0, concat_axis=0, tiled=True)
    w_t = spread(pad_rows(w_tout), "queue").reshape(frames * SLOT, width)

    attended = call(
        temporal_kernel,
        jax.ShapeDtypeStruct((frames, tokens, 2 * HSLOT), BF16),
        (arrived, jnp.asarray(temporal_columns(), BF16)),
        scratch=[pltpu.VMEM((frames, tokens, 1024), F32), pltpu.VMEM((frames, tokens, 2 * HSLOT), F32)],
        flops=4_000_000_000,
    )
    returned = lax.all_to_all(attended, "queue", split_axis=0, concat_axis=0, tiled=True)

    level = lax.dynamic_index_in_dim(levels, queue_pos, 0, keepdims=False)
    following = lax.dynamic_index_in_dim(
        jnp.concatenate([levels[1:], jnp.full((1,), top_level + 1, levels.dtype)]), queue_pos, 0, keepdims=False
    )
    mods = lax.dynamic_index_in_dim(modulation, level, 0, keepdims=False).astype(F32)
    new_mods = lax.dynamic_index_in_dim(modulation, following - 1, 0, keepdims=False).astype(F32)
    a = lax.dynamic_index_in_dim(alpha_bar, level, 0, keepdims=False)
    b = lax.dynamic_index_in_dim(alpha_bar, level - 1, 0, keepdims=False)
    coef = jnp.stack([jnp.sqrt(1.0 - a), 1.0 / jnp.sqrt(a), jnp.sqrt(b), jnp.sqrt(1.0 - b)])

    stepped = call(
        step_kernel,
        jax.ShapeDtypeStruct((videos, latents.shape[-1], tokens), BF16),
        (
            coef,
            returned,
            hidden.reshape(videos, tokens, width),
            latents.reshape(videos, tokens, -1).transpose(0, 2, 1),
            w_t,
            w_final.T,
            mods,
        ),
        smem=(0,),
        flops=1_000_000_000,
    )
    arriving = lax.ppermute(stepped, "queue", [(f, f - 1) for f in range(1, frames)])
    queued = jnp.where(queue_pos == frames - 1, fresh.transpose(0, 2, 1), arriving)

    everyone = lax.all_to_all(
        jnp.tile(queued, (seqs // videos, 1, 1)), "seq", split_axis=0, concat_axis=0, tiled=True
    )
    ua, va, cb, sb = position_factors(seqs, tokens, width)
    groups = [[videos * g + i for i in range(videos)] for g in range(seqs // videos)]
    sout_shard, everyone = lax.optimization_barrier((pad_rows(w_sout), everyone))
    w_s = spread(sout_shard, "queue").reshape(frames * SLOT, width)
    rows = seqs * tokens
    spatial = call(
        spatial_kernel,
        jax.ShapeDtypeStruct((videos, tokens, HEADS * HSLOT), BF16),
        (
            (seq_pos // videos).reshape(1), everyone, w_embed, ua, va, cb, sb, new_mods,
            w_spatial[:, : HEADS * HDIM], w_spatial[:, HEADS * HDIM :],
        ),
        scratch=[
            pltpu.VMEM((rows, width), BF16),
            pltpu.VMEM((HEADS, rows, HDIM), BF16),
            pltpu.VMEM((HEADS, rows, HSLOT), BF16),
            pltpu.VMEM((HEADS, videos * tokens, HDIM), BF16),
            pltpu.VMEM((HEADS, videos * tokens, HSLOT), F32),
        ],
        smem=(0,),
        flops=20_000_000_000,
    )
    heads_out = lax.all_to_all(
        spatial, "seq", split_axis=0, concat_axis=0, tiled=True, axis_index_groups=groups
    )
    block_out = call(
        finish_kernel,
        jax.ShapeDtypeStruct((videos, tokens, width), BF16),
        (seq_pos.reshape(1), heads_out, queued, w_embed, ua, va, cb, sb, new_mods, w_s),
        smem=(0,),
        flops=1_000_000_000,
    )
    return (
        queued.transpose(0, 2, 1).reshape(videos, 1, tokens, -1),
        block_out.reshape(videos, 1, tokens, width),
    )


def solution(mesh):
    in_specs = (
        P(None, "queue", "seq", None),
        P(None, "queue", "seq", None),
        P(None, "queue", "seq", None),
        P(None, "seq", None),
        P(),
        P(),
        P(),
        P("queue", None),
        P(),
        P(),
        P("queue", None),
        P("queue", None),
    )
    out_specs = (P(None, "queue", "seq", None), P(None, "queue", "seq", None))
    return jax.shard_map(shards, mesh=mesh, in_specs=in_specs, out_specs=out_specs, check_vma=False)
```

```python
import math

import jax
import jax.numpy as jnp
import numpy as np
from jax import lax
from jax.experimental import pallas as pl
from jax.experimental.pallas import tpu as pltpu
from jax.sharding import PartitionSpec as P

HEADS = 8
HDIM = 72
HALF = HDIM // 2
SLOT = 80
PADDED = HEADS * SLOT
SCORE_SCALE = 1.0 / math.sqrt(HDIM)
LOG2E = math.log2(math.e)
F32 = jnp.float32
BF16 = jnp.bfloat16
VMEM_LIMIT = 56 * 1024 * 1024


def mm(a, b):
    return jnp.dot(a, b, preferred_element_type=F32)


def mm_nt(a, b):
    return lax.dot_general(a, b, (((1,), (1,)), ((), ())), preferred_element_type=F32)


def call(kernel, out_shape, args, scratch=(), smem=(), hbm=(), flops=0, grid=None, in_specs=None, out_specs=None):
    moved = sum(a.size * a.dtype.itemsize for a in args)
    if in_specs is None:
        in_specs = [
            pl.BlockSpec(memory_space=pltpu.SMEM if i in smem else pl.ANY if i in hbm else pltpu.VMEM)
            for i in range(len(args))
        ]
        out_specs = jax.tree.map(lambda _: pl.BlockSpec(memory_space=pltpu.VMEM), out_shape)
    return pl.pallas_call(
        kernel,
        out_shape=out_shape,
        in_specs=in_specs,
        out_specs=out_specs,
        scratch_shapes=list(scratch),
        compiler_params=pltpu.CompilerParams(vmem_limit_bytes=VMEM_LIMIT),
        cost_estimate=pl.CostEstimate(flops=flops, bytes_accessed=moved, transcendentals=0),
        **({"grid": grid} if grid else {}),
    )(*args)


def layer_norm(values):
    center = values - jnp.mean(values, axis=-1, keepdims=True)
    spread = jnp.mean(center * center, axis=-1, keepdims=True)
    return center * lax.rsqrt(spread + 1e-06)


def pack_kernel(x_ref, w_ref, o_ref):
    width = x_ref.shape[-1] // o_ref.shape[0]
    weight = w_ref[...]
    for part in range(o_ref.shape[0]):
        o_ref[part, :, :width] = x_ref[0, :, part * width : (part + 1) * width]
        o_ref[part, :, width:] = weight


def temporal_columns():
    pick = np.zeros((6 * HDIM, 1024), np.float32)
    for head in range(2):
        base = 3 * HDIM * head
        for i in range(HDIM):
            pick[base + i, 256 * head + i] = 1.0
            pick[base + HDIM + i, 256 * head + 128 + i] = 1.0
            pick[base + 2 * HDIM + i, 512 + 256 * head + SLOT * head + i] = 1.0
    return pick


def weight_rows():
    pick = np.zeros((2 * SLOT, 2 * HDIM), np.float32)
    for shard in range(2):
        for i in range(HALF):
            pick[HALF * shard + i, HDIM * shard + i] = 1.0
            pick[SLOT + HALF * shard + i, HDIM * shard + HALF + i] = 1.0
    return pick


def temporal_kernel(x_ref, pick_ref, rows_ref, o_ref, w_ref, parts, total):
    frames, tokens, _ = x_ref.shape
    pick = pick_ref[...]
    for f in range(frames):
        parts[f] = mm(x_ref[f, :, : 6 * HDIM], pick)
    rows = frames * 8
    same = (
        lax.broadcasted_iota(jnp.int32, (rows, rows), 0) % 8
        == lax.broadcasted_iota(jnp.int32, (rows, rows), 1) % 8
    )
    for block in range(tokens // 8):
        piece = parts[:, 8 * block : 8 * block + 8, :].reshape(rows, 1024).astype(BF16)
        out = None
        for head in range(2):
            q = piece[:, 256 * head : 256 * head + 128]
            k = piece[:, 256 * head + 128 : 256 * head + 256]
            v = piece[:, 512 + 256 * head : 512 + 256 * head + 2 * SLOT]
            scores = jnp.where(same, mm_nt(q, k) * SCORE_SCALE, -jnp.inf)
            top = jnp.max(scores, axis=-1, keepdims=True)
            raised = jnp.exp(scores - top)
            weights = (raised / jnp.sum(raised, axis=-1, keepdims=True)).astype(BF16)
            found = mm(weights, v)
            out = found if out is None else out + found
        total[:, 8 * block : 8 * block + 8, :] = out.reshape(frames, 8, 2 * SLOT)
    o_ref[...] = total[...].astype(BF16)
    for h in range(frames // 2):
        pair = x_ref[2 * h : 2 * h + 2, :, 6 * HDIM :].astype(F32).reshape(2 * tokens, -1).astype(BF16)
        both = mm(rows_ref[...], pair)
        w_ref[SLOT * h : SLOT * (h + 1), :] = jnp.concatenate(
            [both[:SLOT], both[SLOT:]], axis=-1
        ).astype(BF16)


def step_kernel(coef_ref, core_ref, att_ref, hid_ref, lat_ref, mine_ref, other_ref, wf_ref, mod_ref, o_ref):
    videos, tokens, width = hid_ref.shape
    rows = videos * tokens
    pairs = att_ref.shape[0] // videos
    att = att_ref[...].astype(F32).reshape(videos, pairs, tokens, 2 * SLOT)
    own = far = None
    for p in range(pairs):
        part = att[:, p].reshape(rows, 2 * SLOT).astype(BF16)
        at = slice(2 * SLOT * p, 2 * SLOT * (p + 1))
        own_term, far_term = mm(part, mine_ref[at, :]), mm(part, other_ref[at, :])
        own = own_term if own is None else own + own_term
        far = far_term if far is None else far + far_term
    low = core_ref[0] == 0
    proj = jnp.concatenate([jnp.where(low, own, far), jnp.where(low, far, own)], axis=-1)
    residual = hid_ref[...].astype(F32).reshape(rows, width) + mod_ref[0:1, :] * proj
    final_in = (layer_norm(residual) * (1.0 + mod_ref[2:3, :]) + mod_ref[1:2, :]).astype(BF16)
    predicted = mm_nt(wf_ref[...], final_in)
    for v in range(videos):
        pred = predicted[:, tokens * v : tokens * (v + 1)]
        clean = (lat_ref[v].astype(F32) - coef_ref[0] * pred) * coef_ref[1]
        o_ref[v] = (coef_ref[2] * clean + coef_ref[3] * pred).astype(BF16)


def spatial_kernel(
    group_ref, lat_ref, wemb_ref, ua_ref, va_ref, cb_ref, sb_ref, mod_ref, w_ref,
    o_ref, even, odd, own, keys, vals, ws, sem,
):
    chunks, _, tokens = lat_ref.shape
    members = o_ref.shape[0]
    block = members * tokens
    blocks = chunks // members
    copy = pltpu.make_async_copy(w_ref.at[:, : 3 * PADDED], ws, sem)
    copy.start()
    wemb = wemb_ref[...]
    gain = 1.0 + mod_ref[4:5, :]
    shift = mod_ref[3:4, :]
    lane = lax.broadcasted_iota(jnp.int32, (1, PADDED), 1)
    ones = jnp.where(lane % SLOT == HDIM, 1.0, 0.0)

    def build(index, x_ref):
        made = []
        for i in range(members):
            c = index * members + i
            latent = lat_ref[c].astype(F32).T.astype(BF16)
            place = ua_ref[pl.ds(c, 1), :] * cb_ref[...] + va_ref[pl.ds(c, 1), :] * sb_ref[...]
            embedded = mm(latent, wemb) + place
            made.append(layer_norm(embedded) * gain + shift)
            if i % 2:
                x_ref[tokens * (i - 1) : tokens * (i + 1), :] = jnp.concatenate(made, axis=0).astype(BF16)
                made = []

    def project(index, x_ref):
        start = pl.multiple_of(index * block, block)
        x = x_ref[...]
        keys[pl.ds(start, block), :] = mm(x, ws[:, :PADDED]).astype(BF16)
        vals[pl.ds(start, block), :] = (mm(x, ws[:, PADDED : 2 * PADDED]) + ones).astype(BF16)

    def keep(index, x_ref):
        @pl.when(index == group_ref[0])
        def _():
            own[...] = x_ref[...]

    build(0, even)
    copy.wait()

    def two(step, carry):
        project(2 * step, even)
        build(2 * step + 1, odd)
        keep(2 * step, even)
        project(2 * step + 1, odd)
        build(jnp.minimum(2 * step + 2, blocks - 1), even)
        keep(2 * step + 1, odd)
        return carry

    lax.fori_loop(0, blocks // 2, two, 0)

    q_all = mm(own[...], ws[:, 2 * PADDED :])
    merged = [None] * (PADDED // 128)
    for h in range(HEADS):
        first = SLOT * h // 128
        last = (SLOT * h + HDIM) // 128
        here = slice(128 * first, 128 * (last + 1))
        inside = (lane >= SLOT * h) & (lane < SLOT * h + HDIM)
        inside = inside[:, here]
        q = jnp.where(inside, q_all[:, here], 0.0).astype(BF16)
        scores = mm_nt(q, keys[:, here])
        top = jnp.max(scores, axis=-1, keepdims=True)
        raised = jnp.exp2((scores - top) * (SCORE_SCALE * LOG2E)).astype(BF16)
        found = mm(raised, vals[:, here])
        at = SLOT * h + HDIM - 128 * first
        found = jnp.where(inside, found * (1.0 / found[:, at : at + 1]), 0.0)
        for tile in range(first, last + 1):
            piece = found[:, 128 * (tile - first) : 128 * (tile - first + 1)]
            merged[tile] = piece if merged[tile] is None else merged[tile] + piece
    o_ref[...] = jnp.concatenate(merged, axis=-1).reshape(members, tokens, PADDED).astype(BF16)


def finish_kernel(
    seq_ref, att_ref, lat_ref, wemb_ref, ua_ref, va_ref, cb_ref, sb_ref, mod_ref, rows_ref, w_ref,
    o_ref, raw, left, right, sem,
):
    videos, tokens, width = o_ref.shape
    copy = pltpu.make_async_copy(w_ref.at[:, 3 * PADDED :], raw, sem)
    copy.start()
    s = seq_ref[0]
    place = ua_ref[pl.ds(s, 1), :] * cb_ref[...] + va_ref[pl.ds(s, 1), :] * sb_ref[...]
    att = att_ref[...].astype(F32).reshape(videos * tokens, PADDED).astype(BF16)
    copy.wait()
    for h in range(HEADS):
        both = mm(rows_ref[...], raw[2 * HDIM * h : 2 * HDIM * (h + 1), :]).astype(BF16)
        left[SLOT * h : SLOT * (h + 1), :] = both[:SLOT]
        right[SLOT * h : SLOT * (h + 1), :] = both[SLOT:]
    half = width // 2
    proj = jnp.concatenate([mm(att, left[...])[:, :half], mm(att, right[...])[:, :half]], axis=-1)
    gated = proj * mod_ref[5:6, :]
    for v in range(videos):
        latent = lat_ref[v].astype(F32).T.astype(BF16)
        embedded = mm(latent, wemb_ref[...]) + place
        o_ref[v] = (embedded + gated[tokens * v : tokens * (v + 1), :]).astype(BF16)


def position_factors(chunks, tokens, width):
    half = width // 2
    frequency = jnp.exp(jnp.arange(half, dtype=F32) * (-math.log(10000.0) / half))
    start = (jnp.arange(chunks, dtype=F32) * tokens)[:, None] * frequency[None, :]
    inner = jnp.arange(tokens, dtype=F32)[:, None] * frequency[None, :]
    sin_a, cos_a, sin_b, cos_b = jnp.sin(start), jnp.cos(start), jnp.sin(inner), jnp.cos(inner)
    ua = jnp.concatenate([sin_a, cos_a], axis=-1)
    va = jnp.concatenate([cos_a, -sin_a], axis=-1)
    cb = jnp.concatenate([cos_b, cos_b], axis=-1)
    sb = jnp.concatenate([sin_b, sin_b], axis=-1)
    return ua, va, cb, sb


def stack_halves(weight):
    half = weight.shape[-1] // 2
    return jnp.concatenate([weight[:, :half], weight[:, half:]], axis=0)


def pad_heads(columns):
    return jnp.pad(columns, ((0, 0), (0, 0), (0, SLOT - HDIM))).reshape(-1, PADDED)


def shards(
    t_qkv, hidden, latents, fresh, levels, alpha_bar, modulation, w_tout, w_final, w_embed, w_sqkv, w_sout,
):
    frames = lax.axis_size("queue")
    seqs = lax.axis_size("seq")
    queue_pos = lax.axis_index("queue")
    seq_pos = lax.axis_index("seq")
    videos, _, tokens, width = hidden.shape
    top_level = alpha_bar.shape[0] - 1
    pairs = frames // videos

    by_head = w_sqkv.reshape(-1, HEADS, 3, HDIM)
    sout = jnp.pad(stack_halves(w_sout), ((0, 0), (0, PADDED - width // 2)))
    w_shard = jnp.concatenate([pad_heads(by_head[:, :, i]) for i in (1, 2, 0)] + [sout], axis=-1)
    w_spatial = lax.all_gather(w_shard, "queue", axis=0, tiled=True)

    core = seq_pos % 2
    half = width // 2
    tout = stack_halves(lax.dynamic_slice_in_dim(w_tout, core * half, half, axis=1))
    width_part = t_qkv.shape[-1] // pairs
    sent = width_part + tout.shape[-1]
    packed = call(
        pack_kernel,
        jax.ShapeDtypeStruct((frames, tokens, sent), BF16),
        (t_qkv.reshape(videos, tokens, -1), tout),
        grid=(videos,),
        in_specs=[
            pl.BlockSpec((1, tokens, t_qkv.shape[-1]), lambda v: (v, 0, 0)),
            pl.BlockSpec(tout.shape, lambda v: (0, 0)),
        ],
        out_specs=pl.BlockSpec((pairs, tokens, sent), lambda v: (v, 0, 0)),
    )
    arrived = lax.all_to_all(packed, "queue", split_axis=0, concat_axis=0, tiled=True)
    row_pick = jnp.asarray(weight_rows(), BF16)

    attended, w_mine = call(
        temporal_kernel,
        (
            jax.ShapeDtypeStruct((frames, tokens, 2 * SLOT), BF16),
            jax.ShapeDtypeStruct((PADDED, half), BF16),
        ),
        (arrived, jnp.asarray(temporal_columns(), BF16), row_pick),
        scratch=[pltpu.VMEM((frames, tokens, 1024), F32), pltpu.VMEM((frames, tokens, 2 * SLOT), F32)],
        flops=4_000_000_000,
    )
    w_other = lax.ppermute(w_mine, "seq", [(i, i ^ 1) for i in range(seqs)])
    returned = lax.all_to_all(attended, "queue", split_axis=0, concat_axis=0, tiled=True)

    level = lax.dynamic_index_in_dim(levels, queue_pos, 0, keepdims=False)
    following = lax.dynamic_index_in_dim(
        jnp.concatenate([levels[1:], jnp.full((1,), top_level + 1, levels.dtype)]), queue_pos, 0, keepdims=False
    )
    mods = lax.dynamic_index_in_dim(modulation, level, 0, keepdims=False).astype(F32)
    new_mods = lax.dynamic_index_in_dim(modulation, following - 1, 0, keepdims=False).astype(F32)
    a = lax.dynamic_index_in_dim(alpha_bar, level, 0, keepdims=False)
    b = lax.dynamic_index_in_dim(alpha_bar, level - 1, 0, keepdims=False)
    coef = jnp.stack([jnp.sqrt(1.0 - a), 1.0 / jnp.sqrt(a), jnp.sqrt(b), jnp.sqrt(1.0 - b)])

    stepped = call(
        step_kernel,
        jax.ShapeDtypeStruct((videos, latents.shape[-1], tokens), BF16),
        (
            coef,
            core.reshape(1),
            returned,
            hidden.reshape(videos, tokens, width),
            latents.reshape(videos, tokens, -1).transpose(0, 2, 1),
            w_mine,
            w_other,
            w_final.T,
            mods,
        ),
        smem=(0, 1),
        flops=1_000_000_000,
    )
    arriving = lax.ppermute(stepped, "queue", [(f, f - 1) for f in range(1, frames)])
    queued = jnp.where(queue_pos == frames - 1, fresh.transpose(0, 2, 1), arriving)

    everyone = lax.all_to_all(
        jnp.tile(queued, (seqs // videos, 1, 1)), "seq", split_axis=0, concat_axis=0, tiled=True
    )
    ua, va, cb, sb = position_factors(seqs, tokens, width)
    groups = [[videos * g + i for i in range(videos)] for g in range(seqs // videos)]
    rows = seqs * tokens
    own_rows = videos * tokens
    spatial = call(
        spatial_kernel,
        jax.ShapeDtypeStruct((videos, tokens, PADDED), BF16),
        ((seq_pos // videos).reshape(1), everyone, w_embed, ua, va, cb, sb, new_mods, w_spatial),
        scratch=[
            pltpu.VMEM((own_rows, width), BF16),
            pltpu.VMEM((own_rows, width), BF16),
            pltpu.VMEM((own_rows, width), BF16),
            pltpu.VMEM((rows, PADDED), BF16),
            pltpu.VMEM((rows, PADDED), BF16),
            pltpu.VMEM((width, 3 * PADDED), BF16),
            pltpu.SemaphoreType.DMA,
        ],
        smem=(0,),
        hbm=(8,),
        flops=20_000_000_000,
    )
    heads_out = lax.all_to_all(
        spatial, "seq", split_axis=0, concat_axis=0, tiled=True, axis_index_groups=groups
    )
    block_out = call(
        finish_kernel,
        jax.ShapeDtypeStruct((videos, tokens, width), BF16),
        (seq_pos.reshape(1), heads_out, queued, w_embed, ua, va, cb, sb, new_mods, row_pick, w_spatial),
        scratch=[
            pltpu.VMEM((width, PADDED), BF16),
            pltpu.VMEM((PADDED, PADDED), BF16),
            pltpu.VMEM((PADDED, PADDED), BF16),
            pltpu.SemaphoreType.DMA,
        ],
        smem=(0,),
        hbm=(10,),
        flops=1_000_000_000,
    )
    return (
        queued.transpose(0, 2, 1).reshape(videos, 1, tokens, -1),
        block_out.reshape(videos, 1, tokens, width),
    )


def solution(mesh):
    in_specs = (
        P(None, "queue", "seq", None),
        P(None, "queue", "seq", None),
        P(None, "queue", "seq", None),
        P(None, "seq", None),
        P(),
        P(),
        P(),
        P("queue", None),
        P(),
        P(),
        P("queue", None),
        P("queue", None),
    )
    out_specs = (P(None, "queue", "seq", None), P(None, "queue", "seq", None))
    return jax.shard_map(shards, mesh=mesh, in_specs=in_specs, out_specs=out_specs, check_vma=False)
```

```python
import math

import jax
import jax.numpy as jnp
import numpy as np
from jax import lax
from jax.experimental import pallas as pl
from jax.experimental.pallas import tpu as pltpu
from jax.sharding import PartitionSpec as P

HEADS = 8
HDIM = 72
HALF = HDIM // 2
SLOT = 80
PADDED = HEADS * SLOT
SCORE_SCALE = 1.0 / math.sqrt(HDIM)
LOG2E = math.log2(math.e)
F32 = jnp.float32
BF16 = jnp.bfloat16
VMEM_LIMIT = 56 * 1024 * 1024


def mm(a, b):
    return jnp.dot(a, b, preferred_element_type=F32)


def mm_nt(a, b):
    return lax.dot_general(a, b, (((1,), (1,)), ((), ())), preferred_element_type=F32)


def call(kernel, out_shape, args, scratch=(), smem=(), hbm=(), flops=0, grid=None, in_specs=None, out_specs=None):
    moved = sum(a.size * a.dtype.itemsize for a in args)
    if in_specs is None:
        in_specs = [
            pl.BlockSpec(memory_space=pltpu.SMEM if i in smem else pl.ANY if i in hbm else pltpu.VMEM)
            for i in range(len(args))
        ]
        out_specs = jax.tree.map(lambda _: pl.BlockSpec(memory_space=pltpu.VMEM), out_shape)
    return pl.pallas_call(
        kernel,
        out_shape=out_shape,
        in_specs=in_specs,
        out_specs=out_specs,
        scratch_shapes=list(scratch),
        compiler_params=pltpu.CompilerParams(vmem_limit_bytes=VMEM_LIMIT),
        cost_estimate=pl.CostEstimate(flops=flops, bytes_accessed=moved, transcendentals=0),
        **({"grid": grid} if grid else {}),
    )(*args)


def layer_norm(values):
    center = values - jnp.mean(values, axis=-1, keepdims=True)
    spread = jnp.mean(center * center, axis=-1, keepdims=True)
    return center * lax.rsqrt(spread + 1e-06)


def pack_kernel(x_ref, w_ref, o_ref):
    width = x_ref.shape[-1] // o_ref.shape[0]
    weight = w_ref[...]
    for part in range(o_ref.shape[0]):
        o_ref[part, :, :width] = x_ref[0, :, part * width : (part + 1) * width]
        o_ref[part, :, width:] = weight


def temporal_columns():
    pick = np.zeros((6 * HDIM, 1024), np.float32)
    for head in range(2):
        base = 3 * HDIM * head
        for i in range(HDIM):
            pick[base + i, 256 * head + i] = 1.0
            pick[base + HDIM + i, 256 * head + 128 + i] = 1.0
            pick[base + 2 * HDIM + i, 512 + 256 * head + SLOT * head + i] = 1.0
    return pick


def weight_rows():
    pick = np.zeros((2 * SLOT, 2 * HDIM), np.float32)
    for shard in range(2):
        for i in range(HALF):
            pick[HALF * shard + i, HDIM * shard + i] = 1.0
            pick[SLOT + HALF * shard + i, HDIM * shard + HALF + i] = 1.0
    return pick


def temporal_kernel(x_ref, pick_ref, o_ref, parts, total):
    frames, tokens, _ = x_ref.shape
    pick = pick_ref[...]
    for f in range(frames):
        parts[f] = mm(x_ref[f, :, : 6 * HDIM], pick)
    rows = frames * 8
    same = (
        lax.broadcasted_iota(jnp.int32, (rows, rows), 0) % 8
        == lax.broadcasted_iota(jnp.int32, (rows, rows), 1) % 8
    )
    for block in range(tokens // 8):
        piece = parts[:, 8 * block : 8 * block + 8, :].reshape(rows, 1024).astype(BF16)
        out = None
        for head in range(2):
            q = piece[:, 256 * head : 256 * head + 128]
            k = piece[:, 256 * head + 128 : 256 * head + 256]
            v = piece[:, 512 + 256 * head : 512 + 256 * head + 2 * SLOT]
            scores = jnp.where(same, mm_nt(q, k) * SCORE_SCALE, -jnp.inf)
            top = jnp.max(scores, axis=-1, keepdims=True)
            raised = jnp.exp(scores - top)
            weights = (raised / jnp.sum(raised, axis=-1, keepdims=True)).astype(BF16)
            found = mm(weights, v)
            out = found if out is None else out + found
        total[:, 8 * block : 8 * block + 8, :] = out.reshape(frames, 8, 2 * SLOT)
    o_ref[...] = total[...].astype(BF16)


def unstack_kernel(x_ref, rows_ref, w_ref):
    shards, rows, width = x_ref.shape
    start = width - w_ref.shape[-1] // 2
    for h in range(shards // 2):
        pair = x_ref[2 * h : 2 * h + 2, :, start:].astype(F32).reshape(2 * rows, -1).astype(BF16)
        both = mm(rows_ref[...], pair)
        w_ref[SLOT * h : SLOT * (h + 1), :] = jnp.concatenate(
            [both[:SLOT], both[SLOT:]], axis=-1
        ).astype(BF16)


def step_kernel(coef_ref, core_ref, att_ref, hid_ref, lat_ref, mine_ref, other_ref, wf_ref, mod_ref, o_ref):
    videos, tokens, width = hid_ref.shape
    rows = videos * tokens
    pairs = att_ref.shape[0] // videos
    att = att_ref[...].astype(F32).reshape(videos, pairs, tokens, 2 * SLOT)
    own = far = None
    for p in range(pairs):
        part = att[:, p].reshape(rows, 2 * SLOT).astype(BF16)
        at = slice(2 * SLOT * p, 2 * SLOT * (p + 1))
        own_term, far_term = mm(part, mine_ref[at, :]), mm(part, other_ref[at, :])
        own = own_term if own is None else own + own_term
        far = far_term if far is None else far + far_term
    low = core_ref[0] == 0
    proj = jnp.concatenate([jnp.where(low, own, far), jnp.where(low, far, own)], axis=-1)
    residual = hid_ref[...].astype(F32).reshape(rows, width) + mod_ref[0:1, :] * proj
    final_in = (layer_norm(residual) * (1.0 + mod_ref[2:3, :]) + mod_ref[1:2, :]).astype(BF16)
    predicted = mm_nt(wf_ref[...], final_in)
    for v in range(videos):
        pred = predicted[:, tokens * v : tokens * (v + 1)]
        clean = (lat_ref[v].astype(F32) - coef_ref[0] * pred) * coef_ref[1]
        o_ref[v] = (coef_ref[2] * clean + coef_ref[3] * pred).astype(BF16)


def place_kernel(mod_ref, ua_ref, va_ref, cb_ref, sb_ref, o_ref):
    tokens = cb_ref.shape[0]
    members = o_ref.shape[0] // tokens
    gain = 1.0 + mod_ref[4:5, :]
    made = []
    for i in range(members):
        c = pl.program_id(0) * members + i
        place = ua_ref[pl.ds(c, 1), :] * cb_ref[...] + va_ref[pl.ds(c, 1), :] * sb_ref[...]
        made.append((place - jnp.mean(place, axis=-1, keepdims=True)) * gain)
    o_ref[...] = jnp.concatenate(made, axis=0).astype(BF16)


def prepare_kernel(group_ref, few_ref, p_ref, w_ref, few_out, q_out, kv_out):
    kv_out[...] = mm(p_ref[...], w_ref[:, : 2 * PADDED])

    @pl.when(pl.program_id(0) == group_ref[0])
    def _():
        q_out[...] = mm(p_ref[...], w_ref[:, 2 * PADDED :])

    @pl.when(pl.program_id(0) == 0)
    def _():
        few_out[...] = mm(few_ref[...], w_ref[...])


def spatial_kernel(
    group_ref, lat_ref, wemb_ref, ua_ref, va_ref, cb_ref, sb_ref, few_ref, pq_ref, pkv_ref,
    o_ref, held, keys, vals, qs, sem,
):
    chunks, patch, tokens = lat_ref.shape
    members = o_ref.shape[0]
    block = members * tokens
    blocks = chunks // members
    wemb = wemb_ref[...]
    lane = lax.broadcasted_iota(jnp.int32, (1, 2 * PADDED), 1)
    ones = jnp.where((lane >= PADDED) & (lane % SLOT == HDIM), 1.0, 0.0)
    few = few_ref[...]
    mix = few[:patch] + few[patch : 2 * patch]
    offset = few[2 * patch : 2 * patch + 1] + few[2 * patch + 8 : 2 * patch + 9]
    high = mix.astype(BF16).astype(F32)
    mix = jnp.concatenate([high, mix - high], axis=0).astype(BF16)
    kv_mix, q_mix = mix[:, : 2 * PADDED], mix[:, 2 * PADDED :]
    kv_offset, q_offset = offset[:, : 2 * PADDED] + ones, offset[:, 2 * PADDED :]

    def fetch(index):
        start = pl.multiple_of(index * block, block)
        slot = index % 2
        return pltpu.make_async_copy(pkv_ref.at[pl.ds(start, block), :], held.at[slot], sem.at[slot])

    fetch(0).start()

    def one(index, carry):
        @pl.when(index + 1 < blocks)
        def _():
            fetch(index + 1).start()

        latents, scales = [], []
        for i in range(members):
            c = index * members + i
            once = lat_ref[c].astype(F32)
            latent = jnp.concatenate([once, once], axis=0).T
            place = ua_ref[pl.ds(c, 1), :] * cb_ref[...] + va_ref[pl.ds(c, 1), :] * sb_ref[...]
            embedded = mm(latent.astype(BF16), wemb) + place
            center = embedded - jnp.mean(embedded, axis=-1, keepdims=True)
            scales.append(lax.rsqrt(jnp.mean(center * center, axis=-1, keepdims=True) + 1e-06))
            latents.append(latent)
        latent = jnp.concatenate(latents, axis=0).astype(BF16)
        scale = jnp.concatenate(scales, axis=0)
        fetch(index).wait()
        start = pl.multiple_of(index * block, block)
        kv = (mm(latent, kv_mix) + held[index % 2]) * scale + kv_offset
        keys[pl.ds(start, block), :] = kv[:, :PADDED].astype(BF16)
        vals[pl.ds(start, block), :] = kv[:, PADDED:].astype(BF16)

        @pl.when(index == group_ref[0])
        def _():
            qs[...] = ((mm(latent, q_mix) + pq_ref[...]) * scale + q_offset).astype(BF16)

        return carry

    lax.fori_loop(0, blocks, one, 0)

    lane = lane[:, :PADDED]
    q_all = qs[...].astype(F32)
    merged = [None] * (PADDED // 128)
    for h in range(HEADS):
        first = SLOT * h // 128
        last = (SLOT * h + HDIM) // 128
        here = slice(128 * first, 128 * (last + 1))
        inside = (lane >= SLOT * h) & (lane < SLOT * h + HDIM)
        inside = inside[:, here]
        q = jnp.where(inside, q_all[:, here], 0.0).astype(BF16)
        scores = mm_nt(q, keys[:, here])
        top = jnp.max(scores, axis=-1, keepdims=True)
        raised = jnp.exp2((scores - top) * (SCORE_SCALE * LOG2E)).astype(BF16)
        found = mm(raised, vals[:, here])
        at = SLOT * h + HDIM - 128 * first
        found = jnp.where(inside, found * (1.0 / found[:, at : at + 1]), 0.0)
        for tile in range(first, last + 1):
            piece = found[:, 128 * (tile - first) : 128 * (tile - first + 1)]
            merged[tile] = piece if merged[tile] is None else merged[tile] + piece
    o_ref[...] = jnp.concatenate(merged, axis=-1).reshape(members, tokens, PADDED).astype(BF16)


def residual_kernel(
    seq_ref, lat_ref, wemb_ref, ua_ref, va_ref, cb_ref, sb_ref, rows_ref, w_ref, emb_out, w_out, raw, sem
):
    videos, tokens, width = emb_out.shape
    copy = pltpu.make_async_copy(w_ref.at[:, 3 * PADDED :], raw, sem)
    copy.start()
    s = seq_ref[0]
    place = ua_ref[pl.ds(s, 1), :] * cb_ref[...] + va_ref[pl.ds(s, 1), :] * sb_ref[...]
    for v in range(videos):
        latent = lat_ref[v].astype(F32).T.astype(BF16)
        emb_out[v] = mm(latent, wemb_ref[...]) + place
    copy.wait()
    half = width // 2
    for h in range(HEADS):
        both = mm(rows_ref[...], raw[2 * HDIM * h : 2 * HDIM * (h + 1), :])
        w_out[SLOT * h : SLOT * (h + 1), :] = jnp.concatenate(
            [both[:SLOT, :half], both[SLOT:, :half]], axis=-1
        ).astype(BF16)


def finish_kernel(att_ref, emb_ref, mod_ref, w_ref, o_ref):
    videos, tokens, width = o_ref.shape
    att = att_ref[...].astype(F32).reshape(videos * tokens, PADDED).astype(BF16)
    gated = mm(att, w_ref[...]) * mod_ref[5:6, :]
    for v in range(videos):
        o_ref[v] = (emb_ref[v] + gated[tokens * v : tokens * (v + 1), :]).astype(BF16)


def position_factors(chunks, tokens, width):
    half = width // 2
    frequency = jnp.exp(jnp.arange(half, dtype=F32) * (-math.log(10000.0) / half))
    start = (jnp.arange(chunks, dtype=F32) * tokens)[:, None] * frequency[None, :]
    inner = jnp.arange(tokens, dtype=F32)[:, None] * frequency[None, :]
    sin_a, cos_a, sin_b, cos_b = jnp.sin(start), jnp.cos(start), jnp.sin(inner), jnp.cos(inner)
    ua = jnp.concatenate([sin_a, cos_a], axis=-1)
    va = jnp.concatenate([cos_a, -sin_a], axis=-1)
    cb = jnp.concatenate([cos_b, cos_b], axis=-1)
    sb = jnp.concatenate([sin_b, sin_b], axis=-1)
    return ua, va, cb, sb


def stack_halves(weight):
    half = weight.shape[-1] // 2
    return jnp.concatenate([weight[:, :half], weight[:, half:]], axis=0)


def rounding_rest(values):
    return values - lax.reduce_precision(values, 8, 7)


def pad_heads(columns):
    return jnp.pad(columns, ((0, 0), (0, 0), (0, SLOT - HDIM))).reshape(-1, PADDED)


def shards(
    t_qkv, hidden, latents, fresh, levels, alpha_bar, modulation, w_tout, w_final, w_embed, w_sqkv, w_sout,
):
    frames = lax.axis_size("queue")
    seqs = lax.axis_size("seq")
    queue_pos = lax.axis_index("queue")
    seq_pos = lax.axis_index("seq")
    videos, _, tokens, width = hidden.shape
    top_level = alpha_bar.shape[0] - 1
    pairs = frames // videos

    core = seq_pos % 2
    half = width // 2
    tout = stack_halves(lax.dynamic_slice_in_dim(w_tout, core * half, half, axis=1))
    width_part = t_qkv.shape[-1] // pairs
    sent = width_part + tout.shape[-1]
    packed = call(
        pack_kernel,
        jax.ShapeDtypeStruct((frames, tokens, sent), BF16),
        (t_qkv.reshape(videos, tokens, -1), tout),
        grid=(videos,),
        in_specs=[
            pl.BlockSpec((1, tokens, t_qkv.shape[-1]), lambda v: (v, 0, 0)),
            pl.BlockSpec(tout.shape, lambda v: (0, 0)),
        ],
        out_specs=pl.BlockSpec((pairs, tokens, sent), lambda v: (v, 0, 0)),
    )
    w_sqkv, w_sout, packed = lax.optimization_barrier((w_sqkv, w_sout, packed))
    by_head = w_sqkv.reshape(-1, HEADS, 3, HDIM)
    sout = jnp.pad(stack_halves(w_sout), ((0, 0), (0, PADDED - width // 2)))
    w_shard = jnp.concatenate([pad_heads(by_head[:, :, i]) for i in (1, 2, 0)] + [sout], axis=-1)
    w_spatial = lax.all_gather(w_shard, "queue", axis=0, tiled=True)

    arrived = lax.all_to_all(packed, "queue", split_axis=0, concat_axis=0, tiled=True)
    row_pick = jnp.asarray(weight_rows(), BF16)

    attended = call(
        temporal_kernel,
        jax.ShapeDtypeStruct((frames, tokens, 2 * SLOT), BF16),
        (arrived, jnp.asarray(temporal_columns(), BF16)),
        scratch=[pltpu.VMEM((frames, tokens, 1024), F32), pltpu.VMEM((frames, tokens, 2 * SLOT), F32)],
        flops=4_000_000_000,
    )
    w_mine = call(
        unstack_kernel,
        jax.ShapeDtypeStruct((PADDED, half), BF16),
        (arrived, row_pick),
        flops=1_000_000_000,
    )
    w_other = lax.ppermute(w_mine, "seq", [(i, i ^ 1) for i in range(seqs)])
    returned = lax.all_to_all(attended, "queue", split_axis=0, concat_axis=0, tiled=True)

    level = lax.dynamic_index_in_dim(levels, queue_pos, 0, keepdims=False)
    following = lax.dynamic_index_in_dim(
        jnp.concatenate([levels[1:], jnp.full((1,), top_level + 1, levels.dtype)]), queue_pos, 0, keepdims=False
    )
    mods = lax.dynamic_index_in_dim(modulation, level, 0, keepdims=False).astype(F32)
    new_mods = lax.dynamic_index_in_dim(modulation, following - 1, 0, keepdims=False).astype(F32)
    a = lax.dynamic_index_in_dim(alpha_bar, level, 0, keepdims=False)
    b = lax.dynamic_index_in_dim(alpha_bar, level - 1, 0, keepdims=False)
    coef = jnp.stack([jnp.sqrt(1.0 - a), 1.0 / jnp.sqrt(a), jnp.sqrt(b), jnp.sqrt(1.0 - b)])

    stepped = call(
        step_kernel,
        jax.ShapeDtypeStruct((videos, latents.shape[-1], tokens), BF16),
        (
            coef,
            core.reshape(1),
            returned,
            hidden.reshape(videos, tokens, width),
            latents.reshape(videos, tokens, -1).transpose(0, 2, 1),
            w_mine,
            w_other,
            w_final.T,
            mods,
        ),
        smem=(0, 1),
        flops=1_000_000_000,
    )
    arriving = lax.ppermute(stepped, "queue", [(f, f - 1) for f in range(1, frames)])
    queued = jnp.where(queue_pos == frames - 1, fresh.transpose(0, 2, 1), arriving)

    everyone = lax.all_to_all(
        jnp.tile(queued, (seqs // videos, 1, 1)), "seq", split_axis=0, concat_axis=0, tiled=True
    )
    ua, va, cb, sb = position_factors(seqs, tokens, width)
    groups = [[videos * g + i for i in range(videos)] for g in range(seqs // videos)]
    rows = seqs * tokens
    own_rows = videos * tokens
    group = (seq_pos // videos).reshape(1)
    placed = call(
        place_kernel,
        jax.ShapeDtypeStruct((rows, width), BF16),
        (new_mods, ua, va, cb, sb),
        grid=(rows // own_rows,),
        in_specs=[pl.BlockSpec(a.shape, lambda i: (0, 0)) for a in (new_mods, ua, va, cb, sb)],
        out_specs=pl.BlockSpec((own_rows, width), lambda i: (i, 0)),
        flops=100_000_000,
    )
    gain, shift = 1.0 + new_mods[4:5], new_mods[3:4]
    emb_f32 = w_embed.astype(F32)
    centered = (emb_f32 - jnp.mean(emb_f32, axis=-1, keepdims=True)) * gain
    eight = jnp.zeros((7, width), F32)
    few = [centered, rounding_rest(centered), shift, eight, rounding_rest(shift), eight]
    few = jnp.concatenate(few, axis=0).astype(BF16)
    few_out, pq, pkv = call(
        prepare_kernel,
        (
            jax.ShapeDtypeStruct((few.shape[0], 3 * PADDED), F32),
            jax.ShapeDtypeStruct((own_rows, PADDED), F32),
            jax.ShapeDtypeStruct((rows, 2 * PADDED), F32),
        ),
        (group, few, placed, w_spatial),
        grid=(rows // own_rows,),
        in_specs=[
            pl.BlockSpec(memory_space=pltpu.SMEM),
            pl.BlockSpec(few.shape, lambda i: (0, 0)),
            pl.BlockSpec((own_rows, width), lambda i: (i, 0)),
            pl.BlockSpec((width, 3 * PADDED), lambda i: (0, 0)),
        ],
        out_specs=(
            pl.BlockSpec((few.shape[0], 3 * PADDED), lambda i: (0, 0)),
            pl.BlockSpec((own_rows, PADDED), lambda i: (0, 0)),
            pl.BlockSpec((own_rows, 2 * PADDED), lambda i: (i, 0)),
        ),
        flops=8_000_000_000,
    )
    wemb_twice = jnp.concatenate([w_embed, jnp.zeros_like(w_embed)], axis=0)
    spatial = call(
        spatial_kernel,
        jax.ShapeDtypeStruct((videos, tokens, PADDED), BF16),
        (group, everyone, wemb_twice, ua, va, cb, sb, few_out, pq, pkv),
        scratch=[
            pltpu.VMEM((2, own_rows, 2 * PADDED), F32),
            pltpu.VMEM((rows, PADDED), BF16),
            pltpu.VMEM((rows, PADDED), BF16),
            pltpu.VMEM((own_rows, PADDED), BF16),
            pltpu.SemaphoreType.DMA((2,)),
        ],
        smem=(0,),
        hbm=(9,),
        flops=20_000_000_000,
    )
    heads_out = lax.all_to_all(
        spatial, "seq", split_axis=0, concat_axis=0, tiled=True, axis_index_groups=groups
    )
    late, _ = lax.optimization_barrier((w_spatial, spatial))
    embedded, w_s = call(
        residual_kernel,
        (
            jax.ShapeDtypeStruct((videos, tokens, width), F32),
            jax.ShapeDtypeStruct((PADDED, width), BF16),
        ),
        (seq_pos.reshape(1), queued, w_embed, ua, va, cb, sb, row_pick, late),
        scratch=[pltpu.VMEM((width, PADDED), BF16), pltpu.SemaphoreType.DMA],
        smem=(0,),
        hbm=(8,),
        flops=1_000_000_000,
    )
    block_out = call(
        finish_kernel,
        jax.ShapeDtypeStruct((videos, tokens, width), BF16),
        (heads_out, embedded, new_mods, w_s),
        flops=1_000_000_000,
    )
    return (
        queued.transpose(0, 2, 1).reshape(videos, 1, tokens, -1),
        block_out.reshape(videos, 1, tokens, width),
    )


def solution(mesh):
    in_specs = (
        P(None, "queue", "seq", None),
        P(None, "queue", "seq", None),
        P(None, "queue", "seq", None),
        P(None, "seq", None),
        P(),
        P(),
        P(),
        P("queue", None),
        P(),
        P(),
        P("queue", None),
        P("queue", None),
    )
    out_specs = (P(None, "queue", "seq", None), P(None, "queue", "seq", None))
    return jax.shard_map(shards, mesh=mesh, in_specs=in_specs, out_specs=out_specs, check_vma=False)
```

```python
import math

import jax
import jax.numpy as jnp
import numpy as np
from jax import lax
from jax.experimental import pallas as pl
from jax.experimental.pallas import tpu as pltpu
from jax.sharding import PartitionSpec as P

HEADS = 8
HDIM = 72
HALF = HDIM // 2
SLOT = 80
PADDED = HEADS * SLOT
SCORE_SCALE = 1.0 / math.sqrt(HDIM)
LOG2E = math.log2(math.e)
F32 = jnp.float32
BF16 = jnp.bfloat16
MIB = 1024 * 1024


def mm(a, b):
    return jnp.dot(a, b, preferred_element_type=F32)


def mm_nt(a, b):
    return lax.dot_general(a, b, (((1,), (1,)), ((), ())), preferred_element_type=F32)


def call(kernel, out_shape, args, scratch=(), smem=(), hbm=(), hbm_out=(), flops=0, vmem=24, grid=None, in_specs=None, out_specs=None):
    moved = sum(a.size * a.dtype.itemsize for a in args)
    if in_specs is None:
        in_specs = [
            pl.BlockSpec(memory_space=pltpu.SMEM if i in smem else pl.ANY if i in hbm else pltpu.VMEM)
            for i in range(len(args))
        ]
        if isinstance(out_shape, tuple):
            out_specs = tuple(
                pl.BlockSpec(memory_space=pl.ANY if i in hbm_out else pltpu.VMEM) for i in range(len(out_shape))
            )
        else:
            out_specs = pl.BlockSpec(memory_space=pltpu.VMEM)
    return pl.pallas_call(
        kernel,
        out_shape=out_shape,
        in_specs=in_specs,
        out_specs=out_specs,
        scratch_shapes=list(scratch),
        compiler_params=pltpu.CompilerParams(vmem_limit_bytes=vmem * MIB),
        cost_estimate=pl.CostEstimate(flops=flops, bytes_accessed=moved, transcendentals=0),
        **({"grid": grid} if grid else {}),
    )(*args)


def layer_norm(values):
    center = values - jnp.mean(values, axis=-1, keepdims=True)
    spread = jnp.mean(center * center, axis=-1, keepdims=True)
    return center * lax.rsqrt(spread + 1e-06)


def pack_kernel(core_ref, x_ref, w_ref, o_ref):
    width = x_ref.shape[-1] // o_ref.shape[0]
    shard = w_ref[...].astype(F32)
    half = shard.shape[-1] // 2
    shard = jnp.where(core_ref[0] == 0, shard[:, :half], shard[:, half:])
    weight = jnp.concatenate([shard[:, : half // 2], shard[:, half // 2 :]], axis=0).astype(BF16)
    for part in range(o_ref.shape[0]):
        o_ref[part, :, :width] = x_ref[0, :, part * width : (part + 1) * width]
        o_ref[part, :, width:] = weight


def gather_kernel(w_ref, sout_ref, o_ref):
    rows = o_ref.shape[0]
    blank = jnp.zeros((rows, SLOT - HDIM), BF16)
    for i, part in enumerate((1, 2, 0)):
        pieces = []
        for h in range(HEADS):
            at = HDIM * (3 * h + part)
            pieces += [w_ref[:, at : at + HDIM], blank]
        o_ref[:, PADDED * i : PADDED * (i + 1)] = jnp.concatenate(pieces, axis=-1)
    sout = sout_ref[...].astype(F32)
    half = sout.shape[-1] // 2
    sout = jnp.concatenate([sout[:, :half], sout[:, half:]], axis=0)
    sout = jnp.concatenate([sout, jnp.zeros((rows, PADDED - half), F32)], axis=-1)
    o_ref[:, 3 * PADDED :] = sout.astype(BF16)


def temporal_columns():
    pick = np.zeros((6 * HDIM, 768), np.float32)
    for head in range(2):
        base = 3 * HDIM * head
        for i in range(HDIM):
            pick[base + i, 256 * head + i] = 1.0
            pick[base + HDIM + i, 256 * head + 128 + i] = 1.0
            pick[base + 2 * HDIM + i, 512 + SLOT * head + i] = 1.0
    return pick


def weight_rows():
    pick = np.zeros((2 * SLOT, 256), np.float32)
    for shard in range(2):
        for i in range(HALF):
            pick[HALF * shard + i, HDIM * shard + i] = 1.0
            pick[SLOT + HALF * shard + i, HDIM * shard + HALF + i] = 1.0
    return pick


def temporal_kernel(x_ref, pick_ref, o_ref, parts, total):
    frames, tokens, _ = x_ref.shape
    flat = x_ref[:, :, : 6 * HDIM].astype(F32).reshape(frames * tokens, 6 * HDIM).astype(BF16)
    parts[...] = mm(flat, pick_ref[...]).reshape(frames, tokens, -1)
    rows = frames * 8
    first = lax.broadcasted_iota(jnp.int32, (1, 2 * SLOT), 1) < SLOT
    same = (
        lax.broadcasted_iota(jnp.int32, (rows, rows), 0) % 8
        == lax.broadcasted_iota(jnp.int32, (rows, rows), 1) % 8
    )
    for block in range(tokens // 8):
        piece = parts[:, 8 * block : 8 * block + 8, :].reshape(rows, -1).astype(BF16)
        v = piece[:, 512 : 512 + 2 * SLOT]
        out = None
        for head in range(2):
            q = piece[:, 256 * head : 256 * head + 128]
            k = piece[:, 256 * head + 128 : 256 * head + 256]
            scores = jnp.where(same, mm_nt(q, k) * SCORE_SCALE, -jnp.inf)
            top = jnp.max(scores, axis=-1, keepdims=True)
            raised = jnp.exp(scores - top)
            weights = (raised / jnp.sum(raised, axis=-1, keepdims=True)).astype(BF16)
            found = mm(weights, v)
            out = found if out is None else jnp.where(first, out, found)
        total[:, 8 * block : 8 * block + 8, :] = out.reshape(frames, 8, 2 * SLOT)
    o_ref[...] = total[...].astype(BF16)


def unstack_kernel(x_ref, rows_ref, w_ref):
    shards, rows, width = x_ref.shape
    start = 6 * HDIM
    blank = jnp.zeros((SLOT, w_ref.shape[-1] - 2 * (width - start)), F32)
    for h in range(shards // 2):
        pair = x_ref[2 * h : 2 * h + 2, :, start:].astype(F32).reshape(2 * rows, -1).astype(BF16)
        both = mm(rows_ref[:, : 2 * rows], pair)
        w_ref[SLOT * h : SLOT * (h + 1), :] = jnp.concatenate(
            [both[:SLOT], both[SLOT:], blank], axis=-1
        ).astype(BF16)


def step_kernel(coef_ref, core_ref, att_ref, hid_ref, lat_ref, mine_ref, other_ref, wf_ref, mod_ref, o_ref):
    videos, tokens, width = hid_ref.shape
    rows = videos * tokens
    pairs = att_ref.shape[0] // videos
    att = att_ref[...].astype(F32).reshape(videos, pairs, tokens, 2 * SLOT)
    own = far = None
    for p in range(pairs):
        part = att[:, p].reshape(rows, 2 * SLOT).astype(BF16)
        at = slice(2 * SLOT * p, 2 * SLOT * (p + 1))
        own_term, far_term = mm(part, mine_ref[at, :]), mm(part, other_ref[at, :])
        own = own_term if own is None else own + own_term
        far = far_term if far is None else far + far_term
    low = core_ref[0] == 0
    half = width // 2
    proj = jnp.concatenate([jnp.where(low, own, far)[:, :half], jnp.where(low, far, own)[:, :half]], axis=-1)
    residual = hid_ref[...].astype(F32).reshape(rows, width) + mod_ref[0:1, :] * proj
    final_in = (layer_norm(residual) * (1.0 + mod_ref[2:3, :]) + mod_ref[1:2, :]).astype(BF16)
    predicted = mm_nt(wf_ref[...], final_in)
    for v in range(videos):
        pred = predicted[:, tokens * v : tokens * (v + 1)]
        clean = (lat_ref[v].astype(F32) - coef_ref[0] * pred) * coef_ref[1]
        o_ref[v] = (coef_ref[2] * clean + coef_ref[3] * pred).astype(BF16)


def place_kernel(mod_ref, wemb_ref, ua_ref, va_ref, cb_ref, sb_ref, o_ref, sums_ref):
    tokens, width = cb_ref.shape
    members = o_ref.shape[0] // tokens
    gain = 1.0 + mod_ref[4:5, :]
    made = []
    for i in range(members):
        c = pl.program_id(0) * members + i
        place = ua_ref[pl.ds(c, 1), :] * cb_ref[...] + va_ref[pl.ds(c, 1), :] * sb_ref[...]
        center = place - jnp.mean(place, axis=-1, keepdims=True)
        made.append(center * gain)
        high = center.astype(BF16)
        low = (center - high.astype(F32)).astype(BF16)
        cross = (mm_nt(high, wemb_ref[...]) + mm_nt(low, wemb_ref[...])) * (2.0 / width)
        square = jnp.mean(center * center, axis=-1, keepdims=True)
        blank = jnp.zeros((tokens, 7), F32)
        sums_ref[i] = jnp.concatenate([cross, square, blank], axis=-1).T
    o_ref[...] = jnp.concatenate(made, axis=0).astype(BF16)


def prepare_kernel(group_ref, few_ref, p_ref, w_ref, few_out, q_out, kv_out, p, w, made, p_sem, w_sem, out_sem):
    rows = q_out.shape[0]
    steps = made.shape[0] // 2
    step = made.shape[1]

    def load_w(part):
        at = slice(PADDED * part, PADDED * (part + 1))
        return pltpu.make_async_copy(w_ref.at[:, at], w.at[:, at], w_sem.at[part])

    def load_p(part):
        at = slice(step * part, step * (part + 1))
        return pltpu.make_async_copy(p_ref.at[at, :], p.at[at, :], p_sem.at[part])

    def store(part, i):
        at = kv_out.at[step * i : step * (i + 1), PADDED * part : PADDED * (part + 1)]
        slot = steps * part + i
        return pltpu.make_async_copy(made.at[slot], at, out_sem.at[slot])

    load_w(0).start()
    for i in range(steps):
        load_p(i).start()
    load_w(1).start()
    load_w(2).start()
    for part in range(2):
        load_w(part).wait()
        for i in range(steps):
            if part == 0:
                load_p(i).wait()
            here = slice(step * i, step * (i + 1))
            made[steps * part + i] = mm(p[here, :], w[:, PADDED * part : PADDED * (part + 1)]).astype(BF16)
            store(part, i).start()
    load_w(2).wait()
    start = pl.multiple_of(group_ref[0] * rows, rows)
    q_out[...] = mm(p[pl.ds(start, rows), :], w[:, 2 * PADDED :])
    few_out[...] = mm(few_ref[...], w[...])
    for part in range(2):
        for i in range(steps):
            store(part, i).wait()


def spatial_kernel(
    group_ref, lat_ref, gram_ref, sums_ref, few_ref, pq_ref, pkv_ref,
    o_ref, held, columns, keys, vals, sem,
):
    chunks, patch, tokens = lat_ref.shape
    members = o_ref.shape[0]
    block = members * tokens
    blocks = chunks // members

    def fetch(index):
        start = pl.multiple_of(index * block, block)
        return pltpu.make_async_copy(pkv_ref.at[pl.ds(start, block), :], held.at[index], sem.at[index])

    for i in range(blocks):
        fetch(i).start()

    gram = gram_ref[...]
    for c in range(chunks):
        once = lat_ref[c].astype(F32)
        twice = jnp.concatenate([once, once], axis=0)
        sums = sums_ref[c]
        mixed = mm(gram, twice.astype(BF16)) + sums[:patch]
        variance = jnp.sum(mixed * once, axis=0, keepdims=True) + sums[patch : patch + 1]
        scale = lax.rsqrt(jnp.maximum(variance, 0.0) + 1e-06)
        rows = jnp.concatenate([twice, jnp.broadcast_to(scale, (8, tokens))], axis=0)
        columns[tokens * c : tokens * (c + 1), :] = rows.T

    lane = lax.broadcasted_iota(jnp.int32, (1, 2 * PADDED), 1)
    ones = jnp.where((lane >= PADDED) & (lane % SLOT == HDIM), 1.0, 0.0)
    few = few_ref[...]
    mix = few[:patch] + few[patch : 2 * patch]
    offset = few[2 * patch : 2 * patch + 1] + few[2 * patch + 8 : 2 * patch + 9]
    high = mix.astype(BF16).astype(F32)
    mix = jnp.concatenate([high, mix - high], axis=0).astype(BF16)
    kv_mix, q_mix = mix[:, : 2 * PADDED], mix[:, 2 * PADDED :]
    kv_offset, q_offset = offset[:, : 2 * PADDED] + ones, offset[:, 2 * PADDED :]

    def one(index, carry):
        start = pl.multiple_of(index * block, block)
        column = columns[pl.ds(start, block), :]
        latent, scale = column[:, : 2 * patch].astype(BF16), column[:, 2 * patch : 2 * patch + 1]
        mixed = mm(latent, kv_mix)
        fetch(index).wait()
        kv = (mixed + held[index].astype(F32)) * scale + kv_offset
        keys[pl.ds(start, block), :] = kv[:, :PADDED].astype(BF16)
        vals[pl.ds(start, block), :] = kv[:, PADDED:].astype(BF16)
        return carry

    lax.fori_loop(0, blocks, one, 0)

    column = columns[pl.ds(pl.multiple_of(group_ref[0] * block, block), block), :]
    latent, scale = column[:, : 2 * patch].astype(BF16), column[:, 2 * patch : 2 * patch + 1]
    q_all = (mm(latent, q_mix) + pq_ref[...]) * scale + q_offset
    q_all = q_all.astype(BF16).astype(F32)
    lane = lane[:, :PADDED]
    merged = [None] * (PADDED // 128)

    def window(h):
        first = SLOT * h // 128
        last = (SLOT * h + HDIM) // 128
        here = slice(128 * first, 128 * (last + 1))
        inside = (lane >= SLOT * h) & (lane < SLOT * h + HDIM)
        return first, last, here, inside[:, here]

    def score(h):
        _, _, here, inside = window(h)
        return mm_nt(jnp.where(inside, q_all[:, here], 0.0).astype(BF16), keys[:, here])

    def weigh(scores):
        top = jnp.max(scores, axis=-1, keepdims=True)
        return jnp.exp2((scores - top) * (SCORE_SCALE * LOG2E)).astype(BF16)

    def blend(h, raised):
        first, last, here, inside = window(h)
        found = mm(raised, vals[:, here])
        at = SLOT * h + HDIM - 128 * first
        found = jnp.where(inside, found * (1.0 / found[:, at : at + 1]), 0.0)
        for tile in range(first, last + 1):
            piece = found[:, 128 * (tile - first) : 128 * (tile - first + 1)]
            merged[tile] = piece if merged[tile] is None else merged[tile] + piece

    scores = score(0)
    raised = None
    for h in range(HEADS):
        following = score(h + 1) if h + 1 < HEADS else None
        if raised is not None:
            blend(h - 1, raised)
        raised = weigh(scores)
        scores = following
    blend(HEADS - 1, raised)
    o_ref[...] = jnp.concatenate(merged, axis=-1).reshape(members, tokens, PADDED).astype(BF16)


def projection_kernel(rows_ref, w_ref, w_out, raw, sem):
    copy = pltpu.make_async_copy(w_ref.at[:, 3 * PADDED :], raw, sem)
    copy.start()
    copy.wait()
    half = w_out.shape[-1] // 2
    for h in range(HEADS):
        both = mm(rows_ref[:, : 2 * HDIM], raw[2 * HDIM * h : 2 * HDIM * (h + 1), :])
        w_out[SLOT * h : SLOT * (h + 1), :] = jnp.concatenate(
            [both[:SLOT, :half], both[SLOT:, :half]], axis=-1
        ).astype(BF16)


def finish_kernel(
    seq_ref, att_ref, lat_ref, wemb_ref, ua_ref, va_ref, cb_ref, sb_ref, mod_ref, w_ref, o_ref
):
    videos, tokens, width = o_ref.shape
    s = seq_ref[0]
    place = ua_ref[pl.ds(s, 1), :] * cb_ref[...] + va_ref[pl.ds(s, 1), :] * sb_ref[...]
    gate = mod_ref[5:6, :]
    att = att_ref[...].astype(F32).reshape(videos * tokens, PADDED).astype(BF16)
    embedded = [mm(lat_ref[v].astype(F32).T.astype(BF16), wemb_ref[...]) + place for v in range(videos)]
    gated = mm(att, w_ref[...]) * gate
    for v in range(videos):
        o_ref[v] = (embedded[v] + gated[tokens * v : tokens * (v + 1), :]).astype(BF16)


def position_factors(chunks, tokens, width):
    half = width // 2
    frequency = jnp.exp(jnp.arange(half, dtype=F32) * (-math.log(10000.0) / half))
    start = (jnp.arange(chunks, dtype=F32) * tokens)[:, None] * frequency[None, :]
    inner = jnp.arange(tokens, dtype=F32)[:, None] * frequency[None, :]
    sin_a, cos_a, sin_b, cos_b = jnp.sin(start), jnp.cos(start), jnp.sin(inner), jnp.cos(inner)
    ua = jnp.concatenate([sin_a, cos_a], axis=-1)
    va = jnp.concatenate([cos_a, -sin_a], axis=-1)
    cb = jnp.concatenate([cos_b, cos_b], axis=-1)
    sb = jnp.concatenate([sin_b, sin_b], axis=-1)
    return ua, va, cb, sb


def rounding_rest(values):
    return values - lax.reduce_precision(values, 8, 7)


def shards(
    t_qkv, hidden, latents, fresh, levels, alpha_bar, modulation, w_tout, w_final, w_embed, w_sqkv, w_sout,
):
    frames = lax.axis_size("queue")
    seqs = lax.axis_size("seq")
    queue_pos = lax.axis_index("queue")
    seq_pos = lax.axis_index("seq")
    videos, _, tokens, width = hidden.shape
    top_level = alpha_bar.shape[0] - 1
    pairs = frames // videos

    core = seq_pos % 2
    half = width // 2
    width_part = t_qkv.shape[-1] // pairs
    sent = width_part + half // 2
    packed = call(
        pack_kernel,
        jax.ShapeDtypeStruct((frames, tokens, sent), BF16),
        (core.reshape(1), t_qkv.reshape(videos, tokens, -1), w_tout),
        grid=(videos,),
        in_specs=[
            pl.BlockSpec(memory_space=pltpu.SMEM),
            pl.BlockSpec((1, tokens, t_qkv.shape[-1]), lambda v: (v, 0, 0)),
            pl.BlockSpec(w_tout.shape, lambda v: (0, 0)),
        ],
        out_specs=pl.BlockSpec((pairs, tokens, sent), lambda v: (v, 0, 0)),
    )
    w_sqkv, w_sout, packed = lax.optimization_barrier((w_sqkv, w_sout, packed))
    w_shard = call(
        gather_kernel,
        jax.ShapeDtypeStruct((w_sqkv.shape[0], 4 * PADDED), BF16),
        (w_sqkv, w_sout),
    )
    w_spatial = lax.all_gather(w_shard, "queue", axis=0, tiled=True)

    arrived = lax.all_to_all(packed, "queue", split_axis=0, concat_axis=0, tiled=True)
    row_pick = jnp.asarray(weight_rows(), BF16)

    level = lax.dynamic_index_in_dim(levels, queue_pos, 0, keepdims=False)
    following = lax.dynamic_index_in_dim(
        jnp.concatenate([levels[1:], jnp.full((1,), top_level + 1, levels.dtype)]), queue_pos, 0, keepdims=False
    )
    mods = lax.dynamic_index_in_dim(modulation, level, 0, keepdims=False).astype(F32)
    new_mods = lax.dynamic_index_in_dim(modulation, following - 1, 0, keepdims=False).astype(F32)
    a = lax.dynamic_index_in_dim(alpha_bar, level, 0, keepdims=False)
    b = lax.dynamic_index_in_dim(alpha_bar, level - 1, 0, keepdims=False)
    coef = jnp.stack([jnp.sqrt(1.0 - a), 1.0 / jnp.sqrt(a), jnp.sqrt(b), jnp.sqrt(1.0 - b)])

    ua, va, cb, sb = position_factors(seqs, tokens, width)
    rows = seqs * tokens
    own_rows = videos * tokens
    placed, sums = call(
        place_kernel,
        (
            jax.ShapeDtypeStruct((rows, width), BF16),
            jax.ShapeDtypeStruct((seqs, 24, tokens), F32),
        ),
        (new_mods, w_embed, ua, va, cb, sb),
        grid=(rows // own_rows,),
        in_specs=[pl.BlockSpec(a.shape, lambda i: (0, 0)) for a in (new_mods, w_embed, ua, va, cb, sb)],
        out_specs=(
            pl.BlockSpec((own_rows, width), lambda i: (i, 0)),
            pl.BlockSpec((videos, 24, tokens), lambda i: (i, 0, 0)),
        ),
        flops=100_000_000,
    )
    gain, shift = 1.0 + new_mods[4:5], new_mods[3:4]
    emb_f32 = w_embed.astype(F32)
    centered = emb_f32 - jnp.mean(emb_f32, axis=-1, keepdims=True)
    gram = jnp.dot(centered, centered.T, precision=lax.Precision.HIGHEST) * (1.0 / width)
    gram = jnp.concatenate([gram, rounding_rest(gram)], axis=-1).astype(BF16)
    centered = centered * gain
    eight = jnp.zeros((7, width), F32)
    few = [centered, rounding_rest(centered), shift, eight, rounding_rest(shift), eight]
    few = jnp.concatenate(few, axis=0).astype(BF16)
    latents_t = latents.reshape(videos, tokens, -1).transpose(0, 2, 1)
    fresh_t = fresh.transpose(0, 2, 1)
    w_final_t = w_final.T
    early = (arrived, placed, sums, few, gram, mods, new_mods, coef, latents_t, fresh_t, w_final_t)
    early = lax.optimization_barrier(early)
    arrived, placed, sums, few, gram, mods, new_mods, coef, latents_t, fresh_t, w_final_t = early

    attended = call(
        temporal_kernel,
        jax.ShapeDtypeStruct((frames, tokens, 2 * SLOT), BF16),
        (arrived, jnp.asarray(temporal_columns(), BF16)),
        scratch=[pltpu.VMEM((frames, tokens, 768), F32), pltpu.VMEM((frames, tokens, 2 * SLOT), F32)],
        flops=4_000_000_000,
    )
    stacked, attended = lax.optimization_barrier((arrived, attended))
    w_mine = call(
        unstack_kernel,
        jax.ShapeDtypeStruct((PADDED, PADDED), BF16),
        (stacked, row_pick),
        flops=20_000_000_000,
    )
    w_other = lax.ppermute(w_mine, "seq", [(i, i ^ 1) for i in range(seqs)])
    returned = lax.all_to_all(attended, "queue", split_axis=0, concat_axis=0, tiled=True)

    stepped = call(
        step_kernel,
        jax.ShapeDtypeStruct((videos, latents.shape[-1], tokens), BF16),
        (
            coef,
            core.reshape(1),
            returned,
            hidden.reshape(videos, tokens, width),
            latents_t,
            w_mine,
            w_other,
            w_final_t,
            mods,
        ),
        smem=(0, 1),
        flops=1_000_000_000,
    )
    arriving = lax.ppermute(stepped, "queue", [(f, f - 1) for f in range(1, frames)])
    queued = jnp.where(queue_pos == frames - 1, fresh_t, arriving)

    everyone = lax.all_to_all(
        jnp.tile(queued, (seqs // videos, 1, 1)), "seq", split_axis=0, concat_axis=0, tiled=True
    )
    groups = [[videos * g + i for i in range(videos)] for g in range(seqs // videos)]
    group = (seq_pos // videos).reshape(1)
    few_out, pq, pkv = call(
        prepare_kernel,
        (
            jax.ShapeDtypeStruct((few.shape[0], 3 * PADDED), F32),
            jax.ShapeDtypeStruct((own_rows, PADDED), F32),
            jax.ShapeDtypeStruct((rows, 2 * PADDED), BF16),
        ),
        (group, few, placed, w_spatial),
        scratch=[
            pltpu.VMEM((rows, width), BF16),
            pltpu.VMEM((width, 3 * PADDED), BF16),
            pltpu.VMEM((8, rows // 4, PADDED), BF16),
            pltpu.SemaphoreType.DMA((4,)),
            pltpu.SemaphoreType.DMA((3,)),
            pltpu.SemaphoreType.DMA((8,)),
        ],
        smem=(0,),
        hbm=(2, 3),
        hbm_out=(2,),
        flops=8_000_000_000,
        vmem=56,
    )
    spatial = call(
        spatial_kernel,
        jax.ShapeDtypeStruct((videos, tokens, PADDED), BF16),
        (group, everyone, gram, sums, few_out, pq, pkv),
        scratch=[
            pltpu.VMEM((rows // own_rows, own_rows, 2 * PADDED), BF16),
            pltpu.VMEM((rows, 2 * latents.shape[-1] + 8), F32),
            pltpu.VMEM((rows, PADDED), BF16),
            pltpu.VMEM((rows, PADDED), BF16),
            pltpu.SemaphoreType.DMA((rows // own_rows,)),
        ],
        smem=(0,),
        hbm=(6,),
        flops=20_000_000_000,
        vmem=56,
    )
    heads_out = lax.all_to_all(
        spatial, "seq", split_axis=0, concat_axis=0, tiled=True, axis_index_groups=groups
    )
    late, _ = lax.optimization_barrier((w_spatial, spatial))
    w_s = call(
        projection_kernel,
        jax.ShapeDtypeStruct((PADDED, width), BF16),
        (row_pick, late),
        scratch=[pltpu.VMEM((width, PADDED), BF16), pltpu.SemaphoreType.DMA],
        hbm=(1,),
        flops=20_000_000_000,
        vmem=56,
    )
    block_out = call(
        finish_kernel,
        jax.ShapeDtypeStruct((videos, tokens, width), BF16),
        (seq_pos.reshape(1), heads_out, queued, w_embed, ua, va, cb, sb, new_mods, w_s),
        smem=(0,),
        flops=1_000_000_000,
    )
    return (
        queued.transpose(0, 2, 1).reshape(videos, 1, tokens, -1),
        block_out.reshape(videos, 1, tokens, width),
    )


def solution(mesh):
    in_specs = (
        P(None, "queue", "seq", None),
        P(None, "queue", "seq", None),
        P(None, "queue", "seq", None),
        P(None, "seq", None),
        P(),
        P(),
        P(),
        P("queue", None),
        P(),
        P(),
        P("queue", None),
        P("queue", None),
    )
    out_specs = (P(None, "queue", "seq", None), P(None, "queue", "seq", None))
    return jax.shard_map(shards, mesh=mesh, in_specs=in_specs, out_specs=out_specs, check_vma=False)
```

```python
import math

import jax
import jax.numpy as jnp
import numpy as np
from jax import lax
from jax.experimental import pallas as pl
from jax.experimental.pallas import tpu as pltpu
from jax.sharding import PartitionSpec as P

HEADS = 8
HDIM = 72
HALF = HDIM // 2
SLOT = 80
PADDED = HEADS * SLOT
SCORE_SCALE = 1.0 / math.sqrt(HDIM)
LOG2E = math.log2(math.e)
F32 = jnp.float32
BF16 = jnp.bfloat16
MIB = 1024 * 1024


def mm(a, b):
    return jnp.dot(a, b, preferred_element_type=F32)


def mm_nt(a, b):
    return lax.dot_general(a, b, (((1,), (1,)), ((), ())), preferred_element_type=F32)


def call(kernel, out_shape, args, scratch=(), smem=(), hbm=(), hbm_out=(), flops=0, vmem=24, grid=None, in_specs=None, out_specs=None):
    moved = sum(a.size * a.dtype.itemsize for a in args)
    if in_specs is None:
        in_specs = [
            pl.BlockSpec(memory_space=pltpu.SMEM if i in smem else pl.ANY if i in hbm else pltpu.VMEM)
            for i in range(len(args))
        ]
        if isinstance(out_shape, tuple):
            out_specs = tuple(
                pl.BlockSpec(memory_space=pl.ANY if i in hbm_out else pltpu.VMEM) for i in range(len(out_shape))
            )
        else:
            out_specs = pl.BlockSpec(memory_space=pltpu.VMEM)
    return pl.pallas_call(
        kernel,
        out_shape=out_shape,
        in_specs=in_specs,
        out_specs=out_specs,
        scratch_shapes=list(scratch),
        compiler_params=pltpu.CompilerParams(vmem_limit_bytes=vmem * MIB),
        cost_estimate=pl.CostEstimate(flops=flops, bytes_accessed=moved, transcendentals=0),
        **({"grid": grid} if grid else {}),
    )(*args)


def layer_norm(values):
    center = values - jnp.mean(values, axis=-1, keepdims=True)
    spread = jnp.mean(center * center, axis=-1, keepdims=True)
    return center * lax.rsqrt(spread + 1e-06)


def pack_kernel(
    core_ref, x_ref, tout_ref, sqkv_ref, sout_ref, o_ref, shard_ref,
    x, tout, sqkv, sout, packed, shard, x_sem, w_sem, o_sem,
):
    videos, tokens, columns = x.shape
    pairs = packed.shape[0] // videos
    width = columns // pairs

    def load(v):
        return pltpu.make_async_copy(x_ref.at[v], x.at[v], x_sem.at[v])

    weights = [
        pltpu.make_async_copy(source, target, w_sem.at[i])
        for i, (source, target) in enumerate(((tout_ref, tout), (sqkv_ref, sqkv), (sout_ref, sout)))
    ]

    def store(v):
        at = slice(pairs * v, pairs * (v + 1))
        return pltpu.make_async_copy(packed.at[at], o_ref.at[at], o_sem.at[v])

    weights[0].start()
    load(0).start()
    weights[1].start()
    weights[2].start()
    for v in range(1, videos):
        load(v).start()

    weights[0].wait()
    half = tout.shape[-1] // 2
    left, right = tout[:, :half].astype(F32), tout[:, half:].astype(F32)
    own = jnp.where(core_ref[0] == 0, left, right)
    weight = jnp.concatenate([own[:, : half // 2], own[:, half // 2 :]], axis=0).astype(BF16)
    load(0).wait()
    for part in range(pairs):
        packed[part, :, :width] = x[0, :, part * width : (part + 1) * width]
        packed[part, :, width:] = weight
    store(0).start()

    weights[1].wait()
    weights[2].wait()
    blank = jnp.zeros((tokens, SLOT - HDIM), BF16)
    for i, part in enumerate((1, 2, 0)):
        pieces = []
        for h in range(HEADS):
            at = HDIM * (3 * h + part)
            pieces += [sqkv[:, at : at + HDIM], blank]
        shard[:, PADDED * i : PADDED * (i + 1)] = jnp.concatenate(pieces, axis=-1)
    ends = jnp.concatenate([sout[:, :half].astype(F32), sout[:, half:].astype(F32)], axis=0)
    ends = jnp.concatenate([ends, jnp.zeros((tokens, PADDED - half), F32)], axis=-1)
    shard[:, 3 * PADDED :] = ends.astype(BF16)
    last = pltpu.make_async_copy(shard, shard_ref, w_sem.at[3])
    last.start()

    for v in range(1, videos):
        load(v).wait()
        for part in range(pairs):
            packed[pairs * v + part, :, :width] = x[v, :, part * width : (part + 1) * width]
            packed[pairs * v + part, :, width:] = weight
        store(v).start()
    last.wait()
    for v in range(videos):
        store(v).wait()


def temporal_columns():
    pick = np.zeros((6 * HDIM, 768), np.float32)
    for head in range(2):
        base = 3 * HDIM * head
        for i in range(HDIM):
            pick[base + i, 256 * head + i] = 1.0
            pick[base + HDIM + i, 256 * head + 128 + i] = 1.0
            pick[base + 2 * HDIM + i, 512 + SLOT * head + i] = 1.0
    return pick


def weight_rows():
    pick = np.zeros((2 * SLOT, 256), np.float32)
    for shard in range(2):
        for i in range(HALF):
            pick[HALF * shard + i, HDIM * shard + i] = 1.0
            pick[SLOT + HALF * shard + i, HDIM * shard + HALF + i] = 1.0
    return pick


def temporal_kernel(x_ref, pick_ref, o_ref, parts, total):
    frames, tokens, _ = x_ref.shape
    flat = x_ref[:, :, : 6 * HDIM].astype(F32).reshape(frames * tokens, 6 * HDIM).astype(BF16)
    parts[...] = mm(flat, pick_ref[...]).reshape(frames, tokens, -1)
    rows = frames * 8
    first = lax.broadcasted_iota(jnp.int32, (1, 2 * SLOT), 1) < SLOT
    same = (
        lax.broadcasted_iota(jnp.int32, (rows, rows), 0) % 8
        == lax.broadcasted_iota(jnp.int32, (rows, rows), 1) % 8
    )
    blocks = tokens // 8
    pieces = [parts[:, 8 * i : 8 * i + 8, :].reshape(rows, -1).astype(BF16) for i in range(blocks)]
    scores = [
        mm_nt(piece[:, 256 * head : 256 * head + 128], piece[:, 256 * head + 128 : 256 * head + 256])
        for piece in pieces
        for head in range(2)
    ]
    scores = jnp.concatenate(scores, axis=0).reshape(2 * blocks, rows, rows)
    scores = jnp.where(same[None], scores * SCORE_SCALE, -jnp.inf)
    raised = jnp.exp(scores - jnp.max(scores, axis=-1, keepdims=True))
    weights = (raised / jnp.sum(raised, axis=-1, keepdims=True)).astype(BF16)
    for i in range(blocks):
        v = pieces[i][:, 512 : 512 + 2 * SLOT]
        out = jnp.where(first, mm(weights[2 * i], v), mm(weights[2 * i + 1], v))
        total[:, 8 * i : 8 * i + 8, :] = out.reshape(frames, 8, 2 * SLOT)
    side = total[:, :, 128:]
    third = tokens // 3
    side = [side[:, third * i : third * (i + 1), :] for i in range(3)] + [jnp.zeros((frames, third, 32), F32)]
    o_ref[:, :tokens, :] = total[:, :, :128].astype(BF16)
    o_ref[:, tokens:, :] = jnp.concatenate(side, axis=-1).astype(BF16)


def unstack_kernel(x_ref, rows_ref, w_ref):
    shards, rows, width = x_ref.shape
    start = 6 * HDIM
    blank = jnp.zeros((SLOT, w_ref.shape[-1] - 2 * (width - start)), F32)
    for h in range(shards // 2):
        pair = x_ref[2 * h : 2 * h + 2, :, start:].astype(F32).reshape(2 * rows, -1).astype(BF16)
        both = mm(rows_ref[:, : 2 * rows], pair)
        w_ref[SLOT * h : SLOT * (h + 1), :] = jnp.concatenate(
            [both[:SLOT], both[SLOT:], blank], axis=-1
        ).astype(BF16)


def step_kernel(coef_ref, core_ref, att_ref, hid_ref, lat_ref, mine_ref, other_ref, wf_ref, mod_ref, o_ref):
    videos, tokens, width = hid_ref.shape
    rows = videos * tokens
    pairs = att_ref.shape[0] // videos
    att = att_ref[...].astype(F32)
    side = jnp.concatenate([att[:, tokens:, 32 * i : 32 * (i + 1)] for i in range(3)], axis=1)
    att = jnp.concatenate([att[:, :tokens, :], side], axis=-1).reshape(videos, pairs, tokens, 2 * SLOT)
    own = far = None
    for p in range(pairs):
        part = att[:, p].reshape(rows, 2 * SLOT).astype(BF16)
        at = slice(2 * SLOT * p, 2 * SLOT * (p + 1))
        own_term, far_term = mm(part, mine_ref[at, :]), mm(part, other_ref[at, :])
        own = own_term if own is None else own + own_term
        far = far_term if far is None else far + far_term
    low = core_ref[0] == 0
    half = width // 2
    proj = jnp.concatenate([jnp.where(low, own, far)[:, :half], jnp.where(low, far, own)[:, :half]], axis=-1)
    residual = hid_ref[...].astype(F32).reshape(rows, width) + mod_ref[0:1, :] * proj
    final_in = (layer_norm(residual) * (1.0 + mod_ref[2:3, :]) + mod_ref[1:2, :]).astype(BF16)
    predicted = mm_nt(wf_ref[...], final_in)
    for v in range(videos):
        pred = predicted[:, tokens * v : tokens * (v + 1)]
        clean = (lat_ref[v].astype(F32) - coef_ref[0] * pred) * coef_ref[1]
        o_ref[v] = (coef_ref[2] * clean + coef_ref[3] * pred).astype(BF16)


def centered_place(c, ua_ref, va_ref, cb_ref, sb_ref):
    place = ua_ref[pl.ds(c, 1), :] * cb_ref[...] + va_ref[pl.ds(c, 1), :] * sb_ref[...]
    return place - jnp.mean(place, axis=-1, keepdims=True)


def place_kernel(wemb_ref, ua_ref, va_ref, cb_ref, sb_ref, sums_ref):
    tokens, width = cb_ref.shape
    blank = jnp.zeros((tokens, 7), F32)

    def one(few, carry):
        for i in range(4):
            c = 4 * few + i
            center = centered_place(c, ua_ref, va_ref, cb_ref, sb_ref)
            high = center.astype(BF16)
            low = (center - high.astype(F32)).astype(BF16)
            cross = (mm_nt(high, wemb_ref[...]) + mm_nt(low, wemb_ref[...])) * (2.0 / width)
            square = jnp.mean(center * center, axis=-1, keepdims=True)
            sums_ref[c] = jnp.concatenate([cross, square, blank], axis=-1).T
        return carry

    lax.fori_loop(0, sums_ref.shape[0] // 4, one, 0)


def prepare_kernel(
    group_ref, few_ref, mod_ref, ua_ref, va_ref, cb_ref, sb_ref, w_ref, few_out, q_out, kv_out,
    p, w, made, w_sem, out_sem,
):
    rows = q_out.shape[0]
    tokens = cb_ref.shape[0]
    step = 2 * rows
    steps = made.shape[0] // step

    edges = (0, 512, 2 * PADDED, 3 * PADDED)

    def load_w(part):
        at = slice(edges[part], edges[part + 1])
        return pltpu.make_async_copy(w_ref.at[:, at], w.at[:, at], w_sem.at[part])

    def store(part, i):
        at = (slice(step * i, step * (i + 1)), slice(edges[part], edges[part + 1]))
        return pltpu.make_async_copy(made.at[at], kv_out.at[at], out_sem.at[steps * part + i])

    for part in range(3):
        load_w(part).start()
    gain = 1.0 + mod_ref[4:5, :]

    def place(i):
        for c in range(step // tokens * i, step // tokens * (i + 1), 2):
            two = [centered_place(c + j, ua_ref, va_ref, cb_ref, sb_ref) * gain for j in range(2)]
            p[tokens * c : tokens * (c + 2), :] = jnp.concatenate(two, axis=0).astype(BF16)

    place(0)
    for part in range(2):
        load_w(part).wait()
        for i in range(steps):
            here = slice(step * i, step * (i + 1))
            columns = slice(edges[part], edges[part + 1])
            made[here, columns] = mm(p[here, :], w[:, columns]).astype(BF16)
            if part == 0 and i + 1 < steps:
                place(i + 1)
            store(part, i).start()
    load_w(2).wait()
    start = pl.multiple_of(group_ref[0] * rows, rows)
    q_out[...] = mm(p[pl.ds(start, rows), :], w[:, 2 * PADDED :])
    few_out[...] = mm(few_ref[...], w[...])
    for part in range(2):
        for i in range(steps):
            store(part, i).wait()


def spatial_kernel(
    group_ref, lat_ref, gram_ref, sums_ref, few_ref, pq_ref, pkv_ref,
    o_ref, held, columns, keys, vals, sem,
):
    chunks, patch, tokens = lat_ref.shape
    members = o_ref.shape[0]
    block = members * tokens
    blocks = chunks // members

    def fetch(index):
        start = pl.multiple_of(index * block, block)
        return pltpu.make_async_copy(pkv_ref.at[pl.ds(start, block), :], held.at[index], sem.at[index])

    for i in range(blocks):
        fetch(i).start()

    gram = gram_ref[...]
    for c in range(chunks):
        once = lat_ref[c].astype(F32)
        twice = jnp.concatenate([once, once], axis=0)
        sums = sums_ref[c]
        mixed = mm(gram, twice.astype(BF16)) + sums[:patch]
        variance = jnp.sum(mixed * once, axis=0, keepdims=True) + sums[patch : patch + 1]
        scale = lax.rsqrt(jnp.maximum(variance, 0.0) + 1e-06)
        rows = jnp.concatenate([twice, jnp.broadcast_to(scale, (8, tokens))], axis=0)
        columns[tokens * c : tokens * (c + 1), :] = rows.T

    lane = lax.broadcasted_iota(jnp.int32, (1, 2 * PADDED), 1)
    ones = jnp.where((lane >= PADDED) & (lane % SLOT == HDIM), 1.0, 0.0)
    few = few_ref[...]
    mix = few[:patch] + few[patch : 2 * patch]
    offset = few[2 * patch : 2 * patch + 1] + few[2 * patch + 8 : 2 * patch + 9]
    high = mix.astype(BF16).astype(F32)
    mix = jnp.concatenate([high, mix - high], axis=0).astype(BF16)
    kv_mix, q_mix = mix[:, : 2 * PADDED], mix[:, 2 * PADDED :]
    kv_offset, q_offset = offset[:, : 2 * PADDED] + ones, offset[:, 2 * PADDED :]

    def one(index, carry):
        start = pl.multiple_of(index * block, block)
        column = columns[pl.ds(start, block), :]
        latent, scale = column[:, : 2 * patch].astype(BF16), column[:, 2 * patch : 2 * patch + 1]
        mixed = mm(latent, kv_mix)
        fetch(index).wait()
        kv = (mixed + held[index].astype(F32)) * scale + kv_offset
        keys[pl.ds(start, block), :] = kv[:, :PADDED].astype(BF16)
        vals[pl.ds(start, block), :] = kv[:, PADDED:].astype(BF16)
        return carry

    lax.fori_loop(0, blocks, one, 0)

    column = columns[pl.ds(pl.multiple_of(group_ref[0] * block, block), block), :]
    latent, scale = column[:, : 2 * patch].astype(BF16), column[:, 2 * patch : 2 * patch + 1]
    q_all = (mm(latent, q_mix) + pq_ref[...]) * scale + q_offset
    q_all = q_all.astype(BF16).astype(F32)
    lane = lane[:, :PADDED]
    merged = [None] * (PADDED // 128)

    def window(h):
        first = SLOT * h // 128
        last = (SLOT * h + HDIM) // 128
        here = slice(128 * first, 128 * (last + 1))
        inside = (lane >= SLOT * h) & (lane < SLOT * h + HDIM)
        return first, last, here, inside[:, here]

    def score(h):
        _, _, here, inside = window(h)
        return mm_nt(jnp.where(inside, q_all[:, here], 0.0).astype(BF16), keys[:, here])

    def weigh(scores):
        top = jnp.max(scores, axis=-1, keepdims=True)
        return jnp.exp2((scores - top) * (SCORE_SCALE * LOG2E)).astype(BF16)

    def blend(h, raised):
        first, last, here, inside = window(h)
        found = mm(raised, vals[:, here])
        at = SLOT * h + HDIM - 128 * first
        found = jnp.where(inside, found * (1.0 / found[:, at : at + 1]), 0.0)
        for tile in range(first, last + 1):
            piece = found[:, 128 * (tile - first) : 128 * (tile - first + 1)]
            merged[tile] = piece if merged[tile] is None else merged[tile] + piece

    scores = score(0)
    raised = None
    for h in range(HEADS):
        following = score(h + 1) if h + 1 < HEADS else None
        if raised is not None:
            blend(h - 1, raised)
        raised = weigh(scores)
        scores = following
    blend(HEADS - 1, raised)
    o_ref[...] = jnp.concatenate(merged, axis=-1).reshape(members, tokens, PADDED).astype(BF16)


def projection_kernel(rows_ref, w_ref, w_out, raw, sem):
    copy = pltpu.make_async_copy(w_ref.at[:, 3 * PADDED :], raw, sem)
    copy.start()
    copy.wait()
    half = w_out.shape[-1] // 2
    for h in range(HEADS):
        both = mm(rows_ref[:, : 2 * HDIM], raw[2 * HDIM * h : 2 * HDIM * (h + 1), :])
        w_out[SLOT * h : SLOT * (h + 1), :] = jnp.concatenate(
            [both[:SLOT, :half], both[SLOT:, :half]], axis=-1
        ).astype(BF16)


def finish_kernel(
    seq_ref, att_ref, lat_ref, wemb_ref, ua_ref, va_ref, cb_ref, sb_ref, mod_ref, w_ref, o_ref
):
    videos, tokens, width = o_ref.shape
    s = seq_ref[0]
    place = ua_ref[pl.ds(s, 1), :] * cb_ref[...] + va_ref[pl.ds(s, 1), :] * sb_ref[...]
    gate = mod_ref[5:6, :]
    att = att_ref[...].astype(F32).reshape(videos * tokens, PADDED).astype(BF16)
    embedded = [mm(lat_ref[v].astype(F32).T.astype(BF16), wemb_ref[...]) + place for v in range(videos)]
    gated = mm(att, w_ref[...]) * gate
    for v in range(videos):
        o_ref[v] = (embedded[v] + gated[tokens * v : tokens * (v + 1), :]).astype(BF16)


def position_factors(chunks, tokens, width):
    half = width // 2
    frequency = jnp.exp(jnp.arange(half, dtype=F32) * (-math.log(10000.0) / half))
    start = (jnp.arange(chunks, dtype=F32) * tokens)[:, None] * frequency[None, :]
    inner = jnp.arange(tokens, dtype=F32)[:, None] * frequency[None, :]
    sin_a, cos_a, sin_b, cos_b = jnp.sin(start), jnp.cos(start), jnp.sin(inner), jnp.cos(inner)
    ua = jnp.concatenate([sin_a, cos_a], axis=-1)
    va = jnp.concatenate([cos_a, -sin_a], axis=-1)
    cb = jnp.concatenate([cos_b, cos_b], axis=-1)
    sb = jnp.concatenate([sin_b, sin_b], axis=-1)
    return ua, va, cb, sb


def rounding_rest(values):
    return values - lax.reduce_precision(values, 8, 7)


def shards(
    t_qkv, hidden, latents, fresh, levels, alpha_bar, modulation, w_tout, w_final, w_embed, w_sqkv, w_sout,
):
    frames = lax.axis_size("queue")
    seqs = lax.axis_size("seq")
    queue_pos = lax.axis_index("queue")
    seq_pos = lax.axis_index("seq")
    videos, _, tokens, width = hidden.shape
    top_level = alpha_bar.shape[0] - 1
    pairs = frames // videos

    core = seq_pos % 2
    half = width // 2
    width_part = t_qkv.shape[-1] // pairs
    sent = width_part + half // 2
    packed, w_shard = call(
        pack_kernel,
        (
            jax.ShapeDtypeStruct((frames, tokens, sent), BF16),
            jax.ShapeDtypeStruct((w_sqkv.shape[0], 4 * PADDED), BF16),
        ),
        (core.reshape(1), t_qkv.reshape(videos, tokens, -1), w_tout, w_sqkv, w_sout),
        scratch=[
            pltpu.VMEM((videos, tokens, t_qkv.shape[-1]), BF16),
            pltpu.VMEM(w_tout.shape, BF16),
            pltpu.VMEM(w_sqkv.shape, BF16),
            pltpu.VMEM(w_sout.shape, BF16),
            pltpu.VMEM((frames, tokens, sent), BF16),
            pltpu.VMEM((w_sqkv.shape[0], 4 * PADDED), BF16),
            pltpu.SemaphoreType.DMA((videos,)),
            pltpu.SemaphoreType.DMA((4,)),
            pltpu.SemaphoreType.DMA((videos,)),
        ],
        smem=(0,),
        hbm=(1, 2, 3, 4),
        hbm_out=(0, 1),
        vmem=56,
    )
    w_spatial = lax.all_gather(w_shard, "queue", axis=0, tiled=True)

    arrived = lax.all_to_all(packed, "queue", split_axis=0, concat_axis=0, tiled=True)
    row_pick = jnp.asarray(weight_rows(), BF16)

    level = lax.dynamic_index_in_dim(levels, queue_pos, 0, keepdims=False)
    following = lax.dynamic_index_in_dim(
        jnp.concatenate([levels[1:], jnp.full((1,), top_level + 1, levels.dtype)]), queue_pos, 0, keepdims=False
    )
    mods = lax.dynamic_index_in_dim(modulation, level, 0, keepdims=False).astype(F32)
    new_mods = lax.dynamic_index_in_dim(modulation, following - 1, 0, keepdims=False).astype(F32)
    a = lax.dynamic_index_in_dim(alpha_bar, level, 0, keepdims=False)
    b = lax.dynamic_index_in_dim(alpha_bar, level - 1, 0, keepdims=False)
    coef = jnp.stack([jnp.sqrt(1.0 - a), 1.0 / jnp.sqrt(a), jnp.sqrt(b), jnp.sqrt(1.0 - b)])

    ua, va, cb, sb = position_factors(seqs, tokens, width)
    rows = seqs * tokens
    own_rows = videos * tokens
    sums = call(
        place_kernel,
        jax.ShapeDtypeStruct((seqs, 24, tokens), F32),
        (w_embed, ua, va, cb, sb),
        flops=100_000_000,
        vmem=56,
    )
    gain, shift = 1.0 + new_mods[4:5], new_mods[3:4]
    emb_f32 = w_embed.astype(F32)
    centered = emb_f32 - jnp.mean(emb_f32, axis=-1, keepdims=True)
    gram = jnp.dot(centered, centered.T, precision=lax.Precision.HIGHEST) * (1.0 / width)
    gram = jnp.concatenate([gram, rounding_rest(gram)], axis=-1).astype(BF16)
    centered = centered * gain
    eight = jnp.zeros((7, width), F32)
    few = [centered, rounding_rest(centered), shift, eight, rounding_rest(shift), eight]
    few = jnp.concatenate(few, axis=0).astype(BF16)
    latents_t = latents.reshape(videos, tokens, -1).transpose(0, 2, 1)
    fresh_t = fresh.transpose(0, 2, 1)
    w_final_t = w_final.T
    early = (arrived, sums, few, gram, mods, new_mods, coef, latents_t, fresh_t, w_final_t)
    early = lax.optimization_barrier(early)
    arrived, sums, few, gram, mods, new_mods, coef, latents_t, fresh_t, w_final_t = early

    attended = call(
        temporal_kernel,
        jax.ShapeDtypeStruct((frames, tokens + tokens // 3, 128), BF16),
        (arrived, jnp.asarray(temporal_columns(), BF16)),
        scratch=[pltpu.VMEM((frames, tokens, 768), F32), pltpu.VMEM((frames, tokens, 2 * SLOT), F32)],
        flops=4_000_000_000,
    )
    stacked, attended = lax.optimization_barrier((arrived, attended))
    w_mine = call(
        unstack_kernel,
        jax.ShapeDtypeStruct((PADDED, PADDED), BF16),
        (stacked, row_pick),
        flops=20_000_000_000,
    )
    w_other = lax.ppermute(w_mine, "seq", [(i, i ^ 1) for i in range(seqs)])
    returned = lax.all_to_all(attended, "queue", split_axis=0, concat_axis=0, tiled=True)

    stepped = call(
        step_kernel,
        jax.ShapeDtypeStruct((videos, latents.shape[-1], tokens), BF16),
        (
            coef,
            core.reshape(1),
            returned,
            hidden.reshape(videos, tokens, width),
            latents_t,
            w_mine,
            w_other,
            w_final_t,
            mods,
        ),
        smem=(0, 1),
        flops=1_000_000_000,
    )
    arriving = lax.ppermute(stepped, "queue", [(f, f - 1) for f in range(1, frames)])
    queued = jnp.where(queue_pos == frames - 1, fresh_t, arriving)

    everyone = lax.all_to_all(
        jnp.tile(queued, (seqs // videos, 1, 1)), "seq", split_axis=0, concat_axis=0, tiled=True
    )
    groups = [[videos * g + i for i in range(videos)] for g in range(seqs // videos)]
    group = (seq_pos // videos).reshape(1)
    few_out, pq, pkv = call(
        prepare_kernel,
        (
            jax.ShapeDtypeStruct((few.shape[0], 3 * PADDED), F32),
            jax.ShapeDtypeStruct((own_rows, PADDED), F32),
            jax.ShapeDtypeStruct((rows, 2 * PADDED), BF16),
        ),
        (group, few, new_mods, ua, va, cb, sb, w_spatial),
        scratch=[
            pltpu.VMEM((rows, width), BF16),
            pltpu.VMEM((width, 3 * PADDED), BF16),
            pltpu.VMEM((rows, 2 * PADDED), BF16),
            pltpu.SemaphoreType.DMA((3,)),
            pltpu.SemaphoreType.DMA((8,)),
        ],
        smem=(0,),
        hbm=(7,),
        hbm_out=(2,),
        flops=8_000_000_000,
        vmem=56,
    )
    spatial = call(
        spatial_kernel,
        jax.ShapeDtypeStruct((videos, tokens, PADDED), BF16),
        (group, everyone, gram, sums, few_out, pq, pkv),
        scratch=[
            pltpu.VMEM((rows // own_rows, own_rows, 2 * PADDED), BF16),
            pltpu.VMEM((rows, 2 * latents.shape[-1] + 8), F32),
            pltpu.VMEM((rows, PADDED), BF16),
            pltpu.VMEM((rows, PADDED), BF16),
            pltpu.SemaphoreType.DMA((rows // own_rows,)),
        ],
        smem=(0,),
        hbm=(6,),
        flops=20_000_000_000,
        vmem=56,
    )
    heads_out = lax.all_to_all(
        spatial, "seq", split_axis=0, concat_axis=0, tiled=True, axis_index_groups=groups
    )
    late, _ = lax.optimization_barrier((w_spatial, spatial))
    w_s = call(
        projection_kernel,
        jax.ShapeDtypeStruct((PADDED, width), BF16),
        (row_pick, late),
        scratch=[pltpu.VMEM((width, PADDED), BF16), pltpu.SemaphoreType.DMA],
        hbm=(1,),
        flops=20_000_000_000,
        vmem=56,
    )
    block_out = call(
        finish_kernel,
        jax.ShapeDtypeStruct((videos, tokens, width), BF16),
        (seq_pos.reshape(1), heads_out, queued, w_embed, ua, va, cb, sb, new_mods, w_s),
        smem=(0,),
        flops=1_000_000_000,
    )
    return (
        queued.transpose(0, 2, 1).reshape(videos, 1, tokens, -1),
        block_out.reshape(videos, 1, tokens, width),
    )


def solution(mesh):
    in_specs = (
        P(None, "queue", "seq", None),
        P(None, "queue", "seq", None),
        P(None, "queue", "seq", None),
        P(None, "seq", None),
        P(),
        P(),
        P(),
        P("queue", None),
        P(),
        P(),
        P("queue", None),
        P("queue", None),
    )
    out_specs = (P(None, "queue", "seq", None), P(None, "queue", "seq", None))
    return jax.shard_map(shards, mesh=mesh, in_specs=in_specs, out_specs=out_specs, check_vma=False)
```

```python
import math

import jax
import jax.numpy as jnp
import numpy as np
from jax import lax
from jax.experimental import pallas as pl
from jax.experimental.pallas import tpu as pltpu
from jax.sharding import PartitionSpec as P

HEADS = 8
HDIM = 72
HALF = HDIM // 2
SLOT = 80
PADDED = HEADS * SLOT
SCORE_SCALE = 1.0 / math.sqrt(HDIM)
LOG2E = math.log2(math.e)
F32 = jnp.float32
BF16 = jnp.bfloat16
MIB = 1024 * 1024


def mm(a, b):
    return jnp.dot(a, b, preferred_element_type=F32)


def mm_nt(a, b):
    return lax.dot_general(a, b, (((1,), (1,)), ((), ())), preferred_element_type=F32)


def call(kernel, out_shape, args, scratch=(), smem=(), hbm=(), hbm_out=(), flops=0, vmem=24, grid=None, in_specs=None, out_specs=None):
    moved = sum(a.size * a.dtype.itemsize for a in args)
    if in_specs is None:
        in_specs = [
            pl.BlockSpec(memory_space=pltpu.SMEM if i in smem else pl.ANY if i in hbm else pltpu.VMEM)
            for i in range(len(args))
        ]
        if isinstance(out_shape, tuple):
            out_specs = tuple(
                pl.BlockSpec(memory_space=pl.ANY if i in hbm_out else pltpu.VMEM) for i in range(len(out_shape))
            )
        else:
            out_specs = pl.BlockSpec(memory_space=pltpu.VMEM)
    return pl.pallas_call(
        kernel,
        out_shape=out_shape,
        in_specs=in_specs,
        out_specs=out_specs,
        scratch_shapes=list(scratch),
        compiler_params=pltpu.CompilerParams(vmem_limit_bytes=vmem * MIB),
        cost_estimate=pl.CostEstimate(flops=flops, bytes_accessed=moved, transcendentals=0),
        **({"grid": grid} if grid else {}),
    )(*args)


def layer_norm(values):
    center = values - jnp.mean(values, axis=-1, keepdims=True)
    spread = jnp.mean(center * center, axis=-1, keepdims=True)
    return center * lax.rsqrt(spread + 1e-06)


def pack_kernel(
    core_ref, x_ref, tout_ref, sqkv_ref, sout_ref, o_ref, shard_ref,
    x, tout, sqkv, sout, packed, shard, x_sem, w_sem, o_sem,
):
    videos, tokens, columns = x.shape
    pairs = packed.shape[0] // videos
    width = columns // pairs

    def load(v):
        return pltpu.make_async_copy(x_ref.at[v], x.at[v], x_sem.at[v])

    weights = [
        pltpu.make_async_copy(source, target, w_sem.at[i])
        for i, (source, target) in enumerate(((tout_ref, tout), (sqkv_ref, sqkv), (sout_ref, sout)))
    ]

    def store(v):
        at = slice(pairs * v, pairs * (v + 1))
        return pltpu.make_async_copy(packed.at[at], o_ref.at[at], o_sem.at[v])

    weights[0].start()
    load(0).start()
    weights[1].start()
    weights[2].start()
    for v in range(1, videos):
        load(v).start()

    weights[0].wait()
    half = tout.shape[-1] // 2
    left, right = tout[:, :half].astype(F32), tout[:, half:].astype(F32)
    own = jnp.where(core_ref[0] == 0, left, right)
    weight = jnp.concatenate([own[:, : half // 2], own[:, half // 2 :]], axis=0).astype(BF16)
    load(0).wait()
    for part in range(pairs):
        packed[part, :, :width] = x[0, :, part * width : (part + 1) * width]
        packed[part, :, width:] = weight
    store(0).start()

    weights[1].wait()
    weights[2].wait()
    blank = jnp.zeros((tokens, SLOT - HDIM), BF16)
    for i, part in enumerate((1, 2, 0)):
        pieces = []
        for h in range(HEADS):
            at = HDIM * (3 * h + part)
            pieces += [sqkv[:, at : at + HDIM], blank]
        shard[:, PADDED * i : PADDED * (i + 1)] = jnp.concatenate(pieces, axis=-1)
    ends = jnp.concatenate([sout[:, :half].astype(F32), sout[:, half:].astype(F32)], axis=0)
    ends = jnp.concatenate([ends, jnp.zeros((tokens, PADDED - half), F32)], axis=-1)
    shard[:, 3 * PADDED :] = ends.astype(BF16)
    last = pltpu.make_async_copy(shard, shard_ref, w_sem.at[3])
    last.start()

    for v in range(1, videos):
        load(v).wait()
        for part in range(pairs):
            packed[pairs * v + part, :, :width] = x[v, :, part * width : (part + 1) * width]
            packed[pairs * v + part, :, width:] = weight
        store(v).start()
    last.wait()
    for v in range(videos):
        store(v).wait()


def temporal_columns():
    pick = np.zeros((6 * HDIM, 768), np.float32)
    for head in range(2):
        base = 3 * HDIM * head
        for i in range(HDIM):
            pick[base + i, 256 * head + i] = 1.0
            pick[base + HDIM + i, 256 * head + 128 + i] = 1.0
            pick[base + 2 * HDIM + i, 512 + SLOT * head + i] = 1.0
    return pick


def weight_rows():
    pick = np.zeros((2 * SLOT, 256), np.float32)
    for shard in range(2):
        for i in range(HALF):
            pick[HALF * shard + i, HDIM * shard + i] = 1.0
            pick[SLOT + HALF * shard + i, HDIM * shard + HALF + i] = 1.0
    return pick


def temporal_kernel(x_ref, pick_ref, o_ref, parts, total):
    frames, tokens, _ = x_ref.shape
    flat = x_ref[:, :, : 6 * HDIM].astype(F32).reshape(frames * tokens, 6 * HDIM).astype(BF16)
    parts[...] = mm(flat, pick_ref[...]).reshape(frames, tokens, -1)
    rows = frames * 8
    first = lax.broadcasted_iota(jnp.int32, (1, 2 * SLOT), 1) < SLOT
    same = (
        lax.broadcasted_iota(jnp.int32, (rows, rows), 0) % 8
        == lax.broadcasted_iota(jnp.int32, (rows, rows), 1) % 8
    )
    blocks = tokens // 8
    pieces = [parts[:, 8 * i : 8 * i + 8, :].reshape(rows, -1).astype(BF16) for i in range(blocks)]
    scores = [
        mm_nt(piece[:, 256 * head : 256 * head + 128], piece[:, 256 * head + 128 : 256 * head + 256])
        for piece in pieces
        for head in range(2)
    ]
    scores = jnp.concatenate(scores, axis=0).reshape(2 * blocks, rows, rows)
    scores = jnp.where(same[None], scores * SCORE_SCALE, -jnp.inf)
    raised = jnp.exp(scores - jnp.max(scores, axis=-1, keepdims=True))
    weights = (raised / jnp.sum(raised, axis=-1, keepdims=True)).astype(BF16)
    for i in range(blocks):
        v = pieces[i][:, 512 : 512 + 2 * SLOT]
        out = jnp.where(first, mm(weights[2 * i], v), mm(weights[2 * i + 1], v))
        total[:, 8 * i : 8 * i + 8, :] = out.reshape(frames, 8, 2 * SLOT)
    side = total[:, :, 128:]
    third = tokens // 3
    side = [side[:, third * i : third * (i + 1), :] for i in range(3)] + [jnp.zeros((frames, third, 32), F32)]
    o_ref[:, :tokens, :] = total[:, :, :128].astype(BF16)
    o_ref[:, tokens:, :] = jnp.concatenate(side, axis=-1).astype(BF16)


def unstack_kernel(x_ref, rows_ref, w_ref):
    shards, rows, width = x_ref.shape
    start = 6 * HDIM
    blank = jnp.zeros((SLOT, w_ref.shape[-1] - 2 * (width - start)), F32)
    for h in range(shards // 2):
        pair = x_ref[2 * h : 2 * h + 2, :, start:].astype(F32).reshape(2 * rows, -1).astype(BF16)
        both = mm(rows_ref[:, : 2 * rows], pair)
        w_ref[SLOT * h : SLOT * (h + 1), :] = jnp.concatenate(
            [both[:SLOT], both[SLOT:], blank], axis=-1
        ).astype(BF16)


def step_kernel(coef_ref, core_ref, att_ref, hid_ref, lat_ref, mine_ref, other_ref, wf_ref, mod_ref, o_ref):
    videos, tokens, width = hid_ref.shape
    rows = videos * tokens
    pairs = att_ref.shape[0] // videos
    att = att_ref[...].astype(F32)
    side = jnp.concatenate([att[:, tokens:, 32 * i : 32 * (i + 1)] for i in range(3)], axis=1)
    att = jnp.concatenate([att[:, :tokens, :], side], axis=-1).reshape(videos, pairs, tokens, 2 * SLOT)
    own = far = None
    for p in range(pairs):
        part = att[:, p].reshape(rows, 2 * SLOT).astype(BF16)
        at = slice(2 * SLOT * p, 2 * SLOT * (p + 1))
        own_term, far_term = mm(part, mine_ref[at, :]), mm(part, other_ref[at, :])
        own = own_term if own is None else own + own_term
        far = far_term if far is None else far + far_term
    low = core_ref[0] == 0
    half = width // 2
    proj = jnp.concatenate([jnp.where(low, own, far)[:, :half], jnp.where(low, far, own)[:, :half]], axis=-1)
    residual = hid_ref[...].astype(F32).reshape(rows, width) + mod_ref[0:1, :] * proj
    final_in = (layer_norm(residual) * (1.0 + mod_ref[2:3, :]) + mod_ref[1:2, :]).astype(BF16)
    predicted = mm_nt(wf_ref[...], final_in)
    for v in range(videos):
        pred = predicted[:, tokens * v : tokens * (v + 1)]
        clean = (lat_ref[v].astype(F32) - coef_ref[0] * pred) * coef_ref[1]
        o_ref[v] = (coef_ref[2] * clean + coef_ref[3] * pred).astype(BF16)


def centered_place(c, ua_ref, va_ref, cb_ref, sb_ref):
    place = ua_ref[pl.ds(c, 1), :] * cb_ref[...] + va_ref[pl.ds(c, 1), :] * sb_ref[...]
    return place - jnp.mean(place, axis=-1, keepdims=True)


def place_kernel(wemb_ref, ua_ref, va_ref, cb_ref, sb_ref, sums_ref):
    tokens, width = cb_ref.shape
    blank = jnp.zeros((tokens, 7), F32)

    def one(few, carry):
        for i in range(4):
            c = 4 * few + i
            center = centered_place(c, ua_ref, va_ref, cb_ref, sb_ref)
            high = center.astype(BF16)
            low = (center - high.astype(F32)).astype(BF16)
            cross = (mm_nt(high, wemb_ref[...]) + mm_nt(low, wemb_ref[...])) * (2.0 / width)
            square = jnp.mean(center * center, axis=-1, keepdims=True)
            sums_ref[c] = jnp.concatenate([cross, square, blank], axis=-1).T
        return carry

    lax.fori_loop(0, sums_ref.shape[0] // 4, one, 0)


def prepare_kernel(
    group_ref, few_ref, mod_ref, ua_ref, va_ref, cb_ref, sb_ref, w_ref, mix_out, offset_out, q_out, kv_out,
    p, w, made, w_sem, out_sem,
):
    rows = q_out.shape[0]
    tokens = cb_ref.shape[0]
    step = 2 * rows
    steps = made.shape[0] // step

    edges = (0, 512, 2 * PADDED, 3 * PADDED)

    def load_w(part):
        at = slice(edges[part], edges[part + 1])
        return pltpu.make_async_copy(w_ref.at[:, at], w.at[:, at], w_sem.at[part])

    def store(i):
        at = slice(step * i, step * (i + 1))
        return pltpu.make_async_copy(made.at[at], kv_out.at[at], out_sem.at[i])

    for part in range(3):
        load_w(part).start()
    gain = 1.0 + mod_ref[4:5, :]

    def place(i):
        for c in range(step // tokens * i, step // tokens * (i + 1), 2):
            two = [centered_place(c + j, ua_ref, va_ref, cb_ref, sb_ref) * gain for j in range(2)]
            p[tokens * c : tokens * (c + 2), :] = jnp.concatenate(two, axis=0).astype(BF16)

    place(0)
    for i in range(steps):
        here = slice(step * i, step * (i + 1))
        for part in range(2):
            if i == 0:
                load_w(part).wait()
            columns = slice(edges[part], edges[part + 1])
            made[here, columns] = mm(p[here, :], w[:, columns]).astype(BF16)
            if part == 0 and i + 1 < steps:
                place(i + 1)
        store(i).start()
    load_w(2).wait()
    start = pl.multiple_of(group_ref[0] * rows, rows)
    q_out[...] = mm(p[pl.ds(start, rows), :], w[:, 2 * PADDED :]).astype(BF16)
    few = mm(few_ref[...], w[...])
    patch = mix_out.shape[0] // 2
    mix = few[:patch] + few[patch : 2 * patch]
    high = mix.astype(BF16).astype(F32)
    mix_out[...] = jnp.concatenate([high, mix - high], axis=0).astype(BF16)
    offset_out[...] = few[2 * patch : 2 * patch + 8] + few[2 * patch + 8 :]
    for i in range(steps):
        store(i).wait()


def spatial_kernel(
    group_ref, lat_ref, gram_ref, sums_ref, mix_ref, offset_ref, pq_ref, pkv_ref,
    o_ref, held, columns, keys, vals, sem,
):
    chunks, patch, tokens = lat_ref.shape
    members = o_ref.shape[0]
    block = members * tokens
    blocks = chunks // members

    def fetch(index):
        start = pl.multiple_of(index * block, block)
        return pltpu.make_async_copy(pkv_ref.at[pl.ds(start, block), :], held.at[index], sem.at[index])

    for i in range(blocks):
        fetch(i).start()

    gram = gram_ref[...]
    for c in range(chunks):
        once = lat_ref[c].astype(F32)
        twice = jnp.concatenate([once, once], axis=0)
        sums = sums_ref[c]
        mixed = mm(gram, twice.astype(BF16)) + sums[:patch]
        variance = jnp.sum(mixed * once, axis=0, keepdims=True) + sums[patch : patch + 1]
        scale = lax.rsqrt(jnp.maximum(variance, 0.0) + 1e-06)
        rows = jnp.concatenate([twice, jnp.broadcast_to(scale, (8, tokens))], axis=0)
        columns[tokens * c : tokens * (c + 1), :] = rows.T

    lane = lax.broadcasted_iota(jnp.int32, (1, PADDED), 1)
    ones = jnp.where(lane % SLOT == HDIM, 1.0, 0.0)

    kv_mix = mix_ref[:, : 2 * PADDED]
    kv_offset = offset_ref[0:1, : 2 * PADDED] + jnp.concatenate([jnp.zeros_like(ones), ones], axis=-1)

    def one(index, carry):
        start = pl.multiple_of(index * block, block)
        column = columns[pl.ds(start, block), :]
        latent, scale = column[:, : 2 * patch].astype(BF16), column[:, 2 * patch : 2 * patch + 1]
        mixed = mm(latent, kv_mix)
        fetch(index).wait()
        kv = (mixed + held[index].astype(F32)) * scale + kv_offset
        keys[pl.ds(start, block), :] = kv[:, :PADDED].astype(BF16)
        vals[pl.ds(start, block), :] = kv[:, PADDED:].astype(BF16)
        return carry

    lax.fori_loop(0, blocks, one, 0)

    column = columns[pl.ds(pl.multiple_of(group_ref[0] * block, block), block), :]
    latent, scale = column[:, : 2 * patch].astype(BF16), column[:, 2 * patch : 2 * patch + 1]
    q_all = (mm(latent, mix_ref[:, 2 * PADDED :]) + pq_ref[...].astype(F32)) * scale + offset_ref[0:1, 2 * PADDED :]
    q_all = q_all.astype(BF16).astype(F32)
    merged = [None] * (PADDED // 128)

    def window(h):
        first = SLOT * h // 128
        last = (SLOT * h + HDIM) // 128
        here = slice(128 * first, 128 * (last + 1))
        inside = (lane >= SLOT * h) & (lane < SLOT * h + HDIM)
        return first, last, here, inside[:, here]

    def score(h):
        _, _, here, inside = window(h)
        return mm_nt(jnp.where(inside, q_all[:, here], 0.0).astype(BF16), keys[:, here])

    def weigh(scores):
        top = jnp.max(scores, axis=-1, keepdims=True)
        return jnp.exp2((scores - top) * (SCORE_SCALE * LOG2E)).astype(BF16)

    def blend(h, raised):
        first, last, here, inside = window(h)
        found = mm(raised, vals[:, here])
        at = SLOT * h + HDIM - 128 * first
        found = jnp.where(inside, found * (1.0 / found[:, at : at + 1]), 0.0)
        for tile in range(first, last + 1):
            piece = found[:, 128 * (tile - first) : 128 * (tile - first + 1)]
            merged[tile] = piece if merged[tile] is None else merged[tile] + piece

    scores = score(0)
    raised = None
    for h in range(HEADS):
        following = score(h + 1) if h + 1 < HEADS else None
        if raised is not None:
            blend(h - 1, raised)
        raised = weigh(scores)
        scores = following
    blend(HEADS - 1, raised)
    o_ref[...] = jnp.concatenate(merged, axis=-1).reshape(members, tokens, PADDED).astype(BF16)


def projection_kernel(rows_ref, w_ref, w_out, raw, sem):
    copy = pltpu.make_async_copy(w_ref.at[:, 3 * PADDED :], raw, sem)
    copy.start()
    copy.wait()
    half = w_out.shape[-1] // 2
    for h in range(HEADS):
        both = mm(rows_ref[:, : 2 * HDIM], raw[2 * HDIM * h : 2 * HDIM * (h + 1), :])
        w_out[SLOT * h : SLOT * (h + 1), :] = jnp.concatenate(
            [both[:SLOT, :half], both[SLOT:, :half]], axis=-1
        ).astype(BF16)


def finish_kernel(
    seq_ref, att_ref, lat_ref, wemb_ref, ua_ref, va_ref, cb_ref, sb_ref, mod_ref, w_ref, o_ref
):
    videos, tokens, width = o_ref.shape
    s = seq_ref[0]
    place = ua_ref[pl.ds(s, 1), :] * cb_ref[...] + va_ref[pl.ds(s, 1), :] * sb_ref[...]
    gate = mod_ref[5:6, :]
    att = att_ref[...].astype(F32).reshape(videos * tokens, PADDED).astype(BF16)
    embedded = [mm(lat_ref[v].astype(F32).T.astype(BF16), wemb_ref[...]) + place for v in range(videos)]
    gated = mm(att, w_ref[...]) * gate
    for v in range(videos):
        o_ref[v] = (embedded[v] + gated[tokens * v : tokens * (v + 1), :]).astype(BF16)


def position_factors(chunks, tokens, width):
    half = width // 2
    frequency = jnp.exp(jnp.arange(half, dtype=F32) * (-math.log(10000.0) / half))
    start = (jnp.arange(chunks, dtype=F32) * tokens)[:, None] * frequency[None, :]
    inner = jnp.arange(tokens, dtype=F32)[:, None] * frequency[None, :]
    sin_a, cos_a, sin_b, cos_b = jnp.sin(start), jnp.cos(start), jnp.sin(inner), jnp.cos(inner)
    ua = jnp.concatenate([sin_a, cos_a], axis=-1)
    va = jnp.concatenate([cos_a, -sin_a], axis=-1)
    cb = jnp.concatenate([cos_b, cos_b], axis=-1)
    sb = jnp.concatenate([sin_b, sin_b], axis=-1)
    return ua, va, cb, sb


def rounding_rest(values):
    return values - lax.reduce_precision(values, 8, 7)


def shards(
    t_qkv, hidden, latents, fresh, levels, alpha_bar, modulation, w_tout, w_final, w_embed, w_sqkv, w_sout,
):
    frames = lax.axis_size("queue")
    seqs = lax.axis_size("seq")
    queue_pos = lax.axis_index("queue")
    seq_pos = lax.axis_index("seq")
    videos, _, tokens, width = hidden.shape
    top_level = alpha_bar.shape[0] - 1
    pairs = frames // videos

    core = seq_pos % 2
    half = width // 2
    width_part = t_qkv.shape[-1] // pairs
    sent = width_part + half // 2
    packed, w_shard = call(
        pack_kernel,
        (
            jax.ShapeDtypeStruct((frames, tokens, sent), BF16),
            jax.ShapeDtypeStruct((w_sqkv.shape[0], 4 * PADDED), BF16),
        ),
        (core.reshape(1), t_qkv.reshape(videos, tokens, -1), w_tout, w_sqkv, w_sout),
        scratch=[
            pltpu.VMEM((videos, tokens, t_qkv.shape[-1]), BF16),
            pltpu.VMEM(w_tout.shape, BF16),
            pltpu.VMEM(w_sqkv.shape, BF16),
            pltpu.VMEM(w_sout.shape, BF16),
            pltpu.VMEM((frames, tokens, sent), BF16),
            pltpu.VMEM((w_sqkv.shape[0], 4 * PADDED), BF16),
            pltpu.SemaphoreType.DMA((videos,)),
            pltpu.SemaphoreType.DMA((4,)),
            pltpu.SemaphoreType.DMA((videos,)),
        ],
        smem=(0,),
        hbm=(1, 2, 3, 4),
        hbm_out=(0, 1),
        vmem=56,
    )
    w_spatial = lax.all_gather(w_shard, "queue", axis=0, tiled=True)

    arrived = lax.all_to_all(packed, "queue", split_axis=0, concat_axis=0, tiled=True)
    row_pick = jnp.asarray(weight_rows(), BF16)

    level = lax.dynamic_index_in_dim(levels, queue_pos, 0, keepdims=False)
    following = lax.dynamic_index_in_dim(
        jnp.concatenate([levels[1:], jnp.full((1,), top_level + 1, levels.dtype)]), queue_pos, 0, keepdims=False
    )
    mods = lax.dynamic_index_in_dim(modulation, level, 0, keepdims=False).astype(F32)
    new_mods = lax.dynamic_index_in_dim(modulation, following - 1, 0, keepdims=False).astype(F32)
    a = lax.dynamic_index_in_dim(alpha_bar, level, 0, keepdims=False)
    b = lax.dynamic_index_in_dim(alpha_bar, level - 1, 0, keepdims=False)
    coef = jnp.stack([jnp.sqrt(1.0 - a), 1.0 / jnp.sqrt(a), jnp.sqrt(b), jnp.sqrt(1.0 - b)])

    ua, va, cb, sb = position_factors(seqs, tokens, width)
    rows = seqs * tokens
    own_rows = videos * tokens
    sums = call(
        place_kernel,
        jax.ShapeDtypeStruct((seqs, 24, tokens), F32),
        (w_embed, ua, va, cb, sb),
        flops=100_000_000,
        vmem=56,
    )
    gain, shift = 1.0 + new_mods[4:5], new_mods[3:4]
    emb_f32 = w_embed.astype(F32)
    centered = emb_f32 - jnp.mean(emb_f32, axis=-1, keepdims=True)
    gram = jnp.dot(centered, centered.T, precision=lax.Precision.HIGHEST) * (1.0 / width)
    gram = jnp.concatenate([gram, rounding_rest(gram)], axis=-1).astype(BF16)
    centered = centered * gain
    eight = jnp.zeros((7, width), F32)
    few = [centered, rounding_rest(centered), shift, eight, rounding_rest(shift), eight]
    few = jnp.concatenate(few, axis=0).astype(BF16)
    latents_t = latents.reshape(videos, tokens, -1).transpose(0, 2, 1)
    fresh_t = fresh.transpose(0, 2, 1)
    w_final_t = w_final.T
    early = (arrived, sums, few, gram, mods, new_mods, coef, latents_t, fresh_t, w_final_t)
    early = lax.optimization_barrier(early)
    arrived, sums, few, gram, mods, new_mods, coef, latents_t, fresh_t, w_final_t = early

    attended = call(
        temporal_kernel,
        jax.ShapeDtypeStruct((frames, tokens + tokens // 3, 128), BF16),
        (arrived, jnp.asarray(temporal_columns(), BF16)),
        scratch=[pltpu.VMEM((frames, tokens, 768), F32), pltpu.VMEM((frames, tokens, 2 * SLOT), F32)],
        flops=4_000_000_000,
    )
    stacked, attended = lax.optimization_barrier((arrived, attended))
    w_mine = call(
        unstack_kernel,
        jax.ShapeDtypeStruct((PADDED, PADDED), BF16),
        (stacked, row_pick),
        flops=20_000_000_000,
    )
    w_other = lax.ppermute(w_mine, "seq", [(i, i ^ 1) for i in range(seqs)])
    returned = lax.all_to_all(attended, "queue", split_axis=0, concat_axis=0, tiled=True)

    stepped = call(
        step_kernel,
        jax.ShapeDtypeStruct((videos, latents.shape[-1], tokens), BF16),
        (
            coef,
            core.reshape(1),
            returned,
            hidden.reshape(videos, tokens, width),
            latents_t,
            w_mine,
            w_other,
            w_final_t,
            mods,
        ),
        smem=(0, 1),
        flops=1_000_000_000,
    )
    arriving = lax.ppermute(stepped, "queue", [(f, f - 1) for f in range(1, frames)])
    queued = jnp.where(queue_pos == frames - 1, fresh_t, arriving)

    everyone = lax.all_to_all(
        jnp.tile(queued, (seqs // videos, 1, 1)), "seq", split_axis=0, concat_axis=0, tiled=True
    )
    groups = [[videos * g + i for i in range(videos)] for g in range(seqs // videos)]
    group = (seq_pos // videos).reshape(1)
    mix, offset, pq, pkv = call(
        prepare_kernel,
        (
            jax.ShapeDtypeStruct((2 * w_embed.shape[0], 3 * PADDED), BF16),
            jax.ShapeDtypeStruct((8, 3 * PADDED), F32),
            jax.ShapeDtypeStruct((own_rows, PADDED), BF16),
            jax.ShapeDtypeStruct((rows, 2 * PADDED), BF16),
        ),
        (group, few, new_mods, ua, va, cb, sb, w_spatial),
        scratch=[
            pltpu.VMEM((rows, width), BF16),
            pltpu.VMEM((width, 3 * PADDED), BF16),
            pltpu.VMEM((rows, 2 * PADDED), BF16),
            pltpu.SemaphoreType.DMA((3,)),
            pltpu.SemaphoreType.DMA((4,)),
        ],
        smem=(0,),
        hbm=(7,),
        hbm_out=(3,),
        flops=8_000_000_000,
        vmem=56,
    )
    spatial = call(
        spatial_kernel,
        jax.ShapeDtypeStruct((videos, tokens, PADDED), BF16),
        (group, everyone, gram, sums, mix, offset, pq, pkv),
        scratch=[
            pltpu.VMEM((rows // own_rows, own_rows, 2 * PADDED), BF16),
            pltpu.VMEM((rows, 2 * latents.shape[-1] + 8), F32),
            pltpu.VMEM((rows, PADDED), BF16),
            pltpu.VMEM((rows, PADDED), BF16),
            pltpu.SemaphoreType.DMA((rows // own_rows,)),
        ],
        smem=(0,),
        hbm=(7,),
        flops=20_000_000_000,
        vmem=56,
    )
    heads_out = lax.all_to_all(
        spatial, "seq", split_axis=0, concat_axis=0, tiled=True, axis_index_groups=groups
    )
    late, _ = lax.optimization_barrier((w_spatial, spatial))
    w_s = call(
        projection_kernel,
        jax.ShapeDtypeStruct((PADDED, width), BF16),
        (row_pick, late),
        scratch=[pltpu.VMEM((width, PADDED), BF16), pltpu.SemaphoreType.DMA],
        hbm=(1,),
        flops=20_000_000_000,
        vmem=56,
    )
    block_out = call(
        finish_kernel,
        jax.ShapeDtypeStruct((videos, tokens, width), BF16),
        (seq_pos.reshape(1), heads_out, queued, w_embed, ua, va, cb, sb, new_mods, w_s),
        smem=(0,),
        flops=1_000_000_000,
        vmem=56,
    )
    return (
        queued.transpose(0, 2, 1).reshape(videos, 1, tokens, -1),
        block_out.reshape(videos, 1, tokens, width),
    )


def solution(mesh):
    in_specs = (
        P(None, "queue", "seq", None),
        P(None, "queue", "seq", None),
        P(None, "queue", "seq", None),
        P(None, "seq", None),
        P(),
        P(),
        P(),
        P("queue", None),
        P(),
        P(),
        P("queue", None),
        P("queue", None),
    )
    out_specs = (P(None, "queue", "seq", None), P(None, "queue", "seq", None))
    return jax.shard_map(shards, mesh=mesh, in_specs=in_specs, out_specs=out_specs, check_vma=False)
```

```python
import math

import jax
import jax.numpy as jnp
import numpy as np
from jax import lax
from jax.experimental import pallas as pl
from jax.experimental.pallas import tpu as pltpu
from jax.sharding import PartitionSpec as P

HEADS = 8
HDIM = 72
HALF = HDIM // 2
SLOT = 80
PADDED = HEADS * SLOT
DENSE = HEADS * HDIM
SCORE_SCALE = 1.0 / math.sqrt(HDIM)
LOG2E = math.log2(math.e)
F32 = jnp.float32
BF16 = jnp.bfloat16
MIB = 1024 * 1024


def mm(a, b):
    return jnp.dot(a, b, preferred_element_type=F32)


def mm_nt(a, b):
    return lax.dot_general(a, b, (((1,), (1,)), ((), ())), preferred_element_type=F32)


def call(kernel, out_shape, args, scratch=(), smem=(), hbm=(), hbm_out=(), flops=0, vmem=24, grid=None, in_specs=None, out_specs=None):
    moved = sum(a.size * a.dtype.itemsize for a in args)
    if in_specs is None:
        in_specs = [
            pl.BlockSpec(memory_space=pltpu.SMEM if i in smem else pl.ANY if i in hbm else pltpu.VMEM)
            for i in range(len(args))
        ]
        if isinstance(out_shape, tuple):
            out_specs = tuple(
                pl.BlockSpec(memory_space=pl.ANY if i in hbm_out else pltpu.VMEM) for i in range(len(out_shape))
            )
        else:
            out_specs = pl.BlockSpec(memory_space=pltpu.VMEM)
    return pl.pallas_call(
        kernel,
        out_shape=out_shape,
        in_specs=in_specs,
        out_specs=out_specs,
        scratch_shapes=list(scratch),
        compiler_params=pltpu.CompilerParams(vmem_limit_bytes=vmem * MIB),
        cost_estimate=pl.CostEstimate(flops=flops, bytes_accessed=moved, transcendentals=0),
        **({"grid": grid} if grid else {}),
    )(*args)


def layer_norm(values):
    center = values - jnp.mean(values, axis=-1, keepdims=True)
    spread = jnp.mean(center * center, axis=-1, keepdims=True)
    return center * lax.rsqrt(spread + 1e-06)


def pack_kernel(
    core_ref, x_ref, tout_ref, sqkv_ref, sout_ref, o_ref, shard_ref,
    x, tout, sqkv, sout, packed, shard, x_sem, w_sem, o_sem,
):
    videos, tokens, columns = x.shape
    pairs = packed.shape[0] // videos
    width = columns // pairs

    def load(v):
        return pltpu.make_async_copy(x_ref.at[v], x.at[v], x_sem.at[v])

    weights = [
        pltpu.make_async_copy(source, target, w_sem.at[i])
        for i, (source, target) in enumerate(((tout_ref, tout), (sqkv_ref, sqkv), (sout_ref, sout)))
    ]

    def store(v):
        at = slice(pairs * v, pairs * (v + 1))
        return pltpu.make_async_copy(packed.at[at], o_ref.at[at], o_sem.at[v])

    weights[0].start()
    load(0).start()
    weights[1].start()
    weights[2].start()
    for v in range(1, videos):
        load(v).start()

    weights[0].wait()
    half = tout.shape[-1] // 2
    left, right = tout[:, :half].astype(F32), tout[:, half:].astype(F32)
    own = jnp.where(core_ref[0] == 0, left, right)
    weight = jnp.concatenate([own[:, : half // 2], own[:, half // 2 :]], axis=0).astype(BF16)
    load(0).wait()
    for part in range(pairs):
        packed[part, :, :width] = x[0, :, part * width : (part + 1) * width]
        packed[part, :, width:] = weight
    store(0).start()

    weights[1].wait()
    weights[2].wait()
    pieces = []
    for part in (1, 2, 0):
        for h in range(HEADS):
            at = HDIM * (3 * h + part)
            pieces.append(sqkv[:, at : at + HDIM])
    ends = jnp.concatenate([sout[:, :half].astype(F32), sout[:, half:].astype(F32)], axis=0)
    shard[...] = jnp.concatenate(pieces + [ends.astype(BF16)], axis=-1)
    last = pltpu.make_async_copy(shard, shard_ref, w_sem.at[3])
    last.start()

    for v in range(1, videos):
        load(v).wait()
        for part in range(pairs):
            packed[pairs * v + part, :, :width] = x[v, :, part * width : (part + 1) * width]
            packed[pairs * v + part, :, width:] = weight
        store(v).start()
    last.wait()
    for v in range(videos):
        store(v).wait()


def temporal_columns():
    pick = np.zeros((6 * HDIM, 768), np.float32)
    for head in range(2):
        base = 3 * HDIM * head
        for i in range(HDIM):
            pick[base + i, 256 * head + i] = 1.0
            pick[base + HDIM + i, 256 * head + 128 + i] = 1.0
            pick[base + 2 * HDIM + i, 512 + SLOT * head + i] = 1.0
    return pick


def weight_rows(slot):
    pick = np.zeros((2 * slot, 256), np.float32)
    for shard in range(2):
        for i in range(HALF):
            pick[HALF * shard + i, HDIM * shard + i] = 1.0
            pick[slot + HALF * shard + i, HDIM * shard + HALF + i] = 1.0
    return pick


def temporal_kernel(x_ref, pick_ref, o_ref, parts, total):
    frames, tokens, _ = x_ref.shape
    flat = x_ref[:, :, : 6 * HDIM].astype(F32).reshape(frames * tokens, 6 * HDIM).astype(BF16)
    parts[...] = mm(flat, pick_ref[...]).reshape(frames, tokens, -1)
    rows = frames * 8
    first = lax.broadcasted_iota(jnp.int32, (1, 2 * SLOT), 1) < SLOT
    same = (
        lax.broadcasted_iota(jnp.int32, (rows, rows), 0) % 8
        == lax.broadcasted_iota(jnp.int32, (rows, rows), 1) % 8
    )
    blocks = tokens // 8
    pieces = [parts[:, 8 * i : 8 * i + 8, :].reshape(rows, -1).astype(BF16) for i in range(blocks)]
    scores = [
        mm_nt(piece[:, 256 * head : 256 * head + 128], piece[:, 256 * head + 128 : 256 * head + 256])
        for piece in pieces
        for head in range(2)
    ]
    scores = jnp.concatenate(scores, axis=0).reshape(2 * blocks, rows, rows)
    scores = jnp.where(same[None], scores * SCORE_SCALE, -jnp.inf)
    raised = jnp.exp(scores - jnp.max(scores, axis=-1, keepdims=True))
    weights = (raised / jnp.sum(raised, axis=-1, keepdims=True)).astype(BF16)
    for i in range(blocks):
        v = pieces[i][:, 512 : 512 + 2 * SLOT]
        out = jnp.where(first, mm(weights[2 * i], v), mm(weights[2 * i + 1], v))
        total[:, 8 * i : 8 * i + 8, :] = out.reshape(frames, 8, 2 * SLOT)
    side = total[:, :, 128:]
    third = tokens // 3
    side = [side[:, third * i : third * (i + 1), :] for i in range(3)] + [jnp.zeros((frames, third, 32), F32)]
    o_ref[:, :tokens, :] = total[:, :, :128].astype(BF16)
    o_ref[:, tokens:, :] = jnp.concatenate(side, axis=-1).astype(BF16)


def unstack_kernel(x_ref, rows_ref, w_ref):
    shards, rows, width = x_ref.shape
    start = 6 * HDIM
    blank = jnp.zeros((SLOT, w_ref.shape[-1] - 2 * (width - start)), F32)
    for h in range(shards // 2):
        pair = x_ref[2 * h : 2 * h + 2, :, start:].astype(F32).reshape(2 * rows, -1).astype(BF16)
        both = mm(rows_ref[:, : 2 * rows], pair)
        w_ref[SLOT * h : SLOT * (h + 1), :] = jnp.concatenate(
            [both[:SLOT], both[SLOT:], blank], axis=-1
        ).astype(BF16)


def step_kernel(coef_ref, core_ref, att_ref, hid_ref, lat_ref, mine_ref, other_ref, wf_ref, mod_ref, o_ref):
    videos, tokens, width = hid_ref.shape
    rows = videos * tokens
    pairs = att_ref.shape[0] // videos
    att = att_ref[...].astype(F32)
    side = jnp.concatenate([att[:, tokens:, 32 * i : 32 * (i + 1)] for i in range(3)], axis=1)
    att = jnp.concatenate([att[:, :tokens, :], side], axis=-1).reshape(videos, pairs, tokens, 2 * SLOT)
    own = far = None
    for p in range(pairs):
        part = att[:, p].reshape(rows, 2 * SLOT).astype(BF16)
        at = slice(2 * SLOT * p, 2 * SLOT * (p + 1))
        own_term, far_term = mm(part, mine_ref[at, :]), mm(part, other_ref[at, :])
        own = own_term if own is None else own + own_term
        far = far_term if far is None else far + far_term
    low = core_ref[0] == 0
    half = width // 2
    proj = jnp.concatenate([jnp.where(low, own, far)[:, :half], jnp.where(low, far, own)[:, :half]], axis=-1)
    residual = hid_ref[...].astype(F32).reshape(rows, width) + mod_ref[0:1, :] * proj
    final_in = (layer_norm(residual) * (1.0 + mod_ref[2:3, :]) + mod_ref[1:2, :]).astype(BF16)
    predicted = mm_nt(wf_ref[...], final_in)
    for v in range(videos):
        pred = predicted[:, tokens * v : tokens * (v + 1)]
        clean = (lat_ref[v].astype(F32) - coef_ref[0] * pred) * coef_ref[1]
        o_ref[v] = (coef_ref[2] * clean + coef_ref[3] * pred).astype(BF16)


def centered_place(c, ua_ref, va_ref, cb_ref, sb_ref):
    place = ua_ref[pl.ds(c, 1), :] * cb_ref[...] + va_ref[pl.ds(c, 1), :] * sb_ref[...]
    return place - jnp.mean(place, axis=-1, keepdims=True)


def place_kernel(wemb_ref, ua_ref, va_ref, cb_ref, sb_ref, sums_ref):
    tokens, width = cb_ref.shape
    blank = jnp.zeros((tokens, 7), F32)

    def one(few, carry):
        for i in range(4):
            c = 4 * few + i
            center = centered_place(c, ua_ref, va_ref, cb_ref, sb_ref)
            high = center.astype(BF16)
            low = (center - high.astype(F32)).astype(BF16)
            cross = (mm_nt(high, wemb_ref[...]) + mm_nt(low, wemb_ref[...])) * (2.0 / width)
            square = jnp.mean(center * center, axis=-1, keepdims=True)
            sums_ref[c] = jnp.concatenate([cross, square, blank], axis=-1).T
        return carry

    lax.fori_loop(0, sums_ref.shape[0] // 4, one, 0)


def prepare_kernel(
    group_ref, few_ref, mod_ref, ua_ref, va_ref, cb_ref, sb_ref, w_ref, mix_out, offset_out, q_out, kv_out,
    p, w, made, w_sem, out_sem,
):
    rows = q_out.shape[0]
    tokens = cb_ref.shape[0]
    step = 2 * rows
    steps = made.shape[0] // step

    edges = (0, 512, 2 * DENSE, 2 * DENSE + PADDED)

    def load_w(part):
        at = slice(edges[part], edges[part + 1])
        return pltpu.make_async_copy(w_ref.at[:, at], w.at[:, at], w_sem.at[part])

    def store(i):
        at = slice(step * i, step * (i + 1))
        return pltpu.make_async_copy(made.at[at], kv_out.at[at], out_sem.at[i])

    for part in range(3):
        load_w(part).start()
    gain = 1.0 + mod_ref[4:5, :]

    def place(i):
        for c in range(step // tokens * i, step // tokens * (i + 1), 2):
            two = [centered_place(c + j, ua_ref, va_ref, cb_ref, sb_ref) * gain for j in range(2)]
            p[tokens * c : tokens * (c + 2), :] = jnp.concatenate(two, axis=0).astype(BF16)

    place(0)
    for i in range(steps):
        here = slice(step * i, step * (i + 1))
        for part in range(2):
            if i == 0:
                load_w(part).wait()
            columns = slice(edges[part], edges[part + 1])
            if i + 1 < steps:
                made[here, columns] = mm(p[here, :], w[:, columns]).astype(BF16)
            else:
                both = mm(jnp.concatenate([p[here, :], few_ref[...]], axis=0), w[:, columns])
                made[here, columns] = both[:step].astype(BF16)
                few = both[step:] if part == 0 else jnp.concatenate([few, both[step:]], axis=-1)
            if part == 0 and i + 1 < steps:
                place(i + 1)
        store(i).start()
    load_w(2).wait()
    start = pl.multiple_of(group_ref[0] * rows, rows)
    own = jnp.concatenate([p[pl.ds(start, rows), :], few_ref[...]], axis=0)
    own = mm(own, w[:, edges[2] :])
    q_out[...] = own[:rows].astype(BF16)
    few = jnp.concatenate([few, own[rows:]], axis=-1)
    patch = mix_out.shape[0] // 2
    mix = few[:patch] + few[patch : 2 * patch]
    high = mix.astype(BF16).astype(F32)
    mix_out[...] = jnp.concatenate([high, mix - high], axis=0).astype(BF16)
    offset_out[...] = few[2 * patch : 2 * patch + 8] + few[2 * patch + 8 :]
    for i in range(steps):
        store(i).wait()


def spatial_kernel(
    group_ref, lat_ref, gram_ref, sums_ref, mix_ref, offset_ref, pq_ref, pkv_ref,
    o_ref, held, columns, kvs, sem,
):
    chunks, patch, tokens = lat_ref.shape
    members = o_ref.shape[0]
    block = members * tokens
    blocks = chunks // members

    def fetch(index):
        start = pl.multiple_of(index * block, block)
        return pltpu.make_async_copy(pkv_ref.at[pl.ds(start, block), :], held.at[index], sem.at[index])

    for i in range(blocks):
        fetch(i).start()

    gram = gram_ref[...]
    for c in range(chunks):
        once = lat_ref[c].astype(F32)
        twice = jnp.concatenate([once, once], axis=0)
        sums = sums_ref[c]
        mixed = mm(gram, twice.astype(BF16)) + sums[:patch]
        variance = jnp.sum(mixed * once, axis=0, keepdims=True) + sums[patch : patch + 1]
        scale = lax.rsqrt(jnp.maximum(variance, 0.0) + 1e-06)
        rows = jnp.concatenate([twice, jnp.broadcast_to(scale, (8, tokens))], axis=0)
        columns[tokens * c : tokens * (c + 1), :] = rows.T

    lane = lax.broadcasted_iota(jnp.int32, (1, 2 * DENSE), 1)

    kv_mix = mix_ref[:, : 2 * DENSE]
    kv_offset = offset_ref[0:1, : 2 * DENSE]

    def one(index, carry):
        start = pl.multiple_of(index * block, block)
        column = columns[pl.ds(start, block), :]
        latent, scale = column[:, : 2 * patch].astype(BF16), column[:, 2 * patch : 2 * patch + 1]
        mixed = mm(latent, kv_mix)
        fetch(index).wait()
        kv = (mixed + held[index].astype(F32)) * scale + kv_offset
        kvs[pl.ds(start, block), :] = kv.astype(BF16)
        return carry

    lax.fori_loop(0, blocks, one, 0)

    column = columns[pl.ds(pl.multiple_of(group_ref[0] * block, block), block), :]
    latent, scale = column[:, : 2 * patch].astype(BF16), column[:, 2 * patch : 2 * patch + 1]
    q_all = (mm(latent, mix_ref[:, 2 * DENSE :]) + pq_ref[...].astype(F32)) * scale + offset_ref[0:1, 2 * DENSE :]
    q_all = q_all.astype(BF16).astype(F32)
    merged = [None] * (PADDED // 128)

    def window(at):
        first, last = at // 128, (at + HDIM - 1) // 128
        here = slice(128 * first, 128 * (last + 1))
        inside = (lane >= at) & (lane < at + HDIM)
        return first, last, here, inside[:, here]

    def score(h):
        _, _, here, inside = window(HDIM * h)
        return mm_nt(jnp.where(inside, q_all[:, here], 0.0).astype(BF16), kvs[:, here])

    def weigh(scores):
        top = jnp.max(scores, axis=-1, keepdims=True)
        raised = jnp.exp2((scores - top) * (SCORE_SCALE * LOG2E))
        return raised.astype(BF16), jnp.sum(raised, axis=-1, keepdims=True)

    def blend(h, weighed):
        raised, total = weighed
        first, last, here, inside = window(DENSE + HDIM * h)
        found = jnp.where(inside, mm(raised, kvs[:, here]) * (1.0 / total), 0.0)
        for tile in range(first, last + 1):
            piece = found[:, 128 * (tile - first) : 128 * (tile - first + 1)]
            at = tile - DENSE // 128
            merged[at] = piece if merged[at] is None else merged[at] + piece

    scores = score(0)
    raised = None
    for h in range(HEADS):
        following = score(h + 1) if h + 1 < HEADS else None
        if raised is not None:
            blend(h - 1, raised)
        raised = weigh(scores)
        scores = following
    blend(HEADS - 1, raised)
    o_ref[...] = jnp.concatenate(merged, axis=-1).reshape(members, tokens, PADDED).astype(BF16)


def projection_kernel(rows_ref, w_ref, w_out, raw, sem):
    width = raw.shape[-1]
    skip = width - w_out.shape[-1] // 2
    copy = pltpu.make_async_copy(w_ref.at[:, w_ref.shape[-1] - width :], raw, sem)
    copy.start()
    copy.wait()
    made = [jnp.zeros((skip, w_out.shape[-1]), F32)]
    for h in range(HEADS):
        both = mm(rows_ref[:, : 2 * HDIM], raw[2 * HDIM * h : 2 * HDIM * (h + 1), :])
        made.append(jnp.concatenate([both[:HDIM, skip:], both[HDIM:, skip:]], axis=-1))
    w_out[...] = jnp.concatenate(made, axis=0).astype(BF16)


def finish_kernel(
    seq_ref, att_ref, lat_ref, wemb_ref, ua_ref, va_ref, cb_ref, sb_ref, mod_ref, w_ref, o_ref
):
    videos, tokens, width = o_ref.shape
    s = seq_ref[0]
    place = ua_ref[pl.ds(s, 1), :] * cb_ref[...] + va_ref[pl.ds(s, 1), :] * sb_ref[...]
    gate = mod_ref[5:6, :]
    att = att_ref[...].astype(F32).reshape(videos * tokens, PADDED).astype(BF16)
    embedded = [mm(lat_ref[v].astype(F32).T.astype(BF16), wemb_ref[...]) + place for v in range(videos)]
    gated = mm(att, w_ref[...]) * gate
    for v in range(videos):
        o_ref[v] = (embedded[v] + gated[tokens * v : tokens * (v + 1), :]).astype(BF16)


def position_factors(chunks, tokens, width):
    half = width // 2
    frequency = jnp.exp(jnp.arange(half, dtype=F32) * (-math.log(10000.0) / half))
    start = (jnp.arange(chunks, dtype=F32) * tokens)[:, None] * frequency[None, :]
    inner = jnp.arange(tokens, dtype=F32)[:, None] * frequency[None, :]
    sin_a, cos_a, sin_b, cos_b = jnp.sin(start), jnp.cos(start), jnp.sin(inner), jnp.cos(inner)
    ua = jnp.concatenate([sin_a, cos_a], axis=-1)
    va = jnp.concatenate([cos_a, -sin_a], axis=-1)
    cb = jnp.concatenate([cos_b, cos_b], axis=-1)
    sb = jnp.concatenate([sin_b, sin_b], axis=-1)
    return ua, va, cb, sb


def rounding_rest(values):
    return values - lax.reduce_precision(values, 8, 7)


def shards(
    t_qkv, hidden, latents, fresh, levels, alpha_bar, modulation, w_tout, w_final, w_embed, w_sqkv, w_sout,
):
    frames = lax.axis_size("queue")
    seqs = lax.axis_size("seq")
    queue_pos = lax.axis_index("queue")
    seq_pos = lax.axis_index("seq")
    videos, _, tokens, width = hidden.shape
    top_level = alpha_bar.shape[0] - 1
    pairs = frames // videos

    core = seq_pos % 2
    half = width // 2
    width_part = t_qkv.shape[-1] // pairs
    sent = width_part + half // 2
    packed, w_shard = call(
        pack_kernel,
        (
            jax.ShapeDtypeStruct((frames, tokens, sent), BF16),
            jax.ShapeDtypeStruct((w_sqkv.shape[0], 4 * DENSE), BF16),
        ),
        (core.reshape(1), t_qkv.reshape(videos, tokens, -1), w_tout, w_sqkv, w_sout),
        scratch=[
            pltpu.VMEM((videos, tokens, t_qkv.shape[-1]), BF16),
            pltpu.VMEM(w_tout.shape, BF16),
            pltpu.VMEM(w_sqkv.shape, BF16),
            pltpu.VMEM(w_sout.shape, BF16),
            pltpu.VMEM((frames, tokens, sent), BF16),
            pltpu.VMEM((w_sqkv.shape[0], 4 * DENSE), BF16),
            pltpu.SemaphoreType.DMA((videos,)),
            pltpu.SemaphoreType.DMA((4,)),
            pltpu.SemaphoreType.DMA((videos,)),
        ],
        smem=(0,),
        hbm=(1, 2, 3, 4),
        hbm_out=(0, 1),
        vmem=56,
    )
    w_spatial = lax.all_gather(w_shard, "queue", axis=0, tiled=True)

    arrived = lax.all_to_all(packed, "queue", split_axis=0, concat_axis=0, tiled=True)
    row_pick = jnp.asarray(weight_rows(SLOT), BF16)
    dense_pick = jnp.asarray(weight_rows(HDIM), BF16)

    level = lax.dynamic_index_in_dim(levels, queue_pos, 0, keepdims=False)
    following = lax.dynamic_index_in_dim(
        jnp.concatenate([levels[1:], jnp.full((1,), top_level + 1, levels.dtype)]), queue_pos, 0, keepdims=False
    )
    mods = lax.dynamic_index_in_dim(modulation, level, 0, keepdims=False).astype(F32)
    new_mods = lax.dynamic_index_in_dim(modulation, following - 1, 0, keepdims=False).astype(F32)
    a = lax.dynamic_index_in_dim(alpha_bar, level, 0, keepdims=False)
    b = lax.dynamic_index_in_dim(alpha_bar, level - 1, 0, keepdims=False)
    coef = jnp.stack([jnp.sqrt(1.0 - a), 1.0 / jnp.sqrt(a), jnp.sqrt(b), jnp.sqrt(1.0 - b)])

    ua, va, cb, sb = position_factors(seqs, tokens, width)
    rows = seqs * tokens
    own_rows = videos * tokens
    sums = call(
        place_kernel,
        jax.ShapeDtypeStruct((seqs, 24, tokens), F32),
        (w_embed, ua, va, cb, sb),
        flops=100_000_000,
        vmem=56,
    )
    gain, shift = 1.0 + new_mods[4:5], new_mods[3:4]
    emb_f32 = w_embed.astype(F32)
    centered = emb_f32 - jnp.mean(emb_f32, axis=-1, keepdims=True)
    gram = jnp.dot(centered, centered.T, precision=lax.Precision.HIGHEST) * (1.0 / width)
    gram = jnp.concatenate([gram, rounding_rest(gram)], axis=-1).astype(BF16)
    centered = centered * gain
    eight = jnp.zeros((7, width), F32)
    few = [centered, rounding_rest(centered), shift, eight, rounding_rest(shift), eight]
    few = jnp.concatenate(few, axis=0).astype(BF16)
    latents_t = latents.reshape(videos, tokens, -1).transpose(0, 2, 1)
    fresh_t = fresh.transpose(0, 2, 1)
    w_final_t = w_final.T
    early = (arrived, sums, few, gram, mods, new_mods, coef, latents_t, fresh_t, w_final_t)
    early = lax.optimization_barrier(early)
    arrived, sums, few, gram, mods, new_mods, coef, latents_t, fresh_t, w_final_t = early

    attended = call(
        temporal_kernel,
        jax.ShapeDtypeStruct((frames, tokens + tokens // 3, 128), BF16),
        (arrived, jnp.asarray(temporal_columns(), BF16)),
        scratch=[pltpu.VMEM((frames, tokens, 768), F32), pltpu.VMEM((frames, tokens, 2 * SLOT), F32)],
        flops=4_000_000_000,
    )
    stacked, attended = lax.optimization_barrier((arrived, attended))
    w_mine = call(
        unstack_kernel,
        jax.ShapeDtypeStruct((PADDED, PADDED), BF16),
        (stacked, row_pick),
        flops=20_000_000_000,
    )
    w_other = lax.ppermute(w_mine, "seq", [(i, i ^ 1) for i in range(seqs)])
    returned = lax.all_to_all(attended, "queue", split_axis=0, concat_axis=0, tiled=True)

    stepped = call(
        step_kernel,
        jax.ShapeDtypeStruct((videos, latents.shape[-1], tokens), BF16),
        (
            coef,
            core.reshape(1),
            returned,
            hidden.reshape(videos, tokens, width),
            latents_t,
            w_mine,
            w_other,
            w_final_t,
            mods,
        ),
        smem=(0, 1),
        flops=1_000_000_000,
    )
    arriving = lax.ppermute(stepped, "queue", [(f, f - 1) for f in range(1, frames)])
    queued = jnp.where(queue_pos == frames - 1, fresh_t, arriving)

    everyone = lax.all_to_all(
        jnp.tile(queued, (seqs // videos, 1, 1)), "seq", split_axis=0, concat_axis=0, tiled=True
    )
    groups = [[videos * g + i for i in range(videos)] for g in range(seqs // videos)]
    group = (seq_pos // videos).reshape(1)
    mix, offset, pq, pkv = call(
        prepare_kernel,
        (
            jax.ShapeDtypeStruct((2 * w_embed.shape[0], 2 * DENSE + PADDED), BF16),
            jax.ShapeDtypeStruct((8, 2 * DENSE + PADDED), F32),
            jax.ShapeDtypeStruct((own_rows, PADDED), BF16),
            jax.ShapeDtypeStruct((rows, 2 * DENSE), BF16),
        ),
        (group, few, new_mods, ua, va, cb, sb, w_spatial),
        scratch=[
            pltpu.VMEM((rows, width), BF16),
            pltpu.VMEM((width, 2 * DENSE + PADDED), BF16),
            pltpu.VMEM((rows, 2 * DENSE), BF16),
            pltpu.SemaphoreType.DMA((3,)),
            pltpu.SemaphoreType.DMA((4,)),
        ],
        smem=(0,),
        hbm=(7,),
        hbm_out=(3,),
        flops=8_000_000_000,
        vmem=56,
    )
    spatial = call(
        spatial_kernel,
        jax.ShapeDtypeStruct((videos, tokens, PADDED), BF16),
        (group, everyone, gram, sums, mix, offset, pq, pkv),
        scratch=[
            pltpu.VMEM((rows // own_rows, own_rows, 2 * DENSE), BF16),
            pltpu.VMEM((rows, 2 * latents.shape[-1] + 8), F32),
            pltpu.VMEM((rows, 2 * DENSE), BF16),
            pltpu.SemaphoreType.DMA((rows // own_rows,)),
        ],
        smem=(0,),
        hbm=(7,),
        flops=20_000_000_000,
        vmem=56,
    )
    heads_out = lax.all_to_all(
        spatial, "seq", split_axis=0, concat_axis=0, tiled=True, axis_index_groups=groups
    )
    late, _ = lax.optimization_barrier((w_spatial, spatial))
    w_s = call(
        projection_kernel,
        jax.ShapeDtypeStruct((PADDED, width), BF16),
        (dense_pick, late),
        scratch=[pltpu.VMEM((width, PADDED), BF16), pltpu.SemaphoreType.DMA],
        hbm=(1,),
        flops=20_000_000_000,
        vmem=56,
    )
    block_out = call(
        finish_kernel,
        jax.ShapeDtypeStruct((videos, tokens, width), BF16),
        (seq_pos.reshape(1), heads_out, queued, w_embed, ua, va, cb, sb, new_mods, w_s),
        smem=(0,),
        flops=1_000_000_000,
    )
    return (
        queued.transpose(0, 2, 1).reshape(videos, 1, tokens, -1),
        block_out.reshape(videos, 1, tokens, width),
    )


def solution(mesh):
    in_specs = (
        P(None, "queue", "seq", None),
        P(None, "queue", "seq", None),
        P(None, "queue", "seq", None),
        P(None, "seq", None),
        P(),
        P(),
        P(),
        P("queue", None),
        P(),
        P(),
        P("queue", None),
        P("queue", None),
    )
    out_specs = (P(None, "queue", "seq", None), P(None, "queue", "seq", None))
    return jax.shard_map(shards, mesh=mesh, in_specs=in_specs, out_specs=out_specs, check_vma=False)
```

```python
import math

import jax
import jax.numpy as jnp
import numpy as np
from jax import lax
from jax.experimental import pallas as pl
from jax.experimental.pallas import tpu as pltpu
from jax.sharding import PartitionSpec as P

HEADS = 8
HDIM = 72
HALF = HDIM // 2
SLOT = 80
PADDED = HEADS * SLOT
DENSE = HEADS * HDIM
SCORE_SCALE = 1.0 / math.sqrt(HDIM)
LOG2E = math.log2(math.e)
F32 = jnp.float32
BF16 = jnp.bfloat16
MIB = 1024 * 1024


def mm(a, b):
    return jnp.dot(a, b, preferred_element_type=F32)


def mm_nt(a, b):
    return lax.dot_general(a, b, (((1,), (1,)), ((), ())), preferred_element_type=F32)


def call(kernel, out_shape, args, scratch=(), smem=(), hbm=(), hbm_out=(), flops=0, vmem=24, grid=None, in_specs=None, out_specs=None):
    moved = sum(a.size * a.dtype.itemsize for a in args)
    if in_specs is None:
        in_specs = [
            pl.BlockSpec(memory_space=pltpu.SMEM if i in smem else pl.ANY if i in hbm else pltpu.VMEM)
            for i in range(len(args))
        ]
        if isinstance(out_shape, tuple):
            out_specs = tuple(
                pl.BlockSpec(memory_space=pl.ANY if i in hbm_out else pltpu.VMEM) for i in range(len(out_shape))
            )
        else:
            out_specs = pl.BlockSpec(memory_space=pltpu.VMEM)
    return pl.pallas_call(
        kernel,
        out_shape=out_shape,
        in_specs=in_specs,
        out_specs=out_specs,
        scratch_shapes=list(scratch),
        compiler_params=pltpu.CompilerParams(vmem_limit_bytes=vmem * MIB),
        cost_estimate=pl.CostEstimate(flops=flops, bytes_accessed=moved, transcendentals=0),
        **({"grid": grid} if grid else {}),
    )(*args)


def layer_norm(values):
    center = values - jnp.mean(values, axis=-1, keepdims=True)
    spread = jnp.mean(center * center, axis=-1, keepdims=True)
    return center * lax.rsqrt(spread + 1e-06)


def pack_kernel(
    core_ref, x_ref, tout_ref, sqkv_ref, sout_ref, o_ref, shard_ref,
    x, tout, sqkv, sout, packed, shard, x_sem, w_sem, o_sem,
):
    videos, tokens, columns = x.shape
    pairs = packed.shape[0] // videos
    width = columns // pairs

    def load(v):
        return pltpu.make_async_copy(x_ref.at[v], x.at[v], x_sem.at[v])

    weights = [
        pltpu.make_async_copy(source, target, w_sem.at[i])
        for i, (source, target) in enumerate(((tout_ref, tout), (sqkv_ref, sqkv), (sout_ref, sout)))
    ]

    def store(v):
        at = slice(pairs * v, pairs * (v + 1))
        return pltpu.make_async_copy(packed.at[at], o_ref.at[at], o_sem.at[v])

    weights[0].start()
    load(0).start()
    weights[1].start()
    weights[2].start()
    for v in range(1, videos):
        load(v).start()

    weights[0].wait()
    half = tout.shape[-1] // 2
    left, right = tout[:, :half].astype(F32), tout[:, half:].astype(F32)
    own = jnp.where(core_ref[0] == 0, left, right)
    weight = jnp.concatenate([own[:, : half // 2], own[:, half // 2 :]], axis=0).astype(BF16)
    load(0).wait()
    for part in range(pairs):
        packed[part, :, :width] = x[0, :, part * width : (part + 1) * width]
        packed[part, :, width:] = weight
    store(0).start()

    weights[1].wait()
    weights[2].wait()
    pieces = []
    for part in (1, 2, 0):
        for h in range(HEADS):
            at = HDIM * (3 * h + part)
            pieces.append(sqkv[:, at : at + HDIM])
    ends = jnp.concatenate([sout[:, :half].astype(F32), sout[:, half:].astype(F32)], axis=0)
    shard[...] = jnp.concatenate(pieces + [ends.astype(BF16)], axis=-1)
    last = pltpu.make_async_copy(shard, shard_ref, w_sem.at[3])
    last.start()

    for v in range(1, videos):
        load(v).wait()
        for part in range(pairs):
            packed[pairs * v + part, :, :width] = x[v, :, part * width : (part + 1) * width]
            packed[pairs * v + part, :, width:] = weight
        store(v).start()
    last.wait()
    for v in range(videos):
        store(v).wait()


def temporal_columns():
    pick = np.zeros((6 * HDIM, 768), np.float32)
    for head in range(2):
        base = 3 * HDIM * head
        for i in range(HDIM):
            pick[base + i, 256 * head + i] = 1.0
            pick[base + HDIM + i, 256 * head + 128 + i] = 1.0
            pick[base + 2 * HDIM + i, 512 + SLOT * head + i] = 1.0
    return pick


def weight_rows(slot):
    pick = np.zeros((2 * slot, 256), np.float32)
    for shard in range(2):
        for i in range(HALF):
            pick[HALF * shard + i, HDIM * shard + i] = 1.0
            pick[slot + HALF * shard + i, HDIM * shard + HALF + i] = 1.0
    return pick


def temporal_kernel(x_ref, pick_ref, o_ref, parts, total):
    frames, tokens, _ = x_ref.shape
    flat = x_ref[:, :, : 6 * HDIM].astype(F32).reshape(frames * tokens, 6 * HDIM).astype(BF16)
    parts[...] = mm(flat, pick_ref[...]).reshape(frames, tokens, -1)
    rows = frames * 8
    first = lax.broadcasted_iota(jnp.int32, (1, 2 * SLOT), 1) < SLOT
    same = (
        lax.broadcasted_iota(jnp.int32, (rows, rows), 0) % 8
        == lax.broadcasted_iota(jnp.int32, (rows, rows), 1) % 8
    )
    blocks = tokens // 8
    pieces = [parts[:, 8 * i : 8 * i + 8, :].reshape(rows, -1).astype(BF16) for i in range(blocks)]
    scores = [
        mm_nt(piece[:, 256 * head : 256 * head + 128], piece[:, 256 * head + 128 : 256 * head + 256])
        for piece in pieces
        for head in range(2)
    ]
    scores = jnp.concatenate(scores, axis=0).reshape(2 * blocks, rows, rows)
    scores = jnp.where(same[None], scores * SCORE_SCALE, -jnp.inf)
    raised = jnp.exp(scores - jnp.max(scores, axis=-1, keepdims=True))
    weights = (raised / jnp.sum(raised, axis=-1, keepdims=True)).astype(BF16)
    for i in range(blocks):
        v = pieces[i][:, 512 : 512 + 2 * SLOT]
        out = jnp.where(first, mm(weights[2 * i], v), mm(weights[2 * i + 1], v))
        total[:, 8 * i : 8 * i + 8, :] = out.reshape(frames, 8, 2 * SLOT)
    side = total[:, :, 128:]
    third = tokens // 3
    side = [side[:, third * i : third * (i + 1), :] for i in range(3)] + [jnp.zeros((frames, third, 32), F32)]
    o_ref[:, :tokens, :] = total[:, :, :128].astype(BF16)
    o_ref[:, tokens:, :] = jnp.concatenate(side, axis=-1).astype(BF16)


def unstack_kernel(x_ref, rows_ref, w_ref):
    shards, rows, width = x_ref.shape
    start = 6 * HDIM
    blank = jnp.zeros((SLOT, w_ref.shape[-1] - 2 * (width - start)), F32)
    for h in range(shards // 2):
        pair = x_ref[2 * h : 2 * h + 2, :, start:].astype(F32).reshape(2 * rows, -1).astype(BF16)
        both = mm(rows_ref[:, : 2 * rows], pair)
        w_ref[SLOT * h : SLOT * (h + 1), :] = jnp.concatenate(
            [both[:SLOT], both[SLOT:], blank], axis=-1
        ).astype(BF16)


def step_kernel(
    coef_ref, place_ref, att_ref, hid_ref, lat_ref, fresh_ref, mine_ref, other_ref, wf_ref, mod_ref, o_ref
):
    videos, tokens, width = hid_ref.shape
    rows = videos * tokens
    pairs = att_ref.shape[0] // videos
    att = att_ref[...].astype(F32)
    side = jnp.concatenate([att[:, tokens:, 32 * i : 32 * (i + 1)] for i in range(3)], axis=1)
    att = jnp.concatenate([att[:, :tokens, :], side], axis=-1).reshape(videos, pairs, tokens, 2 * SLOT)
    own = far = None
    for p in range(pairs):
        part = att[:, p].reshape(rows, 2 * SLOT).astype(BF16)
        at = slice(2 * SLOT * p, 2 * SLOT * (p + 1))
        own_term, far_term = mm(part, mine_ref[at, :]), mm(part, other_ref[at, :])
        own = own_term if own is None else own + own_term
        far = far_term if far is None else far + far_term
    low = place_ref[0] == 0
    half = width // 2
    proj = jnp.concatenate([jnp.where(low, own, far)[:, :half], jnp.where(low, far, own)[:, :half]], axis=-1)
    residual = hid_ref[...].astype(F32).reshape(rows, width) + mod_ref[0:1, :] * proj
    final_in = (layer_norm(residual) * (1.0 + mod_ref[2:3, :]) + mod_ref[1:2, :]).astype(BF16)
    predicted = mm_nt(wf_ref[...], final_in)
    for v in range(videos):
        pred = predicted[:, tokens * v : tokens * (v + 1)]
        clean = (lat_ref[v].astype(F32) - coef_ref[0] * pred) * coef_ref[1]
        stepped = coef_ref[2] * clean + coef_ref[3] * pred
        o_ref[v] = jnp.where(place_ref[1] == 0, fresh_ref[v].astype(F32), stepped).astype(BF16)


def arrange_kernel(core_ref, own_ref, cross_ref, o_ref):
    first = core_ref[0] == 0
    for parity in range(2):
        own = jnp.where(first, own_ref[2 * parity].astype(F32), own_ref[2 * parity + 1].astype(F32))
        cross = jnp.where(first, cross_ref[2 * parity].astype(F32), cross_ref[2 * parity + 1].astype(F32))
        pair = jnp.concatenate([jnp.where(first, own, cross), jnp.where(first, cross, own)], axis=0)
        for z in range(parity, o_ref.shape[0], 2):
            o_ref[z] = pair.astype(BF16)


def centered_place(c, ua_ref, va_ref, cb_ref, sb_ref):
    place = ua_ref[pl.ds(c, 1), :] * cb_ref[...] + va_ref[pl.ds(c, 1), :] * sb_ref[...]
    return place - jnp.mean(place, axis=-1, keepdims=True)


def place_kernel(wemb_ref, ua_ref, va_ref, cb_ref, sb_ref, sums_ref):
    tokens, width = cb_ref.shape
    blank = jnp.zeros((tokens, 7), F32)

    def one(few, carry):
        for i in range(4):
            c = 4 * few + i
            center = centered_place(c, ua_ref, va_ref, cb_ref, sb_ref)
            high = center.astype(BF16)
            low = (center - high.astype(F32)).astype(BF16)
            cross = (mm_nt(high, wemb_ref[...]) + mm_nt(low, wemb_ref[...])) * (2.0 / width)
            square = jnp.mean(center * center, axis=-1, keepdims=True)
            sums_ref[c] = jnp.concatenate([cross, square, blank], axis=-1).T
        return carry

    lax.fori_loop(0, sums_ref.shape[0] // 4, one, 0)


def prepare_kernel(
    group_ref, few_ref, mod_ref, ua_ref, va_ref, cb_ref, sb_ref, w_ref, mix_out, offset_out, q_out, kv_out,
    p, w, made, w_sem, out_sem,
):
    rows = q_out.shape[0]
    tokens = cb_ref.shape[0]
    step = 2 * rows
    steps = made.shape[0] // step

    edges = (0, 512, 2 * DENSE, 2 * DENSE + PADDED)

    def load_w(part):
        at = slice(edges[part], edges[part + 1])
        return pltpu.make_async_copy(w_ref.at[:, at], w.at[:, at], w_sem.at[part])

    def store(i):
        at = slice(step * i, step * (i + 1))
        return pltpu.make_async_copy(made.at[at], kv_out.at[at], out_sem.at[i])

    for part in range(3):
        load_w(part).start()
    gain = 1.0 + mod_ref[4:5, :]

    def place(i):
        for c in range(step // tokens * i, step // tokens * (i + 1), 2):
            two = [centered_place(c + j, ua_ref, va_ref, cb_ref, sb_ref) * gain for j in range(2)]
            p[tokens * c : tokens * (c + 2), :] = jnp.concatenate(two, axis=0).astype(BF16)

    place(0)
    for i in range(steps):
        here = slice(step * i, step * (i + 1))
        for part in range(2):
            if i == 0:
                load_w(part).wait()
            columns = slice(edges[part], edges[part + 1])
            if i + 1 < steps:
                made[here, columns] = mm(p[here, :], w[:, columns]).astype(BF16)
            else:
                both = mm(jnp.concatenate([p[here, :], few_ref[...]], axis=0), w[:, columns])
                made[here, columns] = both[:step].astype(BF16)
                few = both[step:] if part == 0 else jnp.concatenate([few, both[step:]], axis=-1)
            if part == 0 and i + 1 < steps:
                place(i + 1)
        store(i).start()
    load_w(2).wait()
    start = pl.multiple_of(group_ref[0] * rows, rows)
    own = jnp.concatenate([p[pl.ds(start, rows), :], few_ref[...]], axis=0)
    own = mm(own, w[:, edges[2] :])
    q_out[...] = own[:rows].astype(BF16)
    few = jnp.concatenate([few, own[rows:]], axis=-1)
    patch = mix_out.shape[0] // 2
    mix = few[:patch] + few[patch : 2 * patch]
    high = mix.astype(BF16).astype(F32)
    mix_out[...] = jnp.concatenate([high, mix - high], axis=0).astype(BF16)
    offset_out[...] = few[2 * patch : 2 * patch + 8] + few[2 * patch + 8 :]
    for i in range(steps):
        store(i).wait()


def spatial_kernel(
    group_ref, lat_ref, gram_ref, sums_ref, mix_ref, offset_ref, pq_ref, pkv_ref,
    o_ref, held, columns, kvs, sem,
):
    chunks, patch, tokens = lat_ref.shape
    members = o_ref.shape[0]
    block = members * tokens
    blocks = chunks // members

    def fetch(index):
        start = pl.multiple_of(index * block, block)
        return pltpu.make_async_copy(pkv_ref.at[pl.ds(start, block), :], held.at[index], sem.at[index])

    for i in range(blocks):
        fetch(i).start()

    gram = gram_ref[...]
    for c in range(chunks):
        once = lat_ref[c].astype(F32)
        twice = jnp.concatenate([once, once], axis=0)
        sums = sums_ref[c]
        mixed = mm(gram, twice.astype(BF16)) + sums[:patch]
        variance = jnp.sum(mixed * once, axis=0, keepdims=True) + sums[patch : patch + 1]
        scale = lax.rsqrt(jnp.maximum(variance, 0.0) + 1e-06)
        rows = jnp.concatenate([twice, jnp.broadcast_to(scale, (8, tokens))], axis=0)
        columns[tokens * c : tokens * (c + 1), :] = rows.T

    lane = lax.broadcasted_iota(jnp.int32, (1, 2 * DENSE), 1)

    kv_mix = mix_ref[:, : 2 * DENSE]
    kv_offset = offset_ref[0:1, : 2 * DENSE]

    def one(index, carry):
        start = pl.multiple_of(index * block, block)
        column = columns[pl.ds(start, block), :]
        latent, scale = column[:, : 2 * patch].astype(BF16), column[:, 2 * patch : 2 * patch + 1]
        mixed = mm(latent, kv_mix)
        fetch(index).wait()
        kv = (mixed + held[index].astype(F32)) * scale + kv_offset
        kvs[pl.ds(start, block), :] = kv.astype(BF16)
        return carry

    lax.fori_loop(0, blocks, one, 0)

    column = columns[pl.ds(pl.multiple_of(group_ref[0] * block, block), block), :]
    latent, scale = column[:, : 2 * patch].astype(BF16), column[:, 2 * patch : 2 * patch + 1]
    q_all = (mm(latent, mix_ref[:, 2 * DENSE :]) + pq_ref[...].astype(F32)) * scale + offset_ref[0:1, 2 * DENSE :]
    q_all = q_all.astype(BF16).astype(F32)
    merged = [None] * (PADDED // 128)

    def window(at):
        first, last = at // 128, (at + HDIM - 1) // 128
        here = slice(128 * first, 128 * (last + 1))
        inside = (lane >= at) & (lane < at + HDIM)
        return first, last, here, inside[:, here]

    def score(h):
        _, _, here, inside = window(HDIM * h)
        return mm_nt(jnp.where(inside, q_all[:, here], 0.0).astype(BF16), kvs[:, here])

    def weigh(scores):
        top = jnp.max(scores, axis=-1, keepdims=True)
        raised = jnp.exp2((scores - top) * (SCORE_SCALE * LOG2E))
        return raised.astype(BF16), jnp.sum(raised, axis=-1, keepdims=True)

    def blend(h, weighed):
        raised, total = weighed
        first, last, here, inside = window(DENSE + HDIM * h)
        found = jnp.where(inside, mm(raised, kvs[:, here]) * (1.0 / total), 0.0)
        for tile in range(first, last + 1):
            piece = found[:, 128 * (tile - first) : 128 * (tile - first + 1)]
            at = tile - DENSE // 128
            merged[at] = piece if merged[at] is None else merged[at] + piece

    scores = score(0)
    raised = None
    for h in range(HEADS):
        following = score(h + 1) if h + 1 < HEADS else None
        if raised is not None:
            blend(h - 1, raised)
        raised = weigh(scores)
        scores = following
    blend(HEADS - 1, raised)
    o_ref[...] = jnp.concatenate(merged, axis=-1).reshape(members, tokens, PADDED).astype(BF16)


def projection_kernel(rows_ref, w_ref, w_out, raw, sem):
    width = raw.shape[-1]
    skip = width - w_out.shape[-1] // 2
    copy = pltpu.make_async_copy(w_ref.at[:, w_ref.shape[-1] - width :], raw, sem)
    copy.start()
    copy.wait()
    made = [jnp.zeros((skip, w_out.shape[-1]), F32)]
    for h in range(HEADS):
        both = mm(rows_ref[:, : 2 * HDIM], raw[2 * HDIM * h : 2 * HDIM * (h + 1), :])
        made.append(jnp.concatenate([both[:HDIM, skip:], both[HDIM:, skip:]], axis=-1))
    w_out[...] = jnp.concatenate(made, axis=0).astype(BF16)


def finish_kernel(
    seq_ref, att_ref, lat_ref, wemb_ref, ua_ref, va_ref, cb_ref, sb_ref, mod_ref, w_ref, o_ref
):
    videos, tokens, width = o_ref.shape
    s = seq_ref[0]
    place = ua_ref[pl.ds(s, 1), :] * cb_ref[...] + va_ref[pl.ds(s, 1), :] * sb_ref[...]
    gate = mod_ref[5:6, :]
    att = att_ref[...].astype(F32).reshape(videos * tokens, PADDED).astype(BF16)
    embedded = [mm(lat_ref[v].astype(F32).T.astype(BF16), wemb_ref[...]) + place for v in range(videos)]
    gated = mm(att, w_ref[...]) * gate
    for v in range(videos):
        o_ref[v] = (embedded[v] + gated[tokens * v : tokens * (v + 1), :]).astype(BF16)


def position_factors(chunks, tokens, width):
    half = width // 2
    frequency = jnp.exp(jnp.arange(half, dtype=F32) * (-math.log(10000.0) / half))
    start = (jnp.arange(chunks, dtype=F32) * tokens)[:, None] * frequency[None, :]
    inner = jnp.arange(tokens, dtype=F32)[:, None] * frequency[None, :]
    sin_a, cos_a, sin_b, cos_b = jnp.sin(start), jnp.cos(start), jnp.sin(inner), jnp.cos(inner)
    ua = jnp.concatenate([sin_a, cos_a], axis=-1)
    va = jnp.concatenate([cos_a, -sin_a], axis=-1)
    cb = jnp.concatenate([cos_b, cos_b], axis=-1)
    sb = jnp.concatenate([sin_b, sin_b], axis=-1)
    return ua, va, cb, sb


def rounding_rest(values):
    return values - lax.reduce_precision(values, 8, 7)


def shards(
    t_qkv, hidden, latents, fresh, levels, alpha_bar, modulation, w_tout, w_final, w_embed, w_sqkv, w_sout,
):
    frames = lax.axis_size("queue")
    seqs = lax.axis_size("seq")
    queue_pos = lax.axis_index("queue")
    seq_pos = lax.axis_index("seq")
    videos, _, tokens, width = hidden.shape
    top_level = alpha_bar.shape[0] - 1
    pairs = frames // videos

    core = seq_pos % 2
    half = width // 2
    width_part = t_qkv.shape[-1] // pairs
    sent = width_part + half // 2
    packed, w_shard = call(
        pack_kernel,
        (
            jax.ShapeDtypeStruct((frames, tokens, sent), BF16),
            jax.ShapeDtypeStruct((w_sqkv.shape[0], 4 * DENSE), BF16),
        ),
        (core.reshape(1), t_qkv.reshape(videos, tokens, -1), w_tout, w_sqkv, w_sout),
        scratch=[
            pltpu.VMEM((videos, tokens, t_qkv.shape[-1]), BF16),
            pltpu.VMEM(w_tout.shape, BF16),
            pltpu.VMEM(w_sqkv.shape, BF16),
            pltpu.VMEM(w_sout.shape, BF16),
            pltpu.VMEM((frames, tokens, sent), BF16),
            pltpu.VMEM((w_sqkv.shape[0], 4 * DENSE), BF16),
            pltpu.SemaphoreType.DMA((videos,)),
            pltpu.SemaphoreType.DMA((4,)),
            pltpu.SemaphoreType.DMA((videos,)),
        ],
        smem=(0,),
        hbm=(1, 2, 3, 4),
        hbm_out=(0, 1),
        vmem=56,
    )
    w_spatial = lax.all_gather(w_shard, "queue", axis=0, tiled=True)

    arrived = lax.all_to_all(packed, "queue", split_axis=0, concat_axis=0, tiled=True)
    row_pick = jnp.asarray(weight_rows(SLOT), BF16)
    dense_pick = jnp.asarray(weight_rows(HDIM), BF16)

    level = lax.dynamic_index_in_dim(levels, queue_pos, 0, keepdims=False)
    following = lax.dynamic_index_in_dim(
        jnp.concatenate([levels[1:], jnp.full((1,), top_level + 1, levels.dtype)]), queue_pos, 0, keepdims=False
    )
    mods = lax.dynamic_index_in_dim(modulation, level, 0, keepdims=False).astype(F32)
    new_mods = lax.dynamic_index_in_dim(modulation, following - 1, 0, keepdims=False).astype(F32)
    a = lax.dynamic_index_in_dim(alpha_bar, level, 0, keepdims=False)
    b = lax.dynamic_index_in_dim(alpha_bar, level - 1, 0, keepdims=False)
    coef = jnp.stack([jnp.sqrt(1.0 - a), 1.0 / jnp.sqrt(a), jnp.sqrt(b), jnp.sqrt(1.0 - b)])

    ua, va, cb, sb = position_factors(seqs, tokens, width)
    rows = seqs * tokens
    own_rows = videos * tokens
    sums = call(
        place_kernel,
        jax.ShapeDtypeStruct((seqs, 24, tokens), F32),
        (w_embed, ua, va, cb, sb),
        flops=100_000_000,
        vmem=56,
    )
    gain, shift = 1.0 + new_mods[4:5], new_mods[3:4]
    emb_f32 = w_embed.astype(F32)
    centered = emb_f32 - jnp.mean(emb_f32, axis=-1, keepdims=True)
    gram = jnp.dot(centered, centered.T, precision=lax.Precision.HIGHEST) * (1.0 / width)
    gram = jnp.concatenate([gram, rounding_rest(gram)], axis=-1).astype(BF16)
    centered = centered * gain
    eight = jnp.zeros((7, width), F32)
    few = [centered, rounding_rest(centered), shift, eight, rounding_rest(shift), eight]
    few = jnp.concatenate(few, axis=0).astype(BF16)
    latents_t = latents.reshape(videos, tokens, -1).transpose(0, 2, 1)
    fresh_t = fresh.transpose(0, 2, 1)
    w_final_t = w_final.T
    early = (arrived, sums, few, gram, mods, new_mods, coef, latents_t, fresh_t, w_final_t)
    early = lax.optimization_barrier(early)
    arrived, sums, few, gram, mods, new_mods, coef, latents_t, fresh_t, w_final_t = early

    attended = call(
        temporal_kernel,
        jax.ShapeDtypeStruct((frames, tokens + tokens // 3, 128), BF16),
        (arrived, jnp.asarray(temporal_columns(), BF16)),
        scratch=[pltpu.VMEM((frames, tokens, 768), F32), pltpu.VMEM((frames, tokens, 2 * SLOT), F32)],
        flops=4_000_000_000,
    )
    stacked, attended = lax.optimization_barrier((arrived, attended))
    w_mine = call(
        unstack_kernel,
        jax.ShapeDtypeStruct((PADDED, PADDED), BF16),
        (stacked, row_pick),
        flops=20_000_000_000,
    )
    w_other = lax.ppermute(w_mine, "seq", [(i, i ^ 1) for i in range(seqs)])
    returned = lax.all_to_all(attended, "queue", split_axis=0, concat_axis=0, tiled=True)

    stepped = call(
        step_kernel,
        jax.ShapeDtypeStruct((videos, latents.shape[-1], tokens), BF16),
        (
            coef,
            jnp.stack([core, queue_pos]),
            returned,
            hidden.reshape(videos, tokens, width),
            latents_t,
            fresh_t,
            w_mine,
            w_other,
            w_final_t,
            mods,
        ),
        smem=(0, 1),
        flops=1_000_000_000,
    )
    behind = [(f - 1) % frames for f in range(frames)]
    queued = lax.ppermute(stepped, "queue", list(enumerate(behind)))
    cross = [(f * seqs + i, behind[f] * seqs + (i ^ 1)) for f in range(frames) for i in range(seqs)]
    queued_cross = lax.ppermute(stepped, ("queue", "seq"), cross)

    chips = seqs // 2
    patch = latents.shape[-1]
    sent_latents = call(
        arrange_kernel,
        jax.ShapeDtypeStruct((chips, 2 * patch, tokens), BF16),
        (core.reshape(1), queued, queued_cross),
        smem=(0,),
    )
    same_core = [[2 * z + i for z in range(chips)] for i in range(2)]
    everyone = lax.all_to_all(
        sent_latents, "seq", split_axis=0, concat_axis=0, tiled=True, axis_index_groups=same_core
    ).reshape(seqs, patch, tokens)
    groups = [[videos * g + i for i in range(videos)] for g in range(seqs // videos)]
    group = (seq_pos // videos).reshape(1)
    mix, offset, pq, pkv = call(
        prepare_kernel,
        (
            jax.ShapeDtypeStruct((2 * w_embed.shape[0], 2 * DENSE + PADDED), BF16),
            jax.ShapeDtypeStruct((8, 2 * DENSE + PADDED), F32),
            jax.ShapeDtypeStruct((own_rows, PADDED), BF16),
            jax.ShapeDtypeStruct((rows, 2 * DENSE), BF16),
        ),
        (group, few, new_mods, ua, va, cb, sb, w_spatial),
        scratch=[
            pltpu.VMEM((rows, width), BF16),
            pltpu.VMEM((width, 2 * DENSE + PADDED), BF16),
            pltpu.VMEM((rows, 2 * DENSE), BF16),
            pltpu.SemaphoreType.DMA((3,)),
            pltpu.SemaphoreType.DMA((4,)),
        ],
        smem=(0,),
        hbm=(7,),
        hbm_out=(3,),
        flops=8_000_000_000,
        vmem=56,
    )
    spatial = call(
        spatial_kernel,
        jax.ShapeDtypeStruct((videos, tokens, PADDED), BF16),
        (group, everyone, gram, sums, mix, offset, pq, pkv),
        scratch=[
            pltpu.VMEM((rows // own_rows, own_rows, 2 * DENSE), BF16),
            pltpu.VMEM((rows, 2 * latents.shape[-1] + 8), F32),
            pltpu.VMEM((rows, 2 * DENSE), BF16),
            pltpu.SemaphoreType.DMA((rows // own_rows,)),
        ],
        smem=(0,),
        hbm=(7,),
        flops=20_000_000_000,
        vmem=56,
    )
    heads_out = lax.all_to_all(
        spatial, "seq", split_axis=0, concat_axis=0, tiled=True, axis_index_groups=groups
    )
    late, _ = lax.optimization_barrier((w_spatial, spatial))
    w_s = call(
        projection_kernel,
        jax.ShapeDtypeStruct((PADDED, width), BF16),
        (dense_pick, late),
        scratch=[pltpu.VMEM((width, PADDED), BF16), pltpu.SemaphoreType.DMA],
        hbm=(1,),
        flops=20_000_000_000,
        vmem=56,
    )
    block_out = call(
        finish_kernel,
        jax.ShapeDtypeStruct((videos, tokens, width), BF16),
        (seq_pos.reshape(1), heads_out, queued, w_embed, ua, va, cb, sb, new_mods, w_s),
        smem=(0,),
        flops=1_000_000_000,
    )
    return (
        queued.transpose(0, 2, 1).reshape(videos, 1, tokens, -1),
        block_out.reshape(videos, 1, tokens, width),
    )


def solution(mesh):
    in_specs = (
        P(None, "queue", "seq", None),
        P(None, "queue", "seq", None),
        P(None, "queue", "seq", None),
        P(None, "seq", None),
        P(),
        P(),
        P(),
        P("queue", None),
        P(),
        P(),
        P("queue", None),
        P("queue", None),
    )
    out_specs = (P(None, "queue", "seq", None), P(None, "queue", "seq", None))
    return jax.shard_map(shards, mesh=mesh, in_specs=in_specs, out_specs=out_specs, check_vma=False)
```

```python
import math

import jax
import jax.numpy as jnp
import numpy as np
from jax import lax
from jax.experimental import pallas as pl
from jax.experimental.pallas import tpu as pltpu
from jax.sharding import PartitionSpec as P

HEADS = 8
HDIM = 72
HALF = HDIM // 2
SLOT = 80
PADDED = HEADS * SLOT
DENSE = HEADS * HDIM
SCORE_SCALE = 1.0 / math.sqrt(HDIM)
LOG2E = math.log2(math.e)
F32 = jnp.float32
BF16 = jnp.bfloat16
MIB = 1024 * 1024


def mm(a, b):
    return jnp.dot(a, b, preferred_element_type=F32)


def mm_nt(a, b):
    return lax.dot_general(a, b, (((1,), (1,)), ((), ())), preferred_element_type=F32)


def call(kernel, out_shape, args, scratch=(), smem=(), hbm=(), hbm_out=(), flops=0, vmem=24, grid=None, in_specs=None, out_specs=None):
    moved = sum(a.size * a.dtype.itemsize for a in args)
    if in_specs is None:
        in_specs = [
            pl.BlockSpec(memory_space=pltpu.SMEM if i in smem else pl.ANY if i in hbm else pltpu.VMEM)
            for i in range(len(args))
        ]
        if isinstance(out_shape, tuple):
            out_specs = tuple(
                pl.BlockSpec(memory_space=pl.ANY if i in hbm_out else pltpu.VMEM) for i in range(len(out_shape))
            )
        else:
            out_specs = pl.BlockSpec(memory_space=pltpu.VMEM)
    return pl.pallas_call(
        kernel,
        out_shape=out_shape,
        in_specs=in_specs,
        out_specs=out_specs,
        scratch_shapes=list(scratch),
        compiler_params=pltpu.CompilerParams(vmem_limit_bytes=vmem * MIB),
        cost_estimate=pl.CostEstimate(flops=flops, bytes_accessed=moved, transcendentals=0),
        **({"grid": grid} if grid else {}),
    )(*args)


def layer_norm(values):
    center = values - jnp.mean(values, axis=-1, keepdims=True)
    spread = jnp.mean(center * center, axis=-1, keepdims=True)
    return center * lax.rsqrt(spread + 1e-06)


def pack_kernel(
    core_ref, x_ref, tout_ref, sqkv_ref, sout_ref, o_ref, shard_ref,
    x, tout, sqkv, sout, packed, shard, x_sem, w_sem, o_sem,
):
    videos, tokens, columns = x.shape
    pairs = packed.shape[0] // videos
    width = columns // pairs

    def load(v):
        return pltpu.make_async_copy(x_ref.at[v], x.at[v], x_sem.at[v])

    weights = [
        pltpu.make_async_copy(source, target, w_sem.at[i])
        for i, (source, target) in enumerate(((tout_ref, tout), (sqkv_ref, sqkv), (sout_ref, sout)))
    ]

    def store(v):
        at = slice(pairs * v, pairs * (v + 1))
        return pltpu.make_async_copy(packed.at[at], o_ref.at[at], o_sem.at[v])

    weights[0].start()
    load(0).start()
    weights[1].start()
    weights[2].start()
    for v in range(1, videos):
        load(v).start()

    weights[0].wait()
    half = tout.shape[-1] // 2
    left, right = tout[:, :half].astype(F32), tout[:, half:].astype(F32)
    own = jnp.where(core_ref[0] == 0, left, right)
    weight = jnp.concatenate([own[:, : half // 2], own[:, half // 2 :]], axis=0).astype(BF16)
    load(0).wait()
    for part in range(pairs):
        packed[part, :, :width] = x[0, :, part * width : (part + 1) * width]
        packed[part, :, width:] = weight
    store(0).start()

    weights[1].wait()
    weights[2].wait()
    pieces = []
    for part in (1, 2, 0):
        for h in range(HEADS):
            at = HDIM * (3 * h + part)
            pieces.append(sqkv[:, at : at + HDIM])
    ends = jnp.concatenate([sout[:, :half].astype(F32), sout[:, half:].astype(F32)], axis=0)
    shard[...] = jnp.concatenate(pieces + [ends.astype(BF16)], axis=-1)
    last = pltpu.make_async_copy(shard, shard_ref, w_sem.at[3])
    last.start()

    for v in range(1, videos):
        load(v).wait()
        for part in range(pairs):
            packed[pairs * v + part, :, :width] = x[v, :, part * width : (part + 1) * width]
            packed[pairs * v + part, :, width:] = weight
        store(v).start()
    last.wait()
    for v in range(videos):
        store(v).wait()


def temporal_columns():
    pick = np.zeros((6 * HDIM, 768), np.float32)
    for head in range(2):
        base = 3 * HDIM * head
        for i in range(HDIM):
            pick[base + i, 256 * head + i] = 1.0
            pick[base + HDIM + i, 256 * head + 128 + i] = 1.0
            pick[base + 2 * HDIM + i, 512 + SLOT * head + i] = 1.0
    return pick


def weight_rows(slot):
    pick = np.zeros((2 * slot, 256), np.float32)
    for shard in range(2):
        for i in range(HALF):
            pick[HALF * shard + i, HDIM * shard + i] = 1.0
            pick[slot + HALF * shard + i, HDIM * shard + HALF + i] = 1.0
    return pick


def temporal_kernel(x_ref, pick_ref, o_ref, parts, total):
    frames, tokens, _ = x_ref.shape
    flat = x_ref[:, :, : 6 * HDIM].astype(F32).reshape(frames * tokens, 6 * HDIM).astype(BF16)
    parts[...] = mm(flat, pick_ref[...]).reshape(frames, tokens, -1)
    rows = frames * 8
    first = lax.broadcasted_iota(jnp.int32, (1, 2 * SLOT), 1) < SLOT
    same = (
        lax.broadcasted_iota(jnp.int32, (rows, rows), 0) % 8
        == lax.broadcasted_iota(jnp.int32, (rows, rows), 1) % 8
    )
    blocks = tokens // 8
    pieces = [parts[:, 8 * i : 8 * i + 8, :].reshape(rows, -1).astype(BF16) for i in range(blocks)]
    scores = [
        mm_nt(piece[:, 256 * head : 256 * head + 128], piece[:, 256 * head + 128 : 256 * head + 256])
        for piece in pieces
        for head in range(2)
    ]
    scores = jnp.concatenate(scores, axis=0).reshape(2 * blocks, rows, rows)
    scores = jnp.where(same[None], scores * SCORE_SCALE, -jnp.inf)
    raised = jnp.exp(scores - jnp.max(scores, axis=-1, keepdims=True))
    weights = (raised / jnp.sum(raised, axis=-1, keepdims=True)).astype(BF16)
    for i in range(blocks):
        v = pieces[i][:, 512 : 512 + 2 * SLOT]
        out = jnp.where(first, mm(weights[2 * i], v), mm(weights[2 * i + 1], v))
        total[:, 8 * i : 8 * i + 8, :] = out.reshape(frames, 8, 2 * SLOT)
    side = total[:, :, 128:]
    third = tokens // 3
    side = [side[:, third * i : third * (i + 1), :] for i in range(3)] + [jnp.zeros((frames, third, 32), F32)]
    o_ref[:, :tokens, :] = total[:, :, :128].astype(BF16)
    o_ref[:, tokens:, :] = jnp.concatenate(side, axis=-1).astype(BF16)


def unstack_kernel(x_ref, rows_ref, w_ref):
    shards, rows, width = x_ref.shape
    start = 6 * HDIM
    blank = jnp.zeros((SLOT, w_ref.shape[-1] - 2 * (width - start)), F32)
    for h in range(shards // 2):
        pair = x_ref[2 * h : 2 * h + 2, :, start:].astype(F32).reshape(2 * rows, -1).astype(BF16)
        both = mm(rows_ref[:, : 2 * rows], pair)
        w_ref[SLOT * h : SLOT * (h + 1), :] = jnp.concatenate(
            [both[:SLOT], both[SLOT:], blank], axis=-1
        ).astype(BF16)


def step_kernel(coef_ref, core_ref, att_ref, hid_ref, lat_ref, mine_ref, other_ref, wf_ref, mod_ref, o_ref):
    videos, tokens, width = hid_ref.shape
    rows = videos * tokens
    pairs = att_ref.shape[0] // videos
    att = att_ref[...].astype(F32)
    side = jnp.concatenate([att[:, tokens:, 32 * i : 32 * (i + 1)] for i in range(3)], axis=1)
    att = jnp.concatenate([att[:, :tokens, :], side], axis=-1).reshape(videos, pairs, tokens, 2 * SLOT)
    own = far = None
    for p in range(pairs):
        part = att[:, p].reshape(rows, 2 * SLOT).astype(BF16)
        at = slice(2 * SLOT * p, 2 * SLOT * (p + 1))
        own_term, far_term = mm(part, mine_ref[at, :]), mm(part, other_ref[at, :])
        own = own_term if own is None else own + own_term
        far = far_term if far is None else far + far_term
    low = core_ref[0] == 0
    half = width // 2
    proj = jnp.concatenate([jnp.where(low, own, far)[:, :half], jnp.where(low, far, own)[:, :half]], axis=-1)
    residual = hid_ref[...].astype(F32).reshape(rows, width) + mod_ref[0:1, :] * proj
    final_in = (layer_norm(residual) * (1.0 + mod_ref[2:3, :]) + mod_ref[1:2, :]).astype(BF16)
    predicted = mm_nt(wf_ref[...], final_in)
    for v in range(videos):
        pred = predicted[:, tokens * v : tokens * (v + 1)]
        clean = (lat_ref[v].astype(F32) - coef_ref[0] * pred) * coef_ref[1]
        o_ref[v] = (coef_ref[2] * clean + coef_ref[3] * pred).astype(BF16)


def centered_place(c, ua_ref, va_ref, cb_ref, sb_ref):
    place = ua_ref[pl.ds(c, 1), :] * cb_ref[...] + va_ref[pl.ds(c, 1), :] * sb_ref[...]
    return place - jnp.mean(place, axis=-1, keepdims=True)


def place_kernel(wemb_ref, ua_ref, va_ref, cb_ref, sb_ref, sums_ref):
    tokens, width = cb_ref.shape
    blank = jnp.zeros((tokens, 7), F32)

    def one(few, carry):
        for i in range(8):
            c = 8 * few + i
            center = centered_place(c, ua_ref, va_ref, cb_ref, sb_ref)
            high = center.astype(BF16)
            low = (center - high.astype(F32)).astype(BF16)
            cross = (mm_nt(high, wemb_ref[...]) + mm_nt(low, wemb_ref[...])) * (2.0 / width)
            square = jnp.mean(center * center, axis=-1, keepdims=True)
            sums_ref[c] = jnp.concatenate([cross, square, blank], axis=-1).T
        return carry

    lax.fori_loop(0, sums_ref.shape[0] // 8, one, 0)


def prepare_kernel(
    group_ref, few_ref, mod_ref, ua_ref, va_ref, cb_ref, sb_ref, w_ref, mix_out, offset_out, q_out, kv_out,
    p, w, made, w_sem, out_sem,
):
    rows = q_out.shape[0]
    tokens = cb_ref.shape[0]
    step = 2 * rows
    steps = made.shape[0] // step

    edges = (0, 512, 2 * DENSE, 2 * DENSE + PADDED)

    def load_w(part):
        at = slice(edges[part], edges[part + 1])
        return pltpu.make_async_copy(w_ref.at[:, at], w.at[:, at], w_sem.at[part])

    def store(i):
        at = slice(step * i, step * (i + 1))
        return pltpu.make_async_copy(made.at[at], kv_out.at[at], out_sem.at[i])

    for part in range(3):
        load_w(part).start()
    gain = 1.0 + mod_ref[4:5, :]

    def place(i):
        for c in range(step // tokens * i, step // tokens * (i + 1), 2):
            two = [centered_place(c + j, ua_ref, va_ref, cb_ref, sb_ref) * gain for j in range(2)]
            p[tokens * c : tokens * (c + 2), :] = jnp.concatenate(two, axis=0).astype(BF16)

    place(0)
    for i in range(steps):
        here = slice(step * i, step * (i + 1))
        for part in range(2):
            if i == 0:
                load_w(part).wait()
            columns = slice(edges[part], edges[part + 1])
            if i + 1 < steps:
                made[here, columns] = mm(p[here, :], w[:, columns]).astype(BF16)
            else:
                both = mm(jnp.concatenate([p[here, :], few_ref[...]], axis=0), w[:, columns])
                made[here, columns] = both[:step].astype(BF16)
                few = both[step:] if part == 0 else jnp.concatenate([few, both[step:]], axis=-1)
            if part == 0 and i + 1 < steps:
                place(i + 1)
        store(i).start()
    load_w(2).wait()
    start = pl.multiple_of(group_ref[0] * rows, rows)
    own = jnp.concatenate([p[pl.ds(start, rows), :], few_ref[...]], axis=0)
    own = mm(own, w[:, edges[2] :])
    q_out[...] = own[:rows].astype(BF16)
    few = jnp.concatenate([few, own[rows:]], axis=-1)
    patch = mix_out.shape[0] // 2
    mix = few[:patch] + few[patch : 2 * patch]
    high = mix.astype(BF16).astype(F32)
    mix_out[...] = jnp.concatenate([high, mix - high], axis=0).astype(BF16)
    offset_out[...] = few[2 * patch : 2 * patch + 8] + few[2 * patch + 8 :]
    for i in range(steps):
        store(i).wait()


def spatial_kernel(
    group_ref, lat_ref, gram_ref, sums_ref, mix_ref, offset_ref, pq_ref, pkv_ref,
    o_ref, held, columns, kvs, sem,
):
    chunks, patch, tokens = lat_ref.shape
    members = o_ref.shape[0]
    block = members * tokens
    blocks = chunks // members

    def fetch(index):
        start = pl.multiple_of(index * block, block)
        return pltpu.make_async_copy(pkv_ref.at[pl.ds(start, block), :], held.at[index], sem.at[index])

    for i in range(blocks):
        fetch(i).start()

    gram = gram_ref[...]
    for c in range(chunks):
        once = lat_ref[c].astype(F32)
        twice = jnp.concatenate([once, once], axis=0)
        sums = sums_ref[c]
        mixed = mm(gram, twice.astype(BF16)) + sums[:patch]
        variance = jnp.sum(mixed * once, axis=0, keepdims=True) + sums[patch : patch + 1]
        scale = lax.rsqrt(jnp.maximum(variance, 0.0) + 1e-06)
        rows = jnp.concatenate([twice, jnp.broadcast_to(scale, (8, tokens))], axis=0)
        columns[tokens * c : tokens * (c + 1), :] = rows.T

    lane = lax.broadcasted_iota(jnp.int32, (1, 2 * DENSE), 1)

    kv_mix = mix_ref[:, : 2 * DENSE]
    kv_offset = offset_ref[0:1, : 2 * DENSE]

    def one(index, carry):
        start = pl.multiple_of(index * block, block)
        column = columns[pl.ds(start, block), :]
        latent, scale = column[:, : 2 * patch].astype(BF16), column[:, 2 * patch : 2 * patch + 1]
        mixed = mm(latent, kv_mix)
        fetch(index).wait()
        kv = (mixed + held[index].astype(F32)) * scale + kv_offset
        kvs[pl.ds(start, block), :] = kv.astype(BF16)
        return carry

    lax.fori_loop(0, blocks, one, 0)

    column = columns[pl.ds(pl.multiple_of(group_ref[0] * block, block), block), :]
    latent, scale = column[:, : 2 * patch].astype(BF16), column[:, 2 * patch : 2 * patch + 1]
    q_all = (mm(latent, mix_ref[:, 2 * DENSE :]) + pq_ref[...].astype(F32)) * scale + offset_ref[0:1, 2 * DENSE :]
    q_all = q_all.astype(BF16).astype(F32)
    merged = [None] * (PADDED // 128)

    def window(at):
        first, last = at // 128, (at + HDIM - 1) // 128
        here = slice(128 * first, 128 * (last + 1))
        inside = (lane >= at) & (lane < at + HDIM)
        return first, last, here, inside[:, here]

    def score(h):
        _, _, here, inside = window(HDIM * h)
        return mm_nt(jnp.where(inside, q_all[:, here], 0.0).astype(BF16), kvs[:, here])

    def weigh(scores):
        top = jnp.max(scores, axis=-1, keepdims=True)
        raised = jnp.exp2((scores - top) * (SCORE_SCALE * LOG2E))
        return raised.astype(BF16), jnp.sum(raised, axis=-1, keepdims=True)

    def blend(h, weighed):
        raised, total = weighed
        first, last, here, inside = window(DENSE + HDIM * h)
        found = jnp.where(inside, mm(raised, kvs[:, here]) * (1.0 / total), 0.0)
        for tile in range(first, last + 1):
            piece = found[:, 128 * (tile - first) : 128 * (tile - first + 1)]
            at = tile - DENSE // 128
            merged[at] = piece if merged[at] is None else merged[at] + piece

    scores = score(0)
    raised = None
    for h in range(HEADS):
        following = score(h + 1) if h + 1 < HEADS else None
        if raised is not None:
            blend(h - 1, raised)
        raised = weigh(scores)
        scores = following
    blend(HEADS - 1, raised)
    o_ref[...] = jnp.concatenate(merged, axis=-1).reshape(members, tokens, PADDED).astype(BF16)


def projection_kernel(rows_ref, w_ref, w_out, raw, sem):
    width = raw.shape[-1]
    skip = width - w_out.shape[-1] // 2
    copy = pltpu.make_async_copy(w_ref.at[:, w_ref.shape[-1] - width :], raw, sem)
    copy.start()
    copy.wait()
    made = [jnp.zeros((skip, w_out.shape[-1]), F32)]
    for h in range(HEADS):
        both = mm(rows_ref[:, : 2 * HDIM], raw[2 * HDIM * h : 2 * HDIM * (h + 1), :])
        made.append(jnp.concatenate([both[:HDIM, skip:], both[HDIM:, skip:]], axis=-1))
    w_out[...] = jnp.concatenate(made, axis=0).astype(BF16)


def finish_kernel(
    seq_ref, att_ref, lat_ref, wemb_ref, ua_ref, va_ref, cb_ref, sb_ref, mod_ref, w_ref, o_ref
):
    videos, tokens, width = o_ref.shape
    s = seq_ref[0]
    place = ua_ref[pl.ds(s, 1), :] * cb_ref[...] + va_ref[pl.ds(s, 1), :] * sb_ref[...]
    gate = mod_ref[5:6, :]
    att = att_ref[...].astype(F32).reshape(videos * tokens, PADDED).astype(BF16)
    embedded = [mm(lat_ref[v].astype(F32).T.astype(BF16), wemb_ref[...]) + place for v in range(videos)]
    gated = mm(att, w_ref[...]) * gate
    for v in range(videos):
        o_ref[v] = (embedded[v] + gated[tokens * v : tokens * (v + 1), :]).astype(BF16)


def position_factors(chunks, tokens, width):
    half = width // 2
    frequency = jnp.exp(jnp.arange(half, dtype=F32) * (-math.log(10000.0) / half))
    start = (jnp.arange(chunks, dtype=F32) * tokens)[:, None] * frequency[None, :]
    inner = jnp.arange(tokens, dtype=F32)[:, None] * frequency[None, :]
    sin_a, cos_a, sin_b, cos_b = jnp.sin(start), jnp.cos(start), jnp.sin(inner), jnp.cos(inner)
    ua = jnp.concatenate([sin_a, cos_a], axis=-1)
    va = jnp.concatenate([cos_a, -sin_a], axis=-1)
    cb = jnp.concatenate([cos_b, cos_b], axis=-1)
    sb = jnp.concatenate([sin_b, sin_b], axis=-1)
    return ua, va, cb, sb


def rounding_rest(values):
    return values - lax.reduce_precision(values, 8, 7)


def shards(
    t_qkv, hidden, latents, fresh, levels, alpha_bar, modulation, w_tout, w_final, w_embed, w_sqkv, w_sout,
):
    frames = lax.axis_size("queue")
    seqs = lax.axis_size("seq")
    queue_pos = lax.axis_index("queue")
    seq_pos = lax.axis_index("seq")
    videos, _, tokens, width = hidden.shape
    top_level = alpha_bar.shape[0] - 1
    pairs = frames // videos

    core = seq_pos % 2
    half = width // 2
    width_part = t_qkv.shape[-1] // pairs
    sent = width_part + half // 2
    packed, w_shard = call(
        pack_kernel,
        (
            jax.ShapeDtypeStruct((frames, tokens, sent), BF16),
            jax.ShapeDtypeStruct((w_sqkv.shape[0], 4 * DENSE), BF16),
        ),
        (core.reshape(1), t_qkv.reshape(videos, tokens, -1), w_tout, w_sqkv, w_sout),
        scratch=[
            pltpu.VMEM((videos, tokens, t_qkv.shape[-1]), BF16),
            pltpu.VMEM(w_tout.shape, BF16),
            pltpu.VMEM(w_sqkv.shape, BF16),
            pltpu.VMEM(w_sout.shape, BF16),
            pltpu.VMEM((frames, tokens, sent), BF16),
            pltpu.VMEM((w_sqkv.shape[0], 4 * DENSE), BF16),
            pltpu.SemaphoreType.DMA((videos,)),
            pltpu.SemaphoreType.DMA((4,)),
            pltpu.SemaphoreType.DMA((videos,)),
        ],
        smem=(0,),
        hbm=(1, 2, 3, 4),
        hbm_out=(0, 1),
        vmem=56,
    )
    w_spatial = lax.all_gather(w_shard, "queue", axis=0, tiled=True)

    arrived = lax.all_to_all(packed, "queue", split_axis=0, concat_axis=0, tiled=True)
    row_pick = jnp.asarray(weight_rows(SLOT), BF16)
    dense_pick = jnp.asarray(weight_rows(HDIM), BF16)

    level = lax.dynamic_index_in_dim(levels, queue_pos, 0, keepdims=False)
    following = lax.dynamic_index_in_dim(
        jnp.concatenate([levels[1:], jnp.full((1,), top_level + 1, levels.dtype)]), queue_pos, 0, keepdims=False
    )
    mods = lax.dynamic_index_in_dim(modulation, level, 0, keepdims=False).astype(F32)
    new_mods = lax.dynamic_index_in_dim(modulation, following - 1, 0, keepdims=False).astype(F32)
    a = lax.dynamic_index_in_dim(alpha_bar, level, 0, keepdims=False)
    b = lax.dynamic_index_in_dim(alpha_bar, level - 1, 0, keepdims=False)
    coef = jnp.stack([jnp.sqrt(1.0 - a), 1.0 / jnp.sqrt(a), jnp.sqrt(b), jnp.sqrt(1.0 - b)])

    ua, va, cb, sb = position_factors(seqs, tokens, width)
    rows = seqs * tokens
    own_rows = videos * tokens
    sums = call(
        place_kernel,
        jax.ShapeDtypeStruct((seqs, 24, tokens), F32),
        (w_embed, ua, va, cb, sb),
        flops=100_000_000,
        vmem=56,
    )
    gain, shift = 1.0 + new_mods[4:5], new_mods[3:4]
    emb_f32 = w_embed.astype(F32)
    centered = emb_f32 - jnp.mean(emb_f32, axis=-1, keepdims=True)
    gram = jnp.dot(centered, centered.T, precision=lax.Precision.HIGHEST) * (1.0 / width)
    gram = jnp.concatenate([gram, rounding_rest(gram)], axis=-1).astype(BF16)
    centered = centered * gain
    eight = jnp.zeros((7, width), F32)
    few = [centered, rounding_rest(centered), shift, eight, rounding_rest(shift), eight]
    few = jnp.concatenate(few, axis=0).astype(BF16)
    latents_t = latents.reshape(videos, tokens, -1).transpose(0, 2, 1)
    fresh_t = fresh.transpose(0, 2, 1)
    w_final_t = w_final.T
    early = (arrived, sums, few, gram, mods, new_mods, coef, latents_t, fresh_t, w_final_t)
    early = lax.optimization_barrier(early)
    arrived, sums, few, gram, mods, new_mods, coef, latents_t, fresh_t, w_final_t = early

    attended = call(
        temporal_kernel,
        jax.ShapeDtypeStruct((frames, tokens + tokens // 3, 128), BF16),
        (arrived, jnp.asarray(temporal_columns(), BF16)),
        scratch=[pltpu.VMEM((frames, tokens, 768), F32), pltpu.VMEM((frames, tokens, 2 * SLOT), F32)],
        flops=4_000_000_000,
    )
    stacked, attended = lax.optimization_barrier((arrived, attended))
    w_mine = call(
        unstack_kernel,
        jax.ShapeDtypeStruct((PADDED, PADDED), BF16),
        (stacked, row_pick),
        flops=20_000_000_000,
    )
    w_other = lax.ppermute(w_mine, "seq", [(i, i ^ 1) for i in range(seqs)])
    returned = lax.all_to_all(attended, "queue", split_axis=0, concat_axis=0, tiled=True)

    stepped = call(
        step_kernel,
        jax.ShapeDtypeStruct((videos, latents.shape[-1], tokens), BF16),
        (
            coef,
            core.reshape(1),
            returned,
            hidden.reshape(videos, tokens, width),
            latents_t,
            w_mine,
            w_other,
            w_final_t,
            mods,
        ),
        smem=(0, 1),
        flops=1_000_000_000,
    )
    arriving = lax.ppermute(stepped, "queue", [(f, f - 1) for f in range(1, frames)])
    queued = jnp.where(queue_pos == frames - 1, fresh_t, arriving)

    everyone = lax.all_to_all(
        jnp.tile(queued, (seqs // videos, 1, 1)), "seq", split_axis=0, concat_axis=0, tiled=True
    )
    groups = [[videos * g + i for i in range(videos)] for g in range(seqs // videos)]
    group = (seq_pos // videos).reshape(1)
    mix, offset, pq, pkv = call(
        prepare_kernel,
        (
            jax.ShapeDtypeStruct((2 * w_embed.shape[0], 2 * DENSE + PADDED), BF16),
            jax.ShapeDtypeStruct((8, 2 * DENSE + PADDED), F32),
            jax.ShapeDtypeStruct((own_rows, PADDED), BF16),
            jax.ShapeDtypeStruct((rows, 2 * DENSE), BF16),
        ),
        (group, few, new_mods, ua, va, cb, sb, w_spatial),
        scratch=[
            pltpu.VMEM((rows, width), BF16),
            pltpu.VMEM((width, 2 * DENSE + PADDED), BF16),
            pltpu.VMEM((rows, 2 * DENSE), BF16),
            pltpu.SemaphoreType.DMA((3,)),
            pltpu.SemaphoreType.DMA((4,)),
        ],
        smem=(0,),
        hbm=(7,),
        hbm_out=(3,),
        flops=8_000_000_000,
        vmem=56,
    )
    spatial = call(
        spatial_kernel,
        jax.ShapeDtypeStruct((videos, tokens, PADDED), BF16),
        (group, everyone, gram, sums, mix, offset, pq, pkv),
        scratch=[
            pltpu.VMEM((rows // own_rows, own_rows, 2 * DENSE), BF16),
            pltpu.VMEM((rows, 2 * latents.shape[-1] + 8), F32),
            pltpu.VMEM((rows, 2 * DENSE), BF16),
            pltpu.SemaphoreType.DMA((rows // own_rows,)),
        ],
        smem=(0,),
        hbm=(7,),
        flops=20_000_000_000,
        vmem=56,
    )
    heads_out = lax.all_to_all(
        spatial, "seq", split_axis=0, concat_axis=0, tiled=True, axis_index_groups=groups
    )
    late, _ = lax.optimization_barrier((w_spatial, spatial))
    w_s = call(
        projection_kernel,
        jax.ShapeDtypeStruct((PADDED, width), BF16),
        (dense_pick, late),
        scratch=[pltpu.VMEM((width, PADDED), BF16), pltpu.SemaphoreType.DMA],
        hbm=(1,),
        flops=20_000_000_000,
        vmem=56,
    )
    block_out = call(
        finish_kernel,
        jax.ShapeDtypeStruct((videos, tokens, width), BF16),
        (seq_pos.reshape(1), heads_out, queued, w_embed, ua, va, cb, sb, new_mods, w_s),
        smem=(0,),
        flops=1_000_000_000,
    )
    return (
        queued.transpose(0, 2, 1).reshape(videos, 1, tokens, -1),
        block_out.reshape(videos, 1, tokens, width),
    )


def solution(mesh):
    in_specs = (
        P(None, "queue", "seq", None),
        P(None, "queue", "seq", None),
        P(None, "queue", "seq", None),
        P(None, "seq", None),
        P(),
        P(),
        P(),
        P("queue", None),
        P(),
        P(),
        P("queue", None),
        P("queue", None),
    )
    out_specs = (P(None, "queue", "seq", None), P(None, "queue", "seq", None))
    return jax.shard_map(shards, mesh=mesh, in_specs=in_specs, out_specs=out_specs, check_vma=False)
```
